32 devices in a mesh: dp: 8 (over y, x, core), ctx: 4 (over z).
Axes of the slice: x: 2, y: 2, z: 4, core: 2. Of those that a mesh axis runs over, the one named last changes fastest.
Arguments:
- layer_input_rows: bfloat16 [8, 512, 1536], P('dp', 'ctx'), may hold values from -6 to 6
- routes: int32 [8, 512, 8], P('dp', 'ctx'), may hold values from 0 to 19, all different within a row; in each aligned block of 128 rows (0 to 127, 128 to 255, ..., all dimensions but the last counted through in order) at most 76 rows name the same one
- prefix: int32 [8], P('dp'), may hold values from 1 to 512
- sequence_adapter_index: int32 [8], P('dp'), may hold values from 0 to 7
- attention_norm_gain: float32 [1536], replicated, may hold values from 0.1 to 1.9
- expert_norm_gain: float32 [1536], replicated, may hold values from 0.1 to 1.9
- query_weight: bfloat16 [1536, 1536], replicated, may hold values from -0.15625 to 0.15625
- key_value_weight: bfloat16 [1536, 1024], replicated, may hold values from -0.15625 to 0.15625
- projection_weight: bfloat16 [1536, 1536], replicated, may hold values from -1 to 1
- router_weight: bfloat16 [1536, 20], replicated, may hold values from -0.078125 to 0.078125
- gate_up_weight: bfloat16 [20, 1536, 1024], P('ctx'), may hold values from -0.15625 to 0.15625
- down_weight: bfloat16 [20, 512, 1536], P('ctx'), may hold values from -1 to 1
- adapter_query_key_value_input: bfloat16 [8, 1536, 48], replicated, may hold values from -0.15625 to 0.15625
- adapter_query_output: bfloat16 [8, 16, 1536], replicated, may hold values from -0.25 to 0.25
- adapter_key_value_output: bfloat16 [8, 2, 16, 512], replicated, may hold values from -0.25 to 0.25
- adapter_projection_input: bfloat16 [8, 1536, 16], replicated, may hold values from -0.15625 to 0.15625
- adapter_projection_output: bfloat16 [8, 16, 1536], replicated, may hold values from -0.25 to 0.25
- adapter_gate_up_input: bfloat16 [8, 20, 1536, 32], P(None, 'ctx'), may hold values from -0.15625 to 0.15625
- adapter_gate_up_output: bfloat16 [8, 20, 2, 16, 512], P(None, 'ctx'), may hold values from -0.25 to 0.25
- adapter_down_input: bfloat16 [8, 20, 512, 16], P(None, 'ctx'), may hold values from -0.25 to 0.25
- adapter_down_output: bfloat16 [8, 20, 16, 1536], P(None, 'ctx'), may hold values from -0.25 to 0.25
- cotangent: bfloat16 [8, 512, 1536], P('dp', 'ctx'), may hold values from -6 to 6
Outputs:
- grad_x: float32 [8, 512, 1536], P('dp', 'ctx')
- grad_qkv_a: float32 [8, 1536, 48], P(None, 'dp')
- grad_query_b: float32 [8, 16, 1536], P(None, None, 'dp')
- grad_kv_b: float32 [8, 2, 16, 512], P(None, None, None, 'dp')
- grad_out_a: float32 [8, 1536, 16], P(None, 'dp')
- grad_out_b: float32 [8, 16, 1536], P(None, None, 'dp')
- grad_gateup_a: float32 [8, 20, 1536, 32], P(None, 'ctx', 'dp')
- grad_gateup_b: float32 [8, 20, 2, 16, 512], P(None, 'ctx', None, None, 'dp')
- grad_down_a: float32 [8, 20, 512, 16], P(None, 'ctx', 'dp')
- grad_down_b: float32 [8, 20, 16, 1536], P(None, 'ctx', None, 'dp')
The draws below stay inside these ranges and needn't reach their ends.
Inputs may be any that keep to these rules, and one draw needn't show every extreme that they name: `routes`: each token names 8 different experts. Among the 128 tokens of one device (aligned blocks of 128 positions of a sequence) no expert is named more than 76 times, and in every draw some expert is named exactly 76 times by the tokens of some device.
All inputs are finite; a program needn't handle non-finite values.
Results may differ from the reference program's by a relative error of at most 0.024.
Values may be sent and summed in bfloat16 or wider, within the bound.
No kernel may reach another device: no remote copies, remote signals or barrier semaphores. Data moves between devices by JAX's collectives and lax.ppermute only.
A program may use at most 256 MiB of HBM per device.

```python
import math
import jax
import jax.numpy as jnp
import numpy as np
from jax import lax

MODEL_WIDTH = 1536
QUERY_HEADS = 24
KEY_HEADS = 8
HEAD_SIZE = 64
EXPERT_HIDDEN = 512
TOPK = 8
ADAPTER_RANK = 16
ADAPTER_CHOICES = 8
TOK_DEV = 128
EXPERT_COUNT = 20
SEQ = 512
SEQS = 8
QUERY_FEATURES = 1536
KEY_FEATURES = 512
CAP = 76
N_CTX = 4


def set_ends(entries, own_key, smallest, high):
    extent = entries.shape
    index_at = [jax.random.randint(jax.random.fold_in(own_key, axis), (), 0, extent[axis]) for axis in range(len(extent))]
    entries = entries.at[tuple(index_at)].set(smallest)
    longest = extent.index(max(extent))
    index_at[longest] = (index_at[longest] + 1) % extent[longest]
    return entries.at[tuple(index_at)].set(high)


def block_scale(own_key, dims, cuts, least, largest):
    def one(axis_at, shards_of):
        steps = jax.random.uniform(jax.random.fold_in(jax.random.fold_in(own_key, 6), axis_at), (shards_of,), jnp.float32, least / len(cuts), largest / len(cuts))
        return jnp.repeat(jnp.exp(steps), dims[axis_at] // shards_of).reshape((-1,) + (1,) * (len(dims) - axis_at - 1))

    gain = one(*cuts[0])
    for cut in cuts[1:]:
        gain = gain * one(*cut)
    return gain


def deal_out(stream_key, own, number, rows, number_of, top, bound, slope):
    ranking = jax.random.permutation(stream_key, number_of)
    crowded, ordinary = shares(number_of, rows * top, bound, slope, True), shares(number_of, rows * top, bound, slope, False)
    places = jnp.arange(number_of)

    def named(tallies, rotation):
        used = int((tallies > 0).sum())
        fixed = max(1, used // 4)
        moved = fixed + (places - fixed + rotation * (used - fixed)) % max(1, number_of - fixed)
        return jnp.zeros((number_of,), jnp.int32).at[ranking[jnp.where(places < fixed, places, moved)]].set(jnp.asarray(tallies, jnp.int32))

    tallies = jnp.where(number % 4 == 0, named(crowded, number // 4), named(ordinary, number - number // 4 - 1))
    mixed = jax.random.permutation(jax.random.fold_in(own, 3), number_of)
    donor, receiver = mixed[0:number_of // 2 * 2:2], mixed[1:number_of // 2 * 2:2]
    slack = jnp.minimum(tallies[donor] - 1, bound - tallies[receiver]) // 2
    slack = jnp.where((donor == ranking[0]) | (receiver == ranking[0]) | (tallies[receiver] == 0), 0, jnp.maximum(slack, 0))
    moved = jax.random.randint(jax.random.fold_in(own, 4), (number_of // 2,), 0, 1 << 20) % (slack + 1)
    tallies = tallies.at[donor].add(-moved).at[receiver].add(moved)
    members = jnp.searchsorted(jnp.cumsum(tallies), jnp.arange(rows * top), side="right").astype(jnp.int32)
    table = members.reshape(top, rows).T
    table = table[jax.random.permutation(jax.random.fold_in(own, 1), rows)]
    rotation = jax.random.randint(jax.random.fold_in(own, 2), (rows, 1), 0, top)
    return jnp.take_along_axis(table, (jnp.arange(top)[None, :] + rotation) % top, axis=1)


def shares(count, total, reach, slope, full):
    weights = [(1 << 20) // math.isqrt(rank ** slope) + 1 for rank in range(1, count + 1)]
    largest = reach if full else min(reach, max(-(-total // count), total * weights[0] // sum(weights)))
    least = 1 if total - largest >= count - 1 else 0
    holding, spare = [largest] + [least] * (count - 1), total - largest - least * (count - 1)
    while spare > 0:
        movable = [i for i in range(1, count) if holding[i] < largest] or [i for i in range(1, count) if holding[i] < reach]
        whole, left = sum([weights[i] for i in movable]), spare
        for i in movable:
            extra = min(reach - holding[i], max(1, left * weights[i] // whole), spare)
            holding[i] = holding[i] + extra
            spare = spare - extra
    return np.array(holding)


def centred(own_key, dims, deviation, bound, split=(), held_as=jnp.bfloat16):
    values = jax.random.normal(own_key, dims, jnp.float32) * deviation
    if len(split) > 0:
        values = block_scale(own_key, dims, split, -0.22, 0.18) * values
    return jnp.clip(values, min=-bound, max=bound).astype(held_as)


def setup_inputs(seed: int = 0) -> dict:
    streams_of = jax.random.split(jax.random.key(seed), 23)
    layer_input_rows = centred(streams_of[0], (SEQS, SEQ, MODEL_WIDTH), 1.0, 6.0, ((0, 8), (1, 4)))
    routes_keys = jax.random.split(jax.random.fold_in(streams_of[1], 1), SEQS * SEQ // TOK_DEV)
    routes_turns = jax.random.permutation(jax.random.fold_in(streams_of[1], 3), SEQS * SEQ // TOK_DEV)
    routes = jax.vmap(lambda own, number: deal_out(jax.random.fold_in(streams_of[1], 2), own, number, TOK_DEV, EXPERT_COUNT, TOPK, CAP, 1))(routes_keys, routes_turns).reshape((SEQS, SEQ, TOPK))
    prefix = set_ends(jax.random.randint(streams_of[2], (SEQS,), 1, SEQ + 1), jax.random.fold_in(streams_of[2], 1), 1, SEQ).astype(jnp.int32)
    sequence_adapter_index = set_ends(jax.random.randint(streams_of[3], (SEQS,), 0, ADAPTER_CHOICES), jax.random.fold_in(streams_of[3], 1), 0, ADAPTER_CHOICES - 1).astype(jnp.int32)
    attention_norm_gain = jnp.clip(1.0 + 0.18 * jax.random.normal(streams_of[4], (MODEL_WIDTH,), jnp.float32), 0.1, 1.9)
    expert_norm_gain = jnp.clip(1.0 + 0.18 * jax.random.normal(streams_of[5], (MODEL_WIDTH,), jnp.float32), 0.1, 1.9)
    query_weight = centred(streams_of[6], (MODEL_WIDTH, QUERY_FEATURES), MODEL_WIDTH ** -0.5, 0.15625)
    key_value_weight = centred(streams_of[7], (MODEL_WIDTH, 2 * KEY_FEATURES), MODEL_WIDTH ** -0.5, 0.15625)
    projection_weight = centred(streams_of[8], (QUERY_FEATURES, MODEL_WIDTH), 32 ** -0.5, 1.0)
    router_weight = centred(streams_of[9], (MODEL_WIDTH, EXPERT_COUNT), (4 * MODEL_WIDTH) ** -0.5, 0.078125)
    gate_up_weight = centred(streams_of[10], (EXPERT_COUNT, MODEL_WIDTH, 2 * EXPERT_HIDDEN), MODEL_WIDTH ** -0.5, 0.15625, ((0, 4),))
    down_weight = centred(streams_of[11], (EXPERT_COUNT, EXPERT_HIDDEN, MODEL_WIDTH), (EXPERT_HIDDEN // 16) ** -0.5, 1.0, ((0, 4),))
    adapter_query_key_value_input = centred(streams_of[12], (ADAPTER_CHOICES, MODEL_WIDTH, 3 * ADAPTER_RANK), MODEL_WIDTH ** -0.5, 0.15625)
    adapter_query_output = centred(streams_of[13], (ADAPTER_CHOICES, ADAPTER_RANK, QUERY_FEATURES), (ADAPTER_RANK * 32) ** -0.5, 0.25)
    adapter_key_value_output = centred(streams_of[14], (ADAPTER_CHOICES, 2, ADAPTER_RANK, KEY_FEATURES), (ADAPTER_RANK * 32) ** -0.5, 0.25)
    adapter_projection_input = centred(streams_of[15], (ADAPTER_CHOICES, QUERY_FEATURES, ADAPTER_RANK), QUERY_FEATURES ** -0.5, 0.15625)
    adapter_projection_output = centred(streams_of[16], (ADAPTER_CHOICES, ADAPTER_RANK, MODEL_WIDTH), (ADAPTER_RANK * 32) ** -0.5, 0.25)
    adapter_gate_up_input = centred(streams_of[17], (ADAPTER_CHOICES, EXPERT_COUNT, MODEL_WIDTH, 2 * ADAPTER_RANK), MODEL_WIDTH ** -0.5, 0.15625, ((1, 4),))
    adapter_gate_up_output = centred(streams_of[18], (ADAPTER_CHOICES, EXPERT_COUNT, 2, ADAPTER_RANK, EXPERT_HIDDEN), (ADAPTER_RANK * 32) ** -0.5, 0.25, ((1, 4),))
    adapter_down_input = centred(streams_of[19], (ADAPTER_CHOICES, EXPERT_COUNT, EXPERT_HIDDEN, ADAPTER_RANK), EXPERT_HIDDEN ** -0.5, 0.25, ((1, 4),))
    adapter_down_output = centred(streams_of[20], (ADAPTER_CHOICES, EXPERT_COUNT, ADAPTER_RANK, MODEL_WIDTH), (ADAPTER_RANK * 32) ** -0.5, 0.25, ((1, 4),))
    cotangent = centred(streams_of[21], (SEQS, SEQ, MODEL_WIDTH), 1.0, 6.0, ((0, 8), (1, 4)))
    return {"layer_input_rows": layer_input_rows, "routes": routes, "prefix": prefix, "sequence_adapter_index": sequence_adapter_index, "attention_norm_gain": attention_norm_gain, "expert_norm_gain": expert_norm_gain, "query_weight": query_weight, "key_value_weight": key_value_weight, "projection_weight": projection_weight, "router_weight": router_weight, "gate_up_weight": gate_up_weight, "down_weight": down_weight, "adapter_query_key_value_input": adapter_query_key_value_input, "adapter_query_output": adapter_query_output, "adapter_key_value_output": adapter_key_value_output, "adapter_projection_input": adapter_projection_input, "adapter_projection_output": adapter_projection_output, "adapter_gate_up_input": adapter_gate_up_input, "adapter_gate_up_output": adapter_gate_up_output, "adapter_down_input": adapter_down_input, "adapter_down_output": adapter_down_output, "cotangent": cotangent}


@jax.custom_vjp
def rank_rows(v):
    return lax.optimization_barrier(v.astype(jnp.bfloat16)).astype(jnp.float32)

@jax.custom_vjp
def rank_rows_backward(v):
    return v

def low_keep(v):
    return (rank_rows(v), None)

def low_pass(kept, grad):
    return (grad,)

def back_keep(v):
    return (v, None)

def back_low(kept, grad):
    return (rank_rows(grad),)
rank_rows.defvjp(low_keep, low_pass)
rank_rows_backward.defvjp(back_keep, back_low)
EPS = 1e-05
ADAPTER_SCALE = 2.0
ROPE_BASE = 10000.0
MASKED = -1e+30
HIGHEST = lax.Precision.HIGHEST

def matrix_product(left_side, right_side):
    return jnp.matmul(left_side, right_side, precision=HIGHEST)

def rms_norm(values, gain_vec):
    return values * lax.rsqrt(lax.optimization_barrier(jnp.mean(values * values, axis=-1, keepdims=True)) + EPS) * gain_vec

def rope_tables(positions):
    half_dim = HEAD_SIZE // 2
    frequency = ROPE_BASE ** (-jnp.arange(half_dim, dtype=jnp.float32) / half_dim)
    angles = positions[:, None] * frequency[None, :]
    return (jnp.cos(angles), jnp.sin(angles))

def rotate_pairs(values, cosine_table, sine_table):
    half_dim = HEAD_SIZE // 2
    first_half = values[..., :half_dim]
    second_half = values[..., half_dim:]
    cosine_table = cosine_table[:, None, :]
    sine_table = sine_table[:, None, :]
    return jnp.concatenate([first_half * cosine_table - second_half * sine_table, second_half * cosine_table + first_half * sine_table], axis=-1)

def softmax_rows(scores):
    shifted = jnp.exp(scores - lax.optimization_barrier(jnp.max(scores, axis=-1, keepdims=True)))
    return shifted / lax.optimization_barrier(jnp.sum(shifted, axis=-1, keepdims=True))

def sequence_forward(input_rows, attention_adapter, expert_adapter, routing_weights, prefix_length, adapter_choice, routed_experts):
    query_weight, key_value_weight, projection_weight, router_weight, gate_up_weight, down_weight, attention_norm_gain, expert_norm_gain = routing_weights
    query_key_value_input_map, query_output_map, key_value_output_map, projection_input_map, projection_output_map = attention_adapter
    gate_up_input_map, gate_up_output_map, down_input_map, down_output_map = expert_adapter
    sequence_length = input_rows.shape[0]
    normed_rows = rank_rows(rms_norm(input_rows, attention_norm_gain))
    adapter_input = rank_rows(rank_rows_backward(matrix_product(normed_rows, query_key_value_input_map[adapter_choice])))
    query_preactivation = matrix_product(normed_rows, query_weight) + ADAPTER_SCALE * matrix_product(adapter_input[:, :ADAPTER_RANK], query_output_map[adapter_choice])
    key_value = matrix_product(normed_rows, key_value_weight)
    key_preactivation = key_value[:, :KEY_FEATURES] + ADAPTER_SCALE * matrix_product(adapter_input[:, ADAPTER_RANK:2 * ADAPTER_RANK], key_value_output_map[adapter_choice, 0])
    value_preactivation = key_value[:, KEY_FEATURES:] + ADAPTER_SCALE * matrix_product(adapter_input[:, 2 * ADAPTER_RANK:], key_value_output_map[adapter_choice, 1])
    cosine_table, sine_table = rope_tables(jnp.arange(sequence_length).astype(jnp.float32))
    query_rows = rank_rows(rotate_pairs(rank_rows_backward(query_preactivation).reshape(sequence_length, QUERY_HEADS, HEAD_SIZE), cosine_table, sine_table))
    key_row_block = rank_rows(rotate_pairs(rank_rows_backward(key_preactivation).reshape(sequence_length, KEY_HEADS, HEAD_SIZE), cosine_table, sine_table))
    value_row_block = rank_rows(rank_rows_backward(value_preactivation)).reshape(sequence_length, KEY_HEADS, HEAD_SIZE)
    head_groups = QUERY_HEADS // KEY_HEADS
    block_row_count = min(512, sequence_length)
    key_pos = jnp.arange(sequence_length).astype(jnp.int32)
    scaling = HEAD_SIZE ** (-0.5)

    def attend(starting_row):
        query_block = lax.dynamic_slice_in_dim(query_rows, starting_row, block_row_count, 0).reshape(block_row_count, KEY_HEADS, head_groups, HEAD_SIZE)
        scores = rank_rows_backward(jnp.einsum('qkgd,skd->kgqs', query_block, key_row_block, precision=HIGHEST) * scaling)
        query_pos = starting_row + jnp.arange(block_row_count).astype(jnp.int32)
        allowed = (key_pos[None, :] <= query_pos[:, None]) | (key_pos[None, :] < prefix_length)
        scores = jnp.where(allowed, scores, MASKED)
        attn_probs = rank_rows(softmax_rows(scores))
        return jnp.einsum('kgqs,skd->qkgd', attn_probs, value_row_block, precision=HIGHEST).reshape(block_row_count, QUERY_FEATURES)
    starts = (jnp.arange(sequence_length // block_row_count) * block_row_count).astype(jnp.int32)
    attended_rows = lax.map(jax.checkpoint(attend), starts).reshape(sequence_length, QUERY_FEATURES)
    attended_rows = rank_rows(rank_rows_backward(attended_rows))
    adapter_output = rank_rows(rank_rows_backward(matrix_product(attended_rows, projection_input_map[adapter_choice])))
    adapter_branch = rank_rows_backward(matrix_product(attended_rows, projection_weight) + ADAPTER_SCALE * matrix_product(adapter_output, projection_output_map[adapter_choice]))
    middle = input_rows + adapter_branch
    normed_ffn = rank_rows(rms_norm(middle, expert_norm_gain))
    logits = rank_rows_backward(matrix_product(normed_ffn, router_weight))
    experts_all = logits.shape[1]
    chosen = jnp.take_along_axis(logits, routed_experts, axis=1)
    gate_probs = softmax_rows(chosen)
    copies = rank_rows_backward(jnp.broadcast_to(normed_ffn[:, None, :], (sequence_length, TOPK, MODEL_WIDTH)))
    copies = copies.reshape(sequence_length * TOPK, MODEL_WIDTH)
    flat_ids = routed_experts.reshape(-1).astype(jnp.int32)
    sort_order = jnp.argsort(flat_ids, stable=True).astype(jnp.int32)
    expert_ids = jnp.arange(experts_all).astype(jnp.int32)
    counts = lax.optimization_barrier(jnp.sum((flat_ids[:, None] == expert_ids[None, :]).astype(jnp.int32), axis=0)).astype(jnp.int32)
    offsets = (jnp.cumsum(counts) - counts).astype(jnp.int32)
    rank_sorted = jnp.argsort(sort_order).astype(jnp.int32)
    buffer_rows = N_CTX * CAP
    slot_ids = flat_ids * buffer_rows + rank_sorted - offsets[flat_ids]
    padded = jnp.concatenate([sort_order, jnp.zeros((buffer_rows,), jnp.int32)])

    def expert_apply(expert_index):
        begin_at = offsets[expert_index].astype(jnp.int32)
        pick_rows = lax.dynamic_slice_in_dim(padded, begin_at, buffer_rows, 0)
        is_valid = jnp.arange(buffer_rows).astype(jnp.int32) < counts[expert_index]
        rows_in = jnp.where(is_valid[:, None], copies[pick_rows], 0.0)
        rank_input = rank_rows(rank_rows_backward(matrix_product(rows_in, gate_up_input_map[adapter_choice, expert_index])))
        gate_up_rows = matrix_product(rows_in, gate_up_weight[expert_index])
        gate_preactivation = rank_rows_backward(gate_up_rows[:, :EXPERT_HIDDEN] + ADAPTER_SCALE * matrix_product(rank_input[:, :ADAPTER_RANK], gate_up_output_map[adapter_choice, expert_index, 0]))
        up_preactivation = rank_rows_backward(gate_up_rows[:, EXPERT_HIDDEN:] + ADAPTER_SCALE * matrix_product(rank_input[:, ADAPTER_RANK:], gate_up_output_map[adapter_choice, expert_index, 1]))
        hidden_rows = rank_rows(gate_preactivation / (1.0 + jnp.exp(-gate_preactivation)) * up_preactivation)
        rank_middle = rank_rows(rank_rows_backward(matrix_product(hidden_rows, down_input_map[adapter_choice, expert_index])))
        result_rows = rank_rows(rank_rows_backward(matrix_product(hidden_rows, down_weight[expert_index]) + ADAPTER_SCALE * matrix_product(rank_middle, down_output_map[adapter_choice, expert_index])))
        return jnp.where(is_valid[:, None], result_rows, 0.0)
    results = lax.map(jax.checkpoint(expert_apply), expert_ids)
    expert_out = results.reshape(experts_all * buffer_rows, MODEL_WIDTH)[slot_ids].reshape(sequence_length, TOPK, MODEL_WIDTH)
    return middle + lax.optimization_barrier(jnp.sum(gate_probs[:, :, None] * expert_out, axis=1))

def reference(layer_input_rows, routes, prefix, sequence_adapter_index, attention_norm_gain, expert_norm_gain, query_weight, key_value_weight, projection_weight, router_weight, gate_up_weight, down_weight, adapter_query_key_value_input, adapter_query_output, adapter_key_value_output, adapter_projection_input, adapter_projection_output, adapter_gate_up_input, adapter_gate_up_output, adapter_down_input, adapter_down_output, cotangent):
    routing_weights = tuple((group_member.astype(jnp.float32) for group_member in (query_weight, key_value_weight, projection_weight, router_weight, gate_up_weight, down_weight, attention_norm_gain, expert_norm_gain)))
    attention_adapter = tuple((group_member.astype(jnp.float32) for group_member in (adapter_query_key_value_input, adapter_query_output, adapter_key_value_output, adapter_projection_input, adapter_projection_output)))
    expert_adapter = tuple((group_member.astype(jnp.float32) for group_member in (adapter_gate_up_input, adapter_gate_up_output, adapter_down_input, adapter_down_output)))
    initial_state = jax.tree.map(jnp.zeros_like, (attention_adapter, expert_adapter))

    def one_sequence(totals, inputs_item):
        token_input, routed_experts, prefix_length, adapter_choice, grad_out = inputs_item

        def layer_forward(tokens_f, attn_f, expert_f):
            return sequence_forward(tokens_f, attn_f, expert_f, routing_weights, prefix_length, adapter_choice, routed_experts)
        output_rows, pullback_function = jax.vjp(layer_forward, token_input.astype(jnp.float32), attention_adapter, expert_adapter)
        grad_tokens, attention_gradient, grad_expert = pullback_function(grad_out.astype(jnp.float32))
        totals = jax.tree.map(jnp.add, totals, (attention_gradient, grad_expert))
        return (totals, grad_tokens)
    totals, grad_x = lax.scan(one_sequence, initial_state, (layer_input_rows, routes, prefix, sequence_adapter_index, cotangent))
    attention_gradient, grad_expert = totals
    return (grad_x, attention_gradient[0], attention_gradient[1], attention_gradient[2], attention_gradient[3], attention_gradient[4], grad_expert[0], grad_expert[1], grad_expert[2], grad_expert[3])
```

```python
import jax
import jax.numpy as jnp
from jax import lax
from jax.sharding import PartitionSpec as P

MODEL_WIDTH = 1536
QUERY_HEADS = 24
KEY_HEADS = 8
HEAD_SIZE = 64
EXPERT_HIDDEN = 512
TOPK = 8
ADAPTER_RANK = 16
ADAPTER_CHOICES = 8
QUERY_FEATURES = 1536
KEY_FEATURES = 512
HEAD_GROUP = QUERY_HEADS // KEY_HEADS

EPS = 1e-05
ADAPTER_SCALE = 2.0
ROPE_BASE = 10000.0
MASKED = -1e30
F32 = jnp.float32
BF16 = jnp.bfloat16


def mm(left, right):
    return jnp.dot(left, right, preferred_element_type=F32)


def mm_nt(left, right):
    return lax.dot_general(left, right, (((1,), (1,)), ((), ())), preferred_element_type=F32)


def mm_tn(left, right):
    return lax.dot_general(left, right, (((0,), (0,)), ((), ())), preferred_element_type=F32)


def rotation(size, by):
    return [(i, (i + by) % size) for i in range(size)]


def ring_gather(block, size):
    blocks = [block]
    for _ in range(size - 1):
        blocks.append(lax.ppermute(blocks[-1], "ctx", rotation(size, 1)))
    return blocks


def rope_tables(positions):
    half = HEAD_SIZE // 2
    frequency = ROPE_BASE ** (-jnp.arange(half, dtype=F32) / half)
    angles = positions.astype(F32)[:, None] * frequency[None, :]
    return jnp.cos(angles), jnp.sin(angles)


def rotate(values, tables, direction):
    rows, width = values.shape
    half = HEAD_SIZE // 2
    heads = values.reshape(rows, width // HEAD_SIZE, HEAD_SIZE)
    first, second = heads[..., :half], heads[..., half:]
    cosine, sine = tables[0][:, None, :], direction * tables[1][:, None, :]
    turned = jnp.concatenate(
        [first * cosine - second * sine, second * cosine + first * sine], axis=-1
    )
    return turned.reshape(rows, width)


def heads_of(rows, count):
    return rows.reshape(rows.shape[0], count, HEAD_SIZE).transpose(1, 0, 2)


def grouped(rows):
    return rows.reshape(rows.shape[0], KEY_HEADS, HEAD_GROUP, HEAD_SIZE).transpose(1, 2, 0, 3)


def ungrouped(heads):
    return heads.transpose(2, 0, 1, 3).reshape(heads.shape[2], QUERY_FEATURES)


def chunked(wide, narrow, parts):
    rows = wide.shape[0]
    return jnp.concatenate(
        [
            wide.reshape(rows, parts, -1).transpose(1, 0, 2),
            narrow.reshape(rows, parts, -1).transpose(1, 0, 2),
        ],
        axis=2,
    ).astype(BF16)


def by_adapter(received, selector):
    return jnp.einsum("as,srw->arw", selector, received.astype(F32), precision="highest")


def shards(
    layer_input_rows,
    routes,
    prefix,
    sequence_adapter_index,
    attention_norm_gain,
    expert_norm_gain,
    query_weight,
    key_value_weight,
    projection_weight,
    router_weight,
    gate_up_weight,
    down_weight,
    adapter_query_key_value_input,
    adapter_query_output,
    adapter_key_value_output,
    adapter_projection_input,
    adapter_projection_output,
    adapter_gate_up_input,
    adapter_gate_up_output,
    adapter_down_input,
    adapter_down_output,
    cotangent,
):
    ctx_size = lax.axis_size("ctx")
    dp_size = lax.axis_size("dp")
    rank = lax.axis_index("ctx")
    own = layer_input_rows.shape[1]
    experts_here = gate_up_weight.shape[0]
    experts_all = experts_here * ctx_size
    scaling = HEAD_SIZE ** (-0.5)
    choice = sequence_adapter_index[0]
    prefix_length = prefix[0]

    def picked(table):
        return lax.dynamic_index_in_dim(table, choice, 0, keepdims=False)

    qkv_in = picked(adapter_query_key_value_input)
    query_out = picked(adapter_query_output)
    key_value_out = picked(adapter_key_value_output)
    proj_in = picked(adapter_projection_input)
    proj_out = picked(adapter_projection_output)
    gate_up_in = picked(adapter_gate_up_input)
    gate_up_out = picked(adapter_gate_up_output)
    down_in = picked(adapter_down_input)
    down_out = picked(adapter_down_output)

    choices_all = lax.all_gather(choice, "dp")
    selector = (
        jnp.arange(ADAPTER_CHOICES, dtype=jnp.int32)[:, None] == choices_all[None, :]
    ).astype(F32)

    order = (rank - jnp.arange(ctx_size, dtype=jnp.int32)) % ctx_size
    positions = (order[:, None] * own + jnp.arange(own, dtype=jnp.int32)[None, :]).reshape(-1)
    tables = rope_tables(positions)
    input_blocks = ring_gather(layer_input_rows[0], ctx_size)
    cot_own, input_last = lax.optimization_barrier((cotangent[0], input_blocks[-1]))
    input_blocks[-1] = input_last
    cot_rows = jnp.concatenate(ring_gather(cot_own, ctx_size), axis=0)
    routes_all = lax.all_gather(routes[0], "ctx")[order].reshape(-1, TOPK)
    input_rows = jnp.concatenate(input_blocks, axis=0).astype(F32)

    inv_attn = lax.rsqrt(jnp.mean(input_rows * input_rows, axis=-1, keepdims=True) + EPS)
    normed = (input_rows * inv_attn * attention_norm_gain).astype(BF16)
    lora_in = mm(normed, qkv_in).astype(BF16)
    query_pre = mm(normed, query_weight) + ADAPTER_SCALE * mm(lora_in[:, :ADAPTER_RANK], query_out)
    key_value = mm(normed, key_value_weight)
    key_pre = key_value[:, :KEY_FEATURES] + ADAPTER_SCALE * mm(
        lora_in[:, ADAPTER_RANK : 2 * ADAPTER_RANK], key_value_out[0]
    )
    value_pre = key_value[:, KEY_FEATURES:] + ADAPTER_SCALE * mm(
        lora_in[:, 2 * ADAPTER_RANK :], key_value_out[1]
    )
    queries = rotate(query_pre, tables, 1.0).astype(BF16)
    keys = heads_of(rotate(key_pre, tables, 1.0).astype(BF16), KEY_HEADS)
    values = heads_of(value_pre.astype(BF16), KEY_HEADS)
    query_heads = grouped(queries)
    allowed = (positions[None, :] <= positions[:, None]) | (positions[None, :] < prefix_length)

    def scores_of(head_q, head_k, mask):
        scores = jnp.einsum("gtd,sd->gts", head_q, head_k, preferred_element_type=F32) * scaling
        return jnp.where(mask, scores, MASKED)

    def forward(operands):
        head_q, head_k, head_v = operands
        scores = scores_of(head_q, head_k, allowed)
        top = jnp.max(scores, axis=-1, keepdims=True)
        shifted = jnp.exp(scores - top)
        total = jnp.sum(shifted, axis=-1, keepdims=True)
        probs = (shifted / total).astype(BF16)
        out = jnp.einsum("gts,sd->gtd", probs, head_v, preferred_element_type=F32)
        return out.astype(BF16), (top + jnp.log(total))[:, :own]

    attended_heads, log_total = lax.map(forward, (query_heads, keys, values))
    attended = ungrouped(attended_heads)
    lora_out = mm(attended, proj_in).astype(BF16)
    middle = input_rows + (mm(attended, projection_weight) + ADAPTER_SCALE * mm(lora_out, proj_out))
    inv_ffn = lax.rsqrt(jnp.mean(middle * middle, axis=-1, keepdims=True) + EPS)
    normed_ffn = (middle * inv_ffn * expert_norm_gain).astype(BF16)
    logits = mm(normed_ffn, router_weight)
    expert_ids = jnp.arange(experts_all, dtype=jnp.int32)
    named = jnp.any(routes_all[:, :, None] == expert_ids[None, None, :], axis=1)
    chosen = jnp.where(named, logits, MASKED)
    weights = jnp.where(named, jnp.exp(chosen - jnp.max(chosen, axis=-1, keepdims=True)), 0.0)
    gates = weights / jnp.sum(weights, axis=-1, keepdims=True)
    gates_here = lax.dynamic_slice_in_dim(gates, rank * experts_here, experts_here, 1)

    grad_rows = jnp.zeros((ctx_size * own, MODEL_WIDTH), F32)
    gate_grads, wide, narrow = [], [], []
    for e in range(experts_here):
        gate_of = gates_here[:, e : e + 1]
        rank_in = mm(normed_ffn, gate_up_in[e]).astype(BF16)
        gate_up = mm(normed_ffn, gate_up_weight[e])
        gate_pre = gate_up[:, :EXPERT_HIDDEN] + ADAPTER_SCALE * mm(
            rank_in[:, :ADAPTER_RANK], gate_up_out[e, 0]
        )
        up_pre = gate_up[:, EXPERT_HIDDEN:] + ADAPTER_SCALE * mm(
            rank_in[:, ADAPTER_RANK:], gate_up_out[e, 1]
        )
        sig = 1.0 / (1.0 + jnp.exp(-gate_pre))
        silu = gate_pre * sig
        hidden = (silu * up_pre).astype(BF16)
        rank_mid = mm(hidden, down_in[e]).astype(BF16)
        cot_mid = ADAPTER_SCALE * mm_nt(cot_rows, down_out[e])
        cot_hidden = mm_nt(cot_rows, down_weight[e])
        gate_grads.append(
            jnp.sum(hidden.astype(F32) * cot_hidden, axis=-1)
            + jnp.sum(rank_mid.astype(F32) * cot_mid, axis=-1)
        )
        grad_rank_mid = (gate_of * cot_mid).astype(BF16)
        grad_hidden = gate_of * cot_hidden + mm_nt(grad_rank_mid, down_in[e])
        grad_gate = (grad_hidden * up_pre * sig * (1.0 + gate_pre * (1.0 - sig))).astype(BF16)
        grad_up = (grad_hidden * silu).astype(BF16)
        grad_rank_in = (
            ADAPTER_SCALE
            * jnp.concatenate(
                [mm_nt(grad_gate, gate_up_out[e, 0]), mm_nt(grad_up, gate_up_out[e, 1])], axis=1
            )
        ).astype(BF16)
        grad_rows = (
            grad_rows
            + mm_nt(grad_gate, gate_up_weight[e, :, :EXPERT_HIDDEN])
            + mm_nt(grad_up, gate_up_weight[e, :, EXPERT_HIDDEN:])
            + mm_nt(grad_rank_in, gate_up_in[e])
        )
        wide.append(mm_tn(grad_rank_in, normed_ffn))
        wide.append(
            ADAPTER_SCALE * mm_tn((gate_of * rank_mid.astype(F32)).astype(BF16), cot_rows)
        )
        narrow.append(ADAPTER_SCALE * mm_tn(rank_in[:, :ADAPTER_RANK], grad_gate))
        narrow.append(ADAPTER_SCALE * mm_tn(rank_in[:, ADAPTER_RANK:], grad_up))
        narrow.append(mm_tn(grad_rank_mid, hidden))
    expert_rows = chunked(jnp.concatenate(wide), jnp.concatenate(narrow), dp_size)
    expert_got = lax.all_to_all(expert_rows, "dp", 0, 0, tiled=True)

    partial = grad_rows.astype(BF16).reshape(ctx_size, own, MODEL_WIDTH)
    grad_normed_ffn = partial[0].astype(F32)
    gate_grads = jnp.stack(gate_grads, axis=0).reshape(experts_here, ctx_size, own)
    gate_blocks = [gate_grads[:, 0]]
    for j in range(1, ctx_size):
        back = rotation(ctx_size, -j)
        grad_normed_ffn = grad_normed_ffn + lax.ppermute(partial[j], "ctx", back).astype(F32)
        gate_blocks.append(lax.ppermute(gate_grads[:, j], "ctx", back))
    grad_gates = jnp.concatenate(gate_blocks, axis=0)
    grad_gates = jnp.roll(grad_gates, rank * experts_here, axis=0).T
    gates_own = gates[:own]
    grad_chosen = gates_own * (
        grad_gates - jnp.sum(gates_own * grad_gates, axis=-1, keepdims=True)
    )
    grad_normed_ffn = grad_normed_ffn + mm_nt(grad_chosen.astype(BF16), router_weight)
    middle_own, inv_own = middle[:own], inv_ffn[:own]
    scaled_ffn = grad_normed_ffn * expert_norm_gain
    grad_middle = (
        cot_own.astype(F32)
        + inv_own * scaled_ffn
        - middle_own * inv_own**3 * jnp.mean(scaled_ffn * middle_own, axis=-1, keepdims=True)
    )
    grad_branch = grad_middle.astype(BF16)
    grad_lora_out = (ADAPTER_SCALE * mm_nt(grad_branch, proj_out)).astype(BF16)
    grad_attended = (mm_nt(grad_branch, projection_weight) + mm_nt(grad_lora_out, proj_in)).astype(
        BF16
    )
    grad_out_b = ADAPTER_SCALE * mm_tn(lora_out[:own], grad_branch)
    grad_out_a = mm_tn(grad_lora_out, attended[:own])

    own_allowed = allowed[:own]

    def backward(operands):
        head_q, head_k, head_v, head_grad, head_log = operands
        probs = jnp.exp(scores_of(head_q, head_k, own_allowed) - head_log)
        grad_probs = jnp.einsum("gtd,sd->gts", head_grad, head_v, preferred_element_type=F32)
        grad_scores = (
            probs * (grad_probs - jnp.sum(probs * grad_probs, axis=-1, keepdims=True))
        ).astype(BF16)
        grad_q = scaling * jnp.einsum(
            "gts,sd->gtd", grad_scores, head_k, preferred_element_type=F32
        )
        grad_k = scaling * jnp.einsum(
            "gts,gtd->sd", grad_scores, head_q, preferred_element_type=F32
        )
        grad_v = jnp.einsum(
            "gts,gtd->sd", probs.astype(BF16), head_grad, preferred_element_type=F32
        )
        return grad_q, grad_k, grad_v

    grad_q, grad_k, grad_v = lax.map(
        backward, (query_heads[:, :, :own], keys, values, grouped(grad_attended), log_total)
    )
    tables_own = (tables[0][:own], tables[1][:own])
    grad_query_pre = rotate(ungrouped(grad_q), tables_own, -1.0).astype(BF16)
    key_part = rotate(
        grad_k.transpose(1, 0, 2).reshape(ctx_size * own, KEY_FEATURES), tables, -1.0
    ).astype(BF16)
    value_part = grad_v.transpose(1, 0, 2).reshape(ctx_size * own, KEY_FEATURES).astype(BF16)
    part = jnp.concatenate([key_part, value_part], axis=1)
    blocks = part.reshape(ctx_size, own, 2 * KEY_FEATURES)
    grad_key_value = blocks[0].astype(F32)
    for j in range(1, ctx_size):
        grad_key_value = grad_key_value + lax.ppermute(
            blocks[j], "ctx", rotation(ctx_size, -j)
        ).astype(F32)
    grad_key_value = grad_key_value.astype(BF16)

    lora_q = (ADAPTER_SCALE * mm_nt(grad_query_pre, query_out)).astype(BF16)
    lora_k = (ADAPTER_SCALE * mm_nt(key_part, key_value_out[0])).astype(BF16)
    lora_v = (ADAPTER_SCALE * mm_nt(value_part, key_value_out[1])).astype(BF16)
    wide = jnp.concatenate(
        [
            mm_tn(lora_q, normed[:own]),
            mm_tn(lora_k, normed),
            mm_tn(lora_v, normed),
            ADAPTER_SCALE * mm_tn(lora_in[:own, :ADAPTER_RANK], grad_query_pre),
            grad_out_a,
            grad_out_b,
        ]
    )
    narrow = jnp.concatenate(
        [
            ADAPTER_SCALE * mm_tn(lora_in[:, ADAPTER_RANK : 2 * ADAPTER_RANK], key_part),
            ADAPTER_SCALE * mm_tn(lora_in[:, 2 * ADAPTER_RANK :], value_part),
            jnp.zeros((4 * ADAPTER_RANK, KEY_FEATURES), F32),
        ]
    )
    attention_rows = chunked(wide, narrow, dp_size)
    rows_count = 6 * ADAPTER_RANK // ctx_size
    pieces = attention_rows.reshape(dp_size, ctx_size, rows_count, -1)

    def piece(j):
        return lax.dynamic_index_in_dim(pieces, (rank + j) % ctx_size, 1, keepdims=False)

    share = piece(0).astype(F32)
    for j in range(1, ctx_size):
        share = share + lax.ppermute(piece(j), "ctx", rotation(ctx_size, j)).astype(F32)
    share = lax.all_to_all(share.astype(BF16), "dp", 0, 0, tiled=True)
    share = by_adapter(share, selector).astype(BF16)
    attention_sum = [share]
    for j in range(1, ctx_size):
        attention_sum.append(lax.ppermute(share, "ctx", rotation(ctx_size, j)))
    attention_sum = jnp.stack(attention_sum, axis=1)
    attention_sum = jnp.take(attention_sum, order, axis=1)
    attention_sum = attention_sum.reshape(ADAPTER_CHOICES, 6 * ADAPTER_RANK, -1).astype(F32)
    expert_sum = by_adapter(expert_got, selector)

    grad_key_own = grad_key_value[:, :KEY_FEATURES]
    grad_value_own = grad_key_value[:, KEY_FEATURES:]
    grad_lora_in = (
        ADAPTER_SCALE
        * jnp.concatenate(
            [
                mm_nt(grad_query_pre, query_out),
                mm_nt(grad_key_own, key_value_out[0]),
                mm_nt(grad_value_own, key_value_out[1]),
            ],
            axis=1,
        )
    ).astype(BF16)
    grad_normed = (
        mm_nt(grad_query_pre, query_weight)
        + mm_nt(grad_key_value, key_value_weight)
        + mm_nt(grad_lora_in, qkv_in)
    )
    scaled_attn = grad_normed * attention_norm_gain
    rows_own, inv_first = input_rows[:own], inv_attn[:own]
    grad_inputs = (
        grad_middle
        + inv_first * scaled_attn
        - rows_own * inv_first**3 * jnp.mean(scaled_attn * rows_own, axis=-1, keepdims=True)
    )

    wide_width = MODEL_WIDTH // dp_size
    r = ADAPTER_RANK
    attn_wide, attn_narrow = attention_sum[..., :wide_width], attention_sum[..., wide_width:]
    by_expert = expert_sum.reshape(ADAPTER_CHOICES, experts_here, 3 * r, -1)
    exp_wide, exp_narrow = by_expert[..., :wide_width], by_expert[..., wide_width:]
    return (
        grad_inputs[None],
        attn_wide[:, : 3 * r].transpose(0, 2, 1),
        attn_wide[:, 3 * r : 4 * r],
        attn_narrow[:, : 2 * r].reshape(ADAPTER_CHOICES, 2, r, -1),
        attn_wide[:, 4 * r : 5 * r].transpose(0, 2, 1),
        attn_wide[:, 5 * r :],
        exp_wide[:, :, : 2 * r].transpose(0, 1, 3, 2),
        exp_narrow[:, :, : 2 * r].reshape(ADAPTER_CHOICES, experts_here, 2, r, -1),
        exp_narrow[:, :, 2 * r :].transpose(0, 1, 3, 2),
        exp_wide[:, :, 2 * r :],
    )


def solution(mesh):
    placed = (
        P("dp", "ctx", None),
        P("dp", "ctx", None),
        P("dp"),
        P("dp"),
        P(),
        P(),
        P(),
        P(),
        P(),
        P(),
        P("ctx", None, None),
        P("ctx", None, None),
        P(),
        P(),
        P(),
        P(),
        P(),
        P(None, "ctx", None, None),
        P(None, "ctx", None, None, None),
        P(None, "ctx", None, None),
        P(None, "ctx", None, None),
        P("dp", "ctx", None),
    )
    return jax.shard_map(
        shards,
        mesh=mesh,
        in_specs=placed,
        out_specs=(
            P("dp", "ctx", None),
            P(None, "dp", None),
            P(None, None, "dp"),
            P(None, None, None, "dp"),
            P(None, "dp", None),
            P(None, None, "dp"),
            P(None, "ctx", "dp", None),
            P(None, "ctx", None, None, "dp"),
            P(None, "ctx", "dp", None),
            P(None, "ctx", None, "dp"),
        ),
        check_vma=False,
    )
```

```python
import functools

import jax
import jax.numpy as jnp
from jax import lax
from jax.experimental import pallas as pl
from jax.experimental.pallas import tpu as pltpu
from jax.sharding import PartitionSpec as P

MODEL_WIDTH = 1536
QUERY_HEADS = 24
KEY_HEADS = 8
HEAD_SIZE = 64
EXPERT_HIDDEN = 512
TOPK = 8
ADAPTER_RANK = 16
ADAPTER_CHOICES = 8
QUERY_FEATURES = 1536
KEY_FEATURES = 512
LANES = 128
PAIRS = KEY_HEADS // 2
PAIR_QUERY = QUERY_FEATURES // PAIRS
COLUMNS = 512

EPS = 1e-05
ADAPTER_SCALE = 2.0
ROPE_BASE = 10000.0
MASKED = -1e30
SCALING = HEAD_SIZE ** (-0.5)
F32 = jnp.float32
BF16 = jnp.bfloat16
MIB = 1024 * 1024


def mm(left, right):
    return jnp.dot(left, right, preferred_element_type=F32)


def mm_nt(left, right):
    return lax.dot_general(left, right, (((1,), (1,)), ((), ())), preferred_element_type=F32)


def mm_tn(left, right):
    return lax.dot_general(left, right, (((0,), (0,)), ((), ())), preferred_element_type=F32)


def rotation(size, by):
    return [(i, (i + by) % size) for i in range(size)]


def ring_gather(block, size):
    blocks = [block]
    for _ in range(size - 1):
        blocks.append(lax.ppermute(blocks[-1], "ctx", rotation(size, 1)))
    return blocks[1:] + blocks[:1]


def low_lanes(shape):
    return lax.broadcasted_iota(jnp.int32, shape, 1) % LANES < HEAD_SIZE


def swapped(tile):
    return jnp.concatenate([tile[:, HEAD_SIZE:], tile[:, :HEAD_SIZE]], axis=1)


def turned(tile, cosine, sine):
    half = HEAD_SIZE // 2
    lane = lax.broadcasted_iota(jnp.int32, tile.shape, 1)
    other = jnp.where(
        lane % HEAD_SIZE < half, pltpu.roll(tile, LANES - half, 1), pltpu.roll(tile, half, 1)
    )
    return tile * cosine + other * sine


def placed_heads(tiles):
    return [
        tiles[0],
        swapped(tiles[0]),
        tiles[1],
        tiles[1],
        swapped(tiles[2]),
        tiles[2],
    ]


def lane_tiles(block):
    return [block[:, t * LANES : (t + 1) * LANES] for t in range(block.shape[1] // LANES)]


def call(kernel, scalars, grid, ins, outs, scratch, flops, vmem=48):
    bytes_accessed = sum(a.size * a.dtype.itemsize for a, _, _ in ins)
    return pl.pallas_call(
        kernel,
        grid_spec=pltpu.PrefetchScalarGridSpec(
            num_scalar_prefetch=1,
            grid=(grid,),
            in_specs=[pl.BlockSpec(b, m) for _, b, m in ins],
            out_specs=[pl.BlockSpec(b, m) for _, _, b, m in outs],
            scratch_shapes=scratch,
        ),
        out_shape=[jax.ShapeDtypeStruct(s, d) for s, d, _, _ in outs],
        compiler_params=pltpu.CompilerParams(
            vmem_limit_bytes=vmem * MIB, dimension_semantics=("arbitrary",)
        ),
        cost_estimate=pl.CostEstimate(
            flops=flops, bytes_accessed=bytes_accessed, transcendentals=0
        ),
    )(scalars, *[a for a, _, _ in ins])


def whole(array):
    return (array, array.shape, lambda i, s, n=array.ndim: (0,) * n)


def whole_out(shape, dtype):
    return (shape, dtype, shape, lambda i, s, n=len(shape): (0,) * n)


def chosen_whole(table):
    rest = table.shape[1:]
    return (table, (1,) + rest, lambda i, s, n=len(rest): (s[0],) + (0,) * n)


def qkv_kernel(blocks, scalars, *refs):
    xs, refs = refs[:blocks], refs[blocks:]
    gain, down, query_w, kv_w, query_out, kv_out, cosine, sine = refs[:8]
    q_ref, k_ref, v_ref, normed_ref, lora_ref = refs[8:]
    step = pl.program_id(0)
    q_steps = QUERY_FEATURES // COLUMNS

    @pl.when(step == 0)
    def _():
        rows = xs[0].shape[0]
        for b, x_ref in enumerate(xs):
            x = x_ref[...].astype(F32)
            inv = lax.rsqrt(jnp.mean(x * x, axis=-1, keepdims=True) + EPS)
            normed_ref[b * rows : (b + 1) * rows] = (x * inv * gain[...]).astype(BF16)
        lora_ref[...] = mm_nt(normed_ref[...], down[0]).astype(BF16)

    def rope_to(out_ref, pre, scale):
        cos, sin = cosine[...] * scale, sine[...] * scale
        for t, tile in enumerate(lane_tiles(pre)):
            out_ref[:, t * LANES : (t + 1) * LANES] = turned(tile, cos, sin).astype(BF16)

    r = ADAPTER_RANK

    @pl.when(step < q_steps)
    def _():
        pre = mm(normed_ref[...], query_w[...])
        pre = pre + mm(lora_ref[:, :r] * ADAPTER_SCALE, query_out[0])
        rope_to(q_ref, pre, SCALING)

    @pl.when(step == q_steps)
    def _():
        pre = mm(normed_ref[...], kv_w[...])
        pre = pre + mm(lora_ref[:, r : 2 * r] * ADAPTER_SCALE, kv_out[0, 0])
        rope_to(k_ref, pre, 1.0)

    @pl.when(step == q_steps + 1)
    def _():
        pre = mm(normed_ref[...], kv_w[...])
        v_ref[...] = (pre + mm(lora_ref[:, 2 * r :] * ADAPTER_SCALE, kv_out[0, 1])).astype(BF16)


def qkv(scalars, xs, gain, down, query_w, kv_w, query_out, kv_out, cosine, sine):
    rows = sum(x.shape[0] for x in xs)
    q_steps = QUERY_FEATURES // COLUMNS
    last = q_steps - 1
    return call(
        functools.partial(qkv_kernel, len(xs)),
        scalars,
        q_steps + 2,
        [whole(x) for x in xs]
        + [
            whole(gain),
            chosen_whole(down),
            (query_w, (MODEL_WIDTH, COLUMNS), lambda i, s: (0, jnp.minimum(i, last))),
            (kv_w, (MODEL_WIDTH, COLUMNS), lambda i, s: (0, jnp.maximum(i - q_steps, 0))),
            (query_out, (1, ADAPTER_RANK, COLUMNS), lambda i, s: (s[0], 0, jnp.minimum(i, last))),
            chosen_whole(kv_out),
            whole(cosine),
            whole(sine),
        ],
        [
            (
                (rows, QUERY_FEATURES),
                BF16,
                (rows, COLUMNS),
                lambda i, s: (0, jnp.minimum(i, last)),
            ),
            whole_out((rows, KEY_FEATURES), BF16),
            whole_out((rows, KEY_FEATURES), BF16),
            whole_out((rows, MODEL_WIDTH), BF16),
            whole_out((rows, 3 * ADAPTER_RANK), BF16),
        ],
        [],
        2 * rows * MODEL_WIDTH * (QUERY_FEATURES + 2 * KEY_FEATURES),
    )


def attend_kernel(blocks, with_own, scalars, *refs):
    xs, refs = refs[:blocks], refs[blocks:]
    q_ref, k_ref, v_ref, bias, proj_w, proj_in, proj_out, gain, router, named = refs[:10]
    outs = refs[10:]
    if with_own:
        normed_ref, gates_ref, att_ref, lora_ref, middle_ref, inv_ref, total, rank_total = outs
    else:
        normed_ref, gates_ref, total, rank_total = outs
    step = pl.program_id(0)
    own = xs[0].shape[0]

    keys, values = k_ref[...], v_ref[...]
    low = low_lanes(keys.shape)
    zero, one = jnp.zeros_like(keys), jnp.ones_like(values)
    key_of = [jnp.where(low, keys, zero), jnp.where(low, zero, keys)]
    value_of = [jnp.where(low, values, one), jnp.where(low, one, values)]
    heads = []
    for h, query in enumerate(placed_heads(lane_tiles(q_ref[...]))):
        scores = mm_nt(query, key_of[h // 3]) + bias[...]
        shifted = jnp.exp(scores - jnp.max(scores, axis=-1, keepdims=True)).astype(BF16)
        sums = mm(shifted, value_of[h // 3])
        heads.append(sums / pltpu.roll(sums, HEAD_SIZE, 1))
    low_q = low_lanes(heads[0].shape)
    attended = jnp.concatenate(
        [
            jnp.where(low_q, heads[0], pltpu.roll(heads[1], HEAD_SIZE, 1)),
            jnp.where(low_q, heads[2], heads[3]),
            jnp.where(low_q, pltpu.roll(heads[4], HEAD_SIZE, 1), heads[5]),
        ],
        axis=1,
    ).astype(BF16)
    if with_own:
        att_ref[...] = attended[-own:]
    part = mm(attended, proj_w[...])
    rank_part = mm_nt(attended, proj_in[0])

    @pl.when(step == 0)
    def _():
        total[...] = part
        rank_total[...] = rank_part

    @pl.when(step > 0)
    def _():
        total[...] += part
        rank_total[...] += rank_part

    @pl.when(step == PAIRS - 1)
    def _():
        lora_out = rank_total[...].astype(BF16)
        branch = total[...] + mm(lora_out * ADAPTER_SCALE, proj_out[0])
        for b, x_ref in enumerate(xs):
            middle = x_ref[...].astype(F32) + branch[b * own : (b + 1) * own]
            inv = lax.rsqrt(jnp.mean(middle * middle, axis=-1, keepdims=True) + EPS)
            normed_ref[b * own : (b + 1) * own] = (middle * inv * gain[...]).astype(BF16)
            if with_own and b == blocks - 1:
                middle_ref[...] = middle
                inv_ref[...] = inv
                lora_ref[...] = lora_out[b * own : (b + 1) * own]
        logits = mm_nt(normed_ref[...], router[...])
        mask = named[...] > 0.0
        chosen = jnp.where(mask, logits, MASKED)
        shifted = jnp.exp(chosen - jnp.max(chosen, axis=-1, keepdims=True))
        shifted = jnp.where(mask, shifted, 0.0)
        gates_ref[...] = shifted / jnp.sum(shifted, axis=-1, keepdims=True)


def attend(scalars, part, with_own, xs, q, k, v, bias, proj_w, proj_in, proj_out, gain, router, named):
    own = xs[0].shape[0]
    rows = own * len(xs)
    span = k.shape[0]
    experts = router.shape[0]
    outs = [
        whole_out((rows, MODEL_WIDTH), BF16),
        whole_out((rows, experts), F32),
    ]
    if with_own:
        outs += [
            ((own, QUERY_FEATURES), BF16, (own, PAIR_QUERY), lambda i, s: (0, i)),
            whole_out((own, ADAPTER_RANK), BF16),
            whole_out((own, MODEL_WIDTH), F32),
            whole_out((own, 1), F32),
        ]
    return call(
        functools.partial(attend_kernel, len(xs), with_own),
        scalars,
        PAIRS,
        [whole(x) for x in xs]
        + [
            (q, (rows, PAIR_QUERY), lambda i, s: (part, i)),
            (k, (span, LANES), lambda i, s: (0, i)),
            (v, (span, LANES), lambda i, s: (0, i)),
            (bias, (rows, span), lambda i, s: (part, 0)),
            (proj_w, (PAIR_QUERY, MODEL_WIDTH), lambda i, s: (i, 0)),
            (proj_in, (1, ADAPTER_RANK, PAIR_QUERY), lambda i, s: (s[0], 0, i)),
            chosen_whole(proj_out),
            whole(gain),
            whole(router),
            (named, (rows, experts), lambda i, s: (part, 0)),
        ],
        outs,
        [pltpu.VMEM((rows, MODEL_WIDTH), F32), pltpu.VMEM((rows, ADAPTER_RANK), F32)],
        4 * rows * span * QUERY_FEATURES + 2 * rows * MODEL_WIDTH * QUERY_FEATURES,
    )


def expert_kernel(blocks, parts, first, scalars, *refs):
    cots, refs = refs[:blocks], refs[blocks:]
    x_ref, gates, up_w, down_w, up_in, up_out, down_in, down_out = refs[:8]
    refs = refs[8:]
    if first:
        rows_ref, gg_ref, wide_ref, narrow_ref, cot_all, total, gg_all = refs
    else:
        wide_old, narrow_old, rows_ref, gg_ref, send_ref, cot_all, total, gg_all = refs
    step = pl.program_id(0)
    here = pl.num_programs(0)
    own = cots[0].shape[0]
    r = ADAPTER_RANK

    @pl.when(step == 0)
    def _():
        for b, cot in enumerate(cots):
            cot_all[b * own : (b + 1) * own] = cot[...]
        total[...] = jnp.zeros_like(total)
        gg_all[...] = jnp.zeros_like(gg_all)

    x, cot = x_ref[...], cot_all[...]
    lane = lax.broadcasted_iota(jnp.int32, gates.shape, 1)
    gate_of = jnp.sum(
        jnp.where(lane == scalars[2] * here + step, gates[...], 0.0), axis=1, keepdims=True
    )
    rank_in = mm_nt(x, up_in[0, 0]).astype(BF16)
    rank_in2 = rank_in * ADAPTER_SCALE
    gate_pre = mm(x, up_w[0, :, :EXPERT_HIDDEN]) + mm(rank_in2[:, :r], up_out[0, 0, 0])
    up_pre = mm(x, up_w[0, :, EXPERT_HIDDEN:]) + mm(rank_in2[:, r:], up_out[0, 0, 1])
    sig = 1.0 / (1.0 + jnp.exp(-gate_pre))
    silu = gate_pre * sig
    hidden = (silu * up_pre).astype(BF16)
    rank_mid = mm_nt(hidden, down_in[0, 0]).astype(BF16)
    cot_mid = ADAPTER_SCALE * mm_nt(cot, down_out[0, 0])
    cot_hidden = mm_nt(cot, down_w[0])
    gate_grad = jnp.sum(hidden.astype(F32) * cot_hidden, axis=1, keepdims=True) + jnp.sum(
        rank_mid.astype(F32) * cot_mid, axis=1, keepdims=True
    )
    gg_lane = lax.broadcasted_iota(jnp.int32, gg_all.shape, 1)
    gg_all[...] += jnp.where(gg_lane == step, gate_grad, 0.0)
    grad_rank_mid = (gate_of * cot_mid).astype(BF16)
    grad_hidden = gate_of * cot_hidden + mm(grad_rank_mid, down_in[0, 0])
    grad_up = (grad_hidden * silu).astype(BF16)
    grad_gate = (grad_hidden * up_pre * sig * (1.0 + gate_pre * (1.0 - sig))).astype(BF16)
    grad_rank_in = jnp.concatenate(
        [mm_nt(grad_gate, up_out[0, 0, 0]), mm_nt(grad_up, up_out[0, 0, 1])], axis=1
    )
    grad_rank_in = (ADAPTER_SCALE * grad_rank_in).astype(BF16)
    total[...] += (
        mm_nt(grad_gate, up_w[0, :, :EXPERT_HIDDEN])
        + mm_nt(grad_up, up_w[0, :, EXPERT_HIDDEN:])
        + mm(grad_rank_in, up_in[0, 0])
    )
    gated_mid = (ADAPTER_SCALE * gate_of * rank_mid.astype(F32)).astype(BF16)
    wide = jnp.concatenate([mm_tn(grad_rank_in, x), mm_tn(gated_mid, cot)], axis=0)
    narrow = jnp.concatenate(
        [
            mm_tn(rank_in2[:, :r], grad_gate),
            mm_tn(rank_in2[:, r:], grad_up),
            mm_tn(grad_rank_mid, hidden),
        ],
        axis=0,
    )
    if first:
        wide_ref[0] = wide
        narrow_ref[0] = narrow
    else:
        wide = (wide + wide_old[0]).astype(BF16)
        narrow = (narrow + narrow_old[0]).astype(BF16)
        at = pl.ds(pl.multiple_of(step * (3 * r), 16), 3 * r)
        w, v = MODEL_WIDTH // parts, EXPERT_HIDDEN // parts
        for p in range(parts):
            send_ref[p, at, :w] = wide[:, p * w : (p + 1) * w]
            send_ref[p, at, w:] = narrow[:, p * v : (p + 1) * v]

        @pl.when(step == 0)
        def _():
            tail = send_ref.shape[1] - here * 3 * r
            chosen = jnp.full((tail, w + v), scalars[0], jnp.int32).astype(F32).astype(BF16)
            for p in range(parts):
                send_ref[p, here * 3 * r :] = chosen

    @pl.when(step == here - 1)
    def _():
        rows_ref[...] = total[...].astype(BF16)
        gg_ref[...] = gg_all[...].T[: gg_ref.shape[0]]


def experts(scalars, parts, cots, x, gates, tables, before):
    up_w, down_w, up_in, up_out, down_in, down_out = tables
    own = cots[0].shape[0]
    rows = own * len(cots)
    here = up_w.shape[0]
    r = ADAPTER_RANK
    per_expert = lambda i, s: (i, 0, 0)
    ins = [whole(c) for c in cots] + [
        whole(x),
        whole(gates),
        (up_w, (1,) + up_w.shape[1:], per_expert),
        (down_w, (1,) + down_w.shape[1:], per_expert),
        (up_in, (1, 1) + up_in.shape[2:], lambda i, s: (s[0], i, 0, 0)),
        (up_out, (1, 1) + up_out.shape[2:], lambda i, s: (s[0], i, 0, 0, 0)),
        (down_in, (1, 1) + down_in.shape[2:], lambda i, s: (s[0], i, 0, 0)),
        (down_out, (1, 1) + down_out.shape[2:], lambda i, s: (s[0], i, 0, 0)),
    ]
    outs = [whole_out((rows, MODEL_WIDTH), BF16), whole_out((8, rows), F32)]
    if before is None:
        for width in (MODEL_WIDTH, EXPERT_HIDDEN):
            outs.append(((here, 3 * r, width), F32, (1, 3 * r, width), per_expert))
    else:
        ins += [(b, (1,) + b.shape[1:], per_expert) for b in before]
        width = (MODEL_WIDTH + EXPERT_HIDDEN) // parts
        outs.append(whole_out((parts, here * 3 * r + 16, width), BF16))
    return call(
        functools.partial(expert_kernel, len(cots), parts, before is None),
        scalars,
        here,
        ins,
        outs,
        [
            pltpu.VMEM((rows, MODEL_WIDTH), BF16),
            pltpu.VMEM((rows, MODEL_WIDTH), F32),
            pltpu.VMEM((rows, LANES), F32),
        ],
        here * 2 * rows * MODEL_WIDTH * EXPERT_HIDDEN * 5,
    )


def middle_kernel(blocks, scalars, *refs):
    parts, refs = refs[:blocks], refs[blocks:]
    gate_grads, gates, router, middle_ref, inv_ref, gain, cot = refs[:7]
    proj_w, proj_in, proj_out, q_ref, k_ref, v_ref, bias, cosine, sine = refs[7:16]
    grad_middle, branch_ref, lora_ref, gq_ref, gk_ref, gv_ref, grad_att = refs[16:]
    step = pl.program_id(0)

    @pl.when(step == 0)
    def _():
        gates_own = gates[...]
        gg = gate_grads[...]
        chosen = gates_own * (gg - jnp.sum(gates_own * gg, axis=-1, keepdims=True))
        grad = mm(chosen.astype(BF16), router[...])
        for part in parts:
            grad = grad + part[...].astype(F32)
        scaled = grad * gain[...]
        middle, inv = middle_ref[...], inv_ref[...]
        grad = (
            cot[...].astype(F32)
            + inv * scaled
            - middle * (inv * inv * inv) * jnp.mean(scaled * middle, axis=-1, keepdims=True)
        )
        grad_middle[...] = grad
        branch = grad.astype(BF16)
        branch_ref[...] = branch
        lora = (ADAPTER_SCALE * mm_nt(branch, proj_out[0])).astype(BF16)
        lora_ref[...] = lora
        attended = (mm_nt(branch, proj_w[...]) + mm(lora, proj_in[0])).astype(BF16)
        for i in range(PAIRS):
            grad_att[i] = attended[:, i * PAIR_QUERY : (i + 1) * PAIR_QUERY]

    keys, values = k_ref[...], v_ref[...]
    low = low_lanes(keys.shape)
    zero = jnp.zeros_like(keys)
    key_of = [jnp.where(low, keys, zero), jnp.where(low, zero, keys)]
    value_of = [jnp.where(low, values, zero), jnp.where(low, zero, values)]
    queries = placed_heads(lane_tiles(q_ref[...]))
    grads = placed_heads(lane_tiles(grad_att[step]))
    low_q = low_lanes(queries[0].shape)
    zero_q = jnp.zeros_like(queries[0])
    probs_all, scores_all, queries_all, grads_all = [], [], [], []
    for h in range(6):
        j = h // 3
        scores = mm_nt(key_of[j], queries[h]) + bias[...]
        shifted = jnp.exp(scores - jnp.max(scores, axis=0, keepdims=True))
        probs = shifted / jnp.sum(shifted, axis=0, keepdims=True)
        grad_probs = mm_nt(value_of[j], grads[h])
        grad_scores = probs * (grad_probs - jnp.sum(probs * grad_probs, axis=0, keepdims=True))
        probs_all.append(probs.astype(BF16))
        scores_all.append(grad_scores.astype(BF16))
        inside = low_q if j == 0 else jnp.logical_not(low_q)
        queries_all.append(jnp.where(inside, queries[h], zero_q))
        grads_all.append(jnp.where(inside, grads[h], zero_q))
    scores_six = jnp.concatenate(scores_all, axis=1)
    grad_key = mm(scores_six, jnp.concatenate(queries_all, axis=0))
    gk_ref[...] = turned(grad_key, cosine[...], -sine[...]).astype(BF16)
    gv_ref[...] = mm(
        jnp.concatenate(probs_all, axis=1), jnp.concatenate(grads_all, axis=0)
    ).astype(BF16)
    own = q_ref.shape[0]
    key_t = [key_of[0].astype(F32).T.astype(BF16), key_of[1].astype(F32).T.astype(BF16)]
    halves = [key_t[0][:HEAD_SIZE], key_t[1][HEAD_SIZE:]]
    cos, sin = cosine[-own:], -sine[-own:]
    for t in range(3):
        pair = [mm(halves[h // 3], scores_all[h]) for h in (2 * t, 2 * t + 1)]
        tile = SCALING * jnp.concatenate(pair, axis=0).T
        gq_ref[:, t * LANES : (t + 1) * LANES] = turned(tile, cos, sin).astype(BF16)


def middle_backward(
    scalars, parts, gate_grads, gates, router, middle, inv, gain, cot, proj_w, proj_in, proj_out,
    q, k, v, bias_t, cosine, sine,
):
    own = cot.shape[0]
    span = k.shape[0]
    last = span // own - 1
    experts_all = router.shape[0]
    gates_last = gates.shape[0] // own - 1
    return call(
        functools.partial(middle_kernel, len(parts)),
        scalars,
        PAIRS,
        [(a, (own, MODEL_WIDTH), lambda i, s, b=b: (b, 0)) for a, b in parts]
        + [
            whole(gate_grads),
            (gates, (own, experts_all), lambda i, s: (gates_last, 0)),
            whole(router),
            whole(middle),
            whole(inv),
            whole(gain),
            whole(cot),
            whole(proj_w),
            chosen_whole(proj_in),
            chosen_whole(proj_out),
            (q, (own, PAIR_QUERY), lambda i, s: (last, i)),
            (k, (span, LANES), lambda i, s: (0, i)),
            (v, (span, LANES), lambda i, s: (0, i)),
            whole(bias_t),
            whole(cosine),
            whole(sine),
        ],
        [
            whole_out((own, MODEL_WIDTH), F32),
            whole_out((own, MODEL_WIDTH), BF16),
            whole_out((own, ADAPTER_RANK), BF16),
            ((own, QUERY_FEATURES), BF16, (own, PAIR_QUERY), lambda i, s: (0, i)),
            ((span, KEY_FEATURES), BF16, (span, LANES), lambda i, s: (0, i)),
            ((span, KEY_FEATURES), BF16, (span, LANES), lambda i, s: (0, i)),
        ],
        [pltpu.VMEM((PAIRS, own, PAIR_QUERY), BF16)],
        10 * own * span * QUERY_FEATURES + 2 * own * MODEL_WIDTH * QUERY_FEATURES,
    )


def adapter_kernel(parts, scalars, *refs):
    gq, gk, gv, query_out, kv_out, normed, lora_in, attended, lora_out, branch, grad_lora = refs[:11]
    query_w, send_ref, first_ref = refs[11:]
    own = gq.shape[0]
    r = ADAPTER_RANK
    lora_q = (ADAPTER_SCALE * mm_nt(gq[...], query_out[0])).astype(BF16)
    lora_k = (ADAPTER_SCALE * mm_nt(gk[...], kv_out[0, 0])).astype(BF16)
    lora_v = (ADAPTER_SCALE * mm_nt(gv[...], kv_out[0, 1])).astype(BF16)
    low2 = lora_in[...] * ADAPTER_SCALE
    wide = [
        mm_tn(lora_q, normed[-own:]),
        mm_tn(lora_k, normed[...]),
        mm_tn(lora_v, normed[...]),
        mm_tn(low2[-own:, :r], gq[...]),
        mm_tn(grad_lora[...], attended[...]),
        mm_tn(lora_out[...] * ADAPTER_SCALE, branch[...]),
    ]
    narrow = [mm_tn(low2[:, r : 2 * r], gk[...]), mm_tn(low2[:, 2 * r :], gv[...])]
    w, v = MODEL_WIDTH // parts, KEY_FEATURES // parts
    for n, rows in enumerate(wide):
        rows = rows.astype(BF16)
        for p in range(parts):
            send_ref[p, n * r : (n + 1) * r, :w] = rows[:, p * w : (p + 1) * w]
    for n in range(len(wide)):
        for p in range(parts):
            if n < len(narrow):
                rows = narrow[n][:, p * v : (p + 1) * v].astype(BF16)
            else:
                rows = jnp.zeros((r, v), BF16)
            send_ref[p, n * r : (n + 1) * r, w:] = rows
    first_ref[...] = mm_nt(gq[...], query_w[...])


def adapters(scalars, parts, gq, gk, gv, query_out, kv_out, normed, lora_in, attended, lora_out,
             branch, grad_lora, query_w):
    own = gq.shape[0]
    return call(
        functools.partial(adapter_kernel, parts),
        scalars,
        1,
        [
            whole(gq),
            whole(gk),
            whole(gv),
            chosen_whole(query_out),
            chosen_whole(kv_out),
            whole(normed),
            whole(lora_in),
            whole(attended),
            whole(lora_out),
            whole(branch),
            whole(grad_lora),
            whole(query_w),
        ],
        [
            whole_out((parts, 6 * ADAPTER_RANK, (MODEL_WIDTH + KEY_FEATURES) // parts), BF16),
            whole_out((own, MODEL_WIDTH), F32),
        ],
        [],
        2 * own * MODEL_WIDTH * QUERY_FEATURES * 2,
    )


def input_kernel(blocks, scalars, *refs):
    gks, gvs, refs = refs[:blocks], refs[blocks : 2 * blocks], refs[2 * blocks :]
    gq, first, kv_w, query_out, kv_out, down, x_ref, gain, grad_middle, out_ref = refs
    grad_k, grad_v = [
        functools.reduce(lambda a, b: a + b, [g[...].astype(F32) for g in gs]).astype(BF16)
        for gs in (gks, gvs)
    ]
    lora = jnp.concatenate(
        [
            mm_nt(gq[...], query_out[0]),
            mm_nt(grad_k, kv_out[0, 0]),
            mm_nt(grad_v, kv_out[0, 1]),
        ],
        axis=1,
    )
    lora = (ADAPTER_SCALE * lora).astype(BF16)
    grad = (
        first[...]
        + mm_nt(grad_k, kv_w[:, :KEY_FEATURES])
        + mm_nt(grad_v, kv_w[:, KEY_FEATURES:])
        + mm(lora, down[0])
    )
    x = x_ref[...].astype(F32)
    inv = lax.rsqrt(jnp.mean(x * x, axis=-1, keepdims=True) + EPS)
    scaled = grad * gain[...]
    out_ref[...] = (
        grad_middle[...]
        + inv * scaled
        - x * (inv * inv * inv) * jnp.mean(scaled * x, axis=-1, keepdims=True)
    )


def input_backward(scalars, gks, gvs, gq, first, kv_w, query_out, kv_out, down, x, gain, grad_middle):
    own = x.shape[0]
    blocked = [(a, (own, KEY_FEATURES), lambda i, s, b=b: (b, 0)) for a, b in gks + gvs]
    return call(
        functools.partial(input_kernel, len(gks)),
        scalars,
        1,
        blocked
        + [
            whole(gq),
            whole(first),
            whole(kv_w),
            chosen_whole(query_out),
            chosen_whole(kv_out),
            chosen_whole(down),
            whole(x),
            whole(gain),
            whole(grad_middle),
        ],
        [whole_out((own, MODEL_WIDTH), F32)],
        [],
        4 * own * MODEL_WIDTH * KEY_FEATURES,
    )[0]


def by_adapter(received, selector):
    return jnp.einsum("as,srw->arw", selector, received.astype(F32), precision="highest")


def shards(
    layer_input_rows,
    routes,
    prefix,
    sequence_adapter_index,
    attention_norm_gain,
    expert_norm_gain,
    query_weight,
    key_value_weight,
    projection_weight,
    router_weight,
    gate_up_weight,
    down_weight,
    adapter_query_key_value_input,
    adapter_query_output,
    adapter_key_value_output,
    adapter_projection_input,
    adapter_projection_output,
    adapter_gate_up_input,
    adapter_gate_up_output,
    adapter_down_input,
    adapter_down_output,
    cotangent,
):
    ctx_size = lax.axis_size("ctx")
    dp_size = lax.axis_size("dp")
    rank = lax.axis_index("ctx")
    own = layer_input_rows.shape[1]
    span = own * ctx_size
    experts_here = gate_up_weight.shape[0]
    experts_all = experts_here * ctx_size
    half = ctx_size // 2
    scalars = jnp.stack([sequence_adapter_index[0], prefix[0], rank]).astype(jnp.int32)
    gain_attn = attention_norm_gain[None]
    gain_ffn = expert_norm_gain[None]

    order = (rank - 1 - jnp.arange(ctx_size, dtype=jnp.int32)) % ctx_size
    positions = (order[:, None] * own + jnp.arange(own, dtype=jnp.int32)[None, :]).reshape(-1)
    inputs = ring_gather(layer_input_rows[0], ctx_size)
    route_blocks = ring_gather(routes[0], ctx_size)
    cot_own, inputs[-2] = lax.optimization_barrier((cotangent[0], inputs[-2]))
    cots = ring_gather(cot_own, ctx_size)

    size = HEAD_SIZE // 2
    frequency = ROPE_BASE ** (-jnp.arange(size, dtype=F32) / size)
    angles = positions.astype(F32)[:, None] * frequency[None, :]
    cosine, sine = jnp.cos(angles), jnp.sin(angles)
    cosine = jnp.concatenate([cosine] * 4, axis=1)
    sine = jnp.concatenate([-sine, sine] * 2, axis=1)
    allowed = (positions[None, :] <= positions[:, None]) | (positions[None, :] < prefix[0])
    bias = jnp.where(allowed, 0.0, MASKED).astype(F32)
    bias_t = bias[-own:].T
    expert_ids = jnp.arange(experts_all, dtype=jnp.int32)
    routes_all = jnp.concatenate(route_blocks, axis=0)
    named = jnp.any(routes_all[:, :, None] == expert_ids[None, None, :], axis=1).astype(F32)

    qkv_in_t = adapter_query_key_value_input.transpose(0, 2, 1)
    proj_in_t = adapter_projection_input.transpose(0, 2, 1)
    router_t = router_weight.T
    q, k, v, normed, lora_in = qkv(
        scalars, inputs, gain_attn, qkv_in_t, query_weight, key_value_weight,
        adapter_query_output, adapter_key_value_output, cosine, sine,
    )
    tables = (
        gate_up_weight,
        down_weight,
        adapter_gate_up_input.transpose(0, 1, 3, 2),
        adapter_gate_up_output,
        adapter_down_input.transpose(0, 1, 3, 2),
        adapter_down_output,
    )

    def attend_half(part, with_own):
        return attend(
            scalars, part, with_own, inputs[part * half : (part + 1) * half], q, k, v, bias,
            projection_weight, proj_in_t, adapter_projection_output, gain_ffn, router_t, named,
        )

    normed_first, gates_first = attend_half(0, False)
    rows_first, gg_first, wide, narrow = experts(
        scalars, dp_size, cots[:half], normed_first, gates_first, tables, None
    )
    normed_last, gates_last, attended, lora_out, middle, inv = attend_half(1, True)
    rows_last, gg_last, send = experts(
        scalars, dp_size, cots[half:], normed_last, gates_last, tables, (wide, narrow)
    )

    def back(first, last, axis):
        got = []
        for j in range(ctx_size - 1):
            source, at = (first, j) if j < half else (last, j - half)
            block = lax.slice_in_dim(source, at * own, (at + 1) * own, axis=axis)
            got.append((lax.ppermute(block, "ctx", rotation(ctx_size, -1 - j)), 0))
        return got

    gg_blocks = [b[:experts_here] for b, _ in back(gg_first, gg_last, 1)]
    got = back(rows_first, rows_last, 0)
    got.append((rows_last, half - 1))
    gg_blocks.append(gg_last[:experts_here, -own:])
    gate_grads = jnp.concatenate(gg_blocks, axis=0)
    shift = (jnp.arange(experts_all, dtype=jnp.int32) - (rank + 1) * experts_here) % experts_all
    gate_grads = jnp.take(gate_grads, shift, axis=0).T
    expert_got = lax.all_to_all(send, "dp", 0, 0, tiled=True)

    grad_middle, branch, grad_lora, gq, gk, gv = middle_backward(
        scalars, got, gate_grads, gates_last, router_t, middle, inv, gain_ffn, cot_own,
        projection_weight, proj_in_t, adapter_projection_output, q, k, v, bias_t, cosine, sine,
    )

    def scatter(array):
        blocks = []
        for j in range(ctx_size - 1):
            block = array[j * own : (j + 1) * own]
            blocks.append((lax.ppermute(block, "ctx", rotation(ctx_size, -1 - j)), 0))
        return blocks + [(array, ctx_size - 1)]

    gks, gvs = scatter(gk), scatter(gv)
    attention_rows, first = adapters(
        scalars, dp_size, gq, gk, gv, adapter_query_output, adapter_key_value_output, normed,
        lora_in, attended, lora_out, branch, grad_lora, query_weight,
    )
    grad_inputs = input_backward(
        scalars, gks, gvs, gq, first, key_value_weight, adapter_query_output,
        adapter_key_value_output, qkv_in_t, layer_input_rows[0], gain_attn, grad_middle,
    )

    rows_count = 6 * ADAPTER_RANK // ctx_size
    pieces = attention_rows.reshape(dp_size, ctx_size, rows_count, -1)

    def piece(j):
        return lax.dynamic_index_in_dim(pieces, (rank + j) % ctx_size, 1, keepdims=False)

    choices = expert_got[:, experts_here * 3 * ADAPTER_RANK, 0].astype(F32)
    selector = (jnp.arange(ADAPTER_CHOICES, dtype=F32)[:, None] == choices[None, :]).astype(F32)
    share = piece(0).astype(F32)
    for j in range(1, ctx_size):
        share = share + lax.ppermute(piece(j), "ctx", rotation(ctx_size, j)).astype(F32)
    share = lax.all_to_all(share.astype(BF16), "dp", 0, 0, tiled=True)
    share = by_adapter(share, selector).astype(BF16)
    attention_sum = [share]
    for j in range(1, ctx_size):
        attention_sum.append(lax.ppermute(share, "ctx", rotation(ctx_size, j)))
    attention_sum = jnp.stack(attention_sum, axis=1)
    back_order = (rank - jnp.arange(ctx_size, dtype=jnp.int32)) % ctx_size
    attention_sum = jnp.take(attention_sum, back_order, axis=1)
    attention_sum = attention_sum.reshape(ADAPTER_CHOICES, 6 * ADAPTER_RANK, -1).astype(F32)
    expert_sum = by_adapter(expert_got[:, : experts_here * 3 * ADAPTER_RANK], selector)

    wide_width = MODEL_WIDTH // dp_size
    r = ADAPTER_RANK
    attn_wide, attn_narrow = attention_sum[..., :wide_width], attention_sum[..., wide_width:]
    by_expert = expert_sum.reshape(ADAPTER_CHOICES, experts_here, 3 * r, -1)
    exp_wide, exp_narrow = by_expert[..., :wide_width], by_expert[..., wide_width:]
    return (
        grad_inputs[None],
        attn_wide[:, : 3 * r].transpose(0, 2, 1),
        attn_wide[:, 3 * r : 4 * r],
        attn_narrow[:, : 2 * r].reshape(ADAPTER_CHOICES, 2, r, -1),
        attn_wide[:, 4 * r : 5 * r].transpose(0, 2, 1),
        attn_wide[:, 5 * r :],
        exp_wide[:, :, : 2 * r].transpose(0, 1, 3, 2),
        exp_narrow[:, :, : 2 * r].reshape(ADAPTER_CHOICES, experts_here, 2, r, -1),
        exp_narrow[:, :, 2 * r :].transpose(0, 1, 3, 2),
        exp_wide[:, :, 2 * r :],
    )


def solution(mesh):
    placed = (
        P("dp", "ctx", None),
        P("dp", "ctx", None),
        P("dp"),
        P("dp"),
        P(),
        P(),
        P(),
        P(),
        P(),
        P(),
        P("ctx", None, None),
        P("ctx", None, None),
        P(),
        P(),
        P(),
        P(),
        P(),
        P(None, "ctx", None, None),
        P(None, "ctx", None, None, None),
        P(None, "ctx", None, None),
        P(None, "ctx", None, None),
        P("dp", "ctx", None),
    )
    return jax.shard_map(
        shards,
        mesh=mesh,
        in_specs=placed,
        out_specs=(
            P("dp", "ctx", None),
            P(None, "dp", None),
            P(None, None, "dp"),
            P(None, None, None, "dp"),
            P(None, "dp", None),
            P(None, None, "dp"),
            P(None, "ctx", "dp", None),
            P(None, "ctx", None, None, "dp"),
            P(None, "ctx", "dp", None),
            P(None, "ctx", None, "dp"),
        ),
        check_vma=False,
    )
```

```python
import functools

import jax
import jax.numpy as jnp
from jax import lax
from jax.experimental import pallas as pl
from jax.experimental.pallas import tpu as pltpu
from jax.sharding import PartitionSpec as P

MODEL_WIDTH = 1536
QUERY_HEADS = 24
KEY_HEADS = 8
HEAD_SIZE = 64
EXPERT_HIDDEN = 512
TOPK = 8
ADAPTER_RANK = 16
ADAPTER_CHOICES = 8
QUERY_FEATURES = 1536
KEY_FEATURES = 512
LANES = 128
PAIRS = KEY_HEADS // 2
PAIR_QUERY = QUERY_FEATURES // PAIRS
GATE_LANES = 8
SENT = MODEL_WIDTH + LANES
COLUMNS = 512

EPS = 1e-05
ADAPTER_SCALE = 2.0
ROPE_BASE = 10000.0
MASKED = -1e30
SCALING = HEAD_SIZE ** (-0.5)
F32 = jnp.float32
BF16 = jnp.bfloat16
MIB = 1024 * 1024


def mm(left, right):
    return jnp.dot(left, right, preferred_element_type=F32)


def mm_nt(left, right):
    return lax.dot_general(left, right, (((1,), (1,)), ((), ())), preferred_element_type=F32)


def mm_tn(left, right):
    return lax.dot_general(left, right, (((0,), (0,)), ((), ())), preferred_element_type=F32)


def rotation(size, by):
    return [(i, (i + by) % size) for i in range(size)]


def after(value, *others):
    return lax.optimization_barrier((value, *others))[0]


def rotations(block, size):
    return [lax.ppermute(block, "ctx", rotation(size, j)) for j in range(1, size)] + [block]


def send_back(blocks, size, first):
    return [
        lax.ppermute(b, "ctx", rotation(size, -1 - j)) for j, b in enumerate(blocks, first)
    ]


def low_lanes(shape):
    return lax.broadcasted_iota(jnp.int32, shape, 1) % LANES < HEAD_SIZE


def swapped(tile):
    return jnp.concatenate([tile[:, HEAD_SIZE:], tile[:, :HEAD_SIZE]], axis=1)


def turned(tile, cosine, sine):
    half = HEAD_SIZE // 2
    lane = lax.broadcasted_iota(jnp.int32, tile.shape, 1)
    other = jnp.where(
        lane % HEAD_SIZE < half, pltpu.roll(tile, LANES - half, 1), pltpu.roll(tile, half, 1)
    )
    return tile * cosine + other * sine


def placed_heads(tiles):
    return [
        tiles[0],
        swapped(tiles[0]),
        tiles[1],
        tiles[1],
        swapped(tiles[2]),
        tiles[2],
    ]


def lane_tiles(block):
    return [block[:, t * LANES : (t + 1) * LANES] for t in range(block.shape[1] // LANES)]


def call(kernel, scalars, grid, ins, outs, scratch, flops, vmem=62):
    return list(pl.pallas_call(
        kernel,
        grid_spec=pltpu.PrefetchScalarGridSpec(
            num_scalar_prefetch=1,
            grid=(grid,),
            in_specs=[pl.BlockSpec(b, m) for _, b, m in ins],
            out_specs=[pl.BlockSpec(b, m) for _, _, b, m in outs],
            scratch_shapes=scratch,
        ),
        out_shape=[jax.ShapeDtypeStruct(s, d) for s, d, _, _ in outs],
        compiler_params=pltpu.CompilerParams(
            vmem_limit_bytes=vmem * MIB, dimension_semantics=("arbitrary",)
        ),
        cost_estimate=pl.CostEstimate(
            flops=0, bytes_accessed=0, transcendentals=0
        ),
    )(scalars, *[a for a, _, _ in ins]))


def whole(array):
    return (array, array.shape, lambda i, s, n=array.ndim: (0,) * n)


def whole_out(shape, dtype):
    return (shape, dtype, shape, lambda i, s, n=len(shape): (0,) * n)


def chosen_whole(table):
    rest = table.shape[1:]
    return (table, (1,) + rest, lambda i, s, n=len(rest): (s[0],) + (0,) * n)


def qkv_kernel(blocks, scalars, *refs):
    xs, refs = refs[:blocks], refs[blocks:]
    gain, down, query_w, kv_w, query_out, kv_out, cosine, sine = refs[:8]
    q_ref, k_ref, v_ref, normed_ref, lora_ref = refs[8:]
    step = pl.program_id(0)
    q_steps = QUERY_FEATURES // COLUMNS

    @pl.when(step == 0)
    def _():
        rows = xs[0].shape[0]
        for b, x_ref in enumerate(xs):
            x = x_ref[...].astype(F32)
            inv = lax.rsqrt(jnp.mean(x * x, axis=-1, keepdims=True) + EPS)
            normed_ref[b * rows : (b + 1) * rows] = (x * inv * gain[...]).astype(BF16)
        lora_ref[...] = mm_nt(normed_ref[...], down[0]).astype(BF16)

    def rope_to(out_ref, pre, scale):
        cos, sin = cosine[...] * scale, sine[...] * scale
        for t, tile in enumerate(lane_tiles(pre)):
            out_ref[:, t * LANES : (t + 1) * LANES] = turned(tile, cos, sin).astype(BF16)

    r = ADAPTER_RANK

    @pl.when(step < q_steps)
    def _():
        pre = mm(normed_ref[...], query_w[...])
        pre = pre + mm(lora_ref[:, :r] * ADAPTER_SCALE, query_out[0])
        rope_to(q_ref, pre, SCALING)

    @pl.when(step == q_steps)
    def _():
        pre = mm(normed_ref[...], kv_w[...])
        pre = pre + mm(lora_ref[:, r : 2 * r] * ADAPTER_SCALE, kv_out[0, 0])
        rope_to(k_ref, pre, 1.0)

    @pl.when(step == q_steps + 1)
    def _():
        pre = mm(normed_ref[...], kv_w[...])
        v_ref[...] = (pre + mm(lora_ref[:, 2 * r :] * ADAPTER_SCALE, kv_out[0, 1])).astype(BF16)


def qkv(scalars, xs, gain, down, query_w, kv_w, query_out, kv_out, cosine, sine):
    rows = sum(x.shape[0] for x in xs)
    q_steps = QUERY_FEATURES // COLUMNS
    last = q_steps - 1
    return call(
        functools.partial(qkv_kernel, len(xs)),
        scalars,
        q_steps + 2,
        [whole(x) for x in xs]
        + [
            whole(gain),
            chosen_whole(down),
            (query_w, (MODEL_WIDTH, COLUMNS), lambda i, s: (0, jnp.minimum(i, last))),
            (kv_w, (MODEL_WIDTH, COLUMNS), lambda i, s: (0, jnp.maximum(i - q_steps, 0))),
            (query_out, (1, ADAPTER_RANK, COLUMNS), lambda i, s: (s[0], 0, jnp.minimum(i, last))),
            chosen_whole(kv_out),
            whole(cosine),
            whole(sine),
        ],
        [
            (
                (rows, QUERY_FEATURES),
                BF16,
                (rows, COLUMNS),
                lambda i, s: (0, jnp.minimum(i, last)),
            ),
            whole_out((rows, KEY_FEATURES), BF16),
            whole_out((rows, KEY_FEATURES), BF16),
            whole_out((rows, MODEL_WIDTH), BF16),
            whole_out((rows, 3 * ADAPTER_RANK), BF16),
        ],
        [],
        2 * rows * MODEL_WIDTH * (QUERY_FEATURES + 2 * KEY_FEATURES),
    )


def attend_kernel(blocks, with_own, scalars, *refs):
    xs, refs = refs[:blocks], refs[blocks:]
    q_ref, k_ref, v_ref, bias, proj_w, proj_in, proj_out, gain, router, named = refs[:10]
    outs = refs[10:]
    if with_own:
        normed_ref, gates_ref, att_ref, lora_ref, middle_ref, inv_ref, total, rank_total = outs
    else:
        normed_ref, gates_ref, total, rank_total = outs
    step = pl.program_id(0)
    own = xs[0].shape[0]

    keys, values = k_ref[...], v_ref[...]
    low = low_lanes(keys.shape)
    zero, one = jnp.zeros_like(keys), jnp.ones_like(values)
    key_of = [jnp.where(low, keys, zero), jnp.where(low, zero, keys)]
    value_of = [jnp.where(low, values, one), jnp.where(low, one, values)]
    heads = []
    for h, query in enumerate(placed_heads(lane_tiles(q_ref[...]))):
        scores = mm_nt(query, key_of[h // 3]) + bias[...]
        shifted = jnp.exp(scores - jnp.max(scores, axis=-1, keepdims=True)).astype(BF16)
        sums = mm(shifted, value_of[h // 3])
        heads.append(sums / pltpu.roll(sums, HEAD_SIZE, 1))
    low_q = low_lanes(heads[0].shape)
    attended = jnp.concatenate(
        [
            jnp.where(low_q, heads[0], pltpu.roll(heads[1], HEAD_SIZE, 1)),
            jnp.where(low_q, heads[2], heads[3]),
            jnp.where(low_q, pltpu.roll(heads[4], HEAD_SIZE, 1), heads[5]),
        ],
        axis=1,
    ).astype(BF16)
    if with_own:
        att_ref[...] = attended[-own:]
    part = mm(attended, proj_w[...])
    rank_part = mm_nt(attended, proj_in[0])

    @pl.when(step == 0)
    def _():
        total[...] = part
        rank_total[...] = rank_part

    @pl.when(step > 0)
    def _():
        total[...] += part
        rank_total[...] += rank_part

    @pl.when(step == PAIRS - 1)
    def _():
        lora_out = rank_total[...].astype(BF16)
        branch = total[...] + mm(lora_out * ADAPTER_SCALE, proj_out[0])
        for b, x_ref in enumerate(xs):
            middle = x_ref[...].astype(F32) + branch[b * own : (b + 1) * own]
            inv = lax.rsqrt(jnp.mean(middle * middle, axis=-1, keepdims=True) + EPS)
            normed_ref[b * own : (b + 1) * own] = (middle * inv * gain[...]).astype(BF16)
            if with_own and b == blocks - 1:
                middle_ref[...] = middle
                inv_ref[...] = inv
                lora_ref[...] = lora_out[b * own : (b + 1) * own]
        logits = mm_nt(normed_ref[...], router[...])
        mask = named[...] > 0.0
        chosen = jnp.where(mask, logits, MASKED)
        shifted = jnp.exp(chosen - jnp.max(chosen, axis=-1, keepdims=True))
        shifted = jnp.where(mask, shifted, 0.0)
        gates_ref[...] = shifted / jnp.sum(shifted, axis=-1, keepdims=True)


def attend(scalars, part, with_own, xs, q, k, v, bias, proj_w, proj_in, proj_out, gain, router, named):
    own = xs[0].shape[0]
    rows = own * len(xs)
    span = k.shape[0]
    outs = [
        whole_out((rows, MODEL_WIDTH), BF16),
        whole_out((rows, LANES), F32),
    ]
    if with_own:
        outs += [
            ((own, QUERY_FEATURES), BF16, (own, PAIR_QUERY), lambda i, s: (0, i)),
            whole_out((own, ADAPTER_RANK), BF16),
            whole_out((own, MODEL_WIDTH), F32),
            whole_out((own, 1), F32),
        ]
    return call(
        functools.partial(attend_kernel, len(xs), with_own),
        scalars,
        PAIRS,
        [whole(x) for x in xs]
        + [
            (q, (rows, PAIR_QUERY), lambda i, s: (part, i)),
            (k, (span, LANES), lambda i, s: (0, i)),
            (v, (span, LANES), lambda i, s: (0, i)),
            (bias, (rows, span), lambda i, s: (part, 0)),
            (proj_w, (PAIR_QUERY, MODEL_WIDTH), lambda i, s: (i, 0)),
            (proj_in, (1, ADAPTER_RANK, PAIR_QUERY), lambda i, s: (s[0], 0, i)),
            chosen_whole(proj_out),
            whole(gain),
            whole(router),
            (named, (rows, LANES), lambda i, s: (part, 0)),
        ],
        outs,
        [pltpu.VMEM((rows, MODEL_WIDTH), F32), pltpu.VMEM((rows, ADAPTER_RANK), F32)],
        4 * rows * span * QUERY_FEATURES + 2 * rows * MODEL_WIDTH * QUERY_FEATURES,
    )


def expert_kernel(blocks, parts, first, scalars, *refs):
    cots, refs = refs[:blocks], refs[blocks:]
    x_ref, gates, up_w, down_w, up_in, up_out, down_in, down_out = refs[:8]
    refs = refs[8:]
    if not first:
        (wide_old, narrow_old), refs = refs[:2], refs[2:]
    rows_refs, refs = refs[:blocks], refs[blocks:]
    if first:
        (wide_ref, narrow_ref), refs = refs[:2], refs[2:]
    else:
        send_ref, refs = refs[0], refs[1:]
    cot_all, total, gg_all, rank_in_all, cot_mid_all, grad_rank_all, gated_all = refs
    step = pl.program_id(0)
    here = up_in.shape[1]
    own = cots[0].shape[0]
    r = ADAPTER_RANK
    up_in_rows = up_in[0].reshape(here * 2 * r, MODEL_WIDTH)
    x = x_ref[...]

    @pl.when(step == 0)
    def _():
        for b, cot in enumerate(cots):
            cot_all[b * own : (b + 1) * own] = cot[...]
        gg_all[...] = jnp.zeros_like(gg_all)
        rank_in = mm_nt(x, up_in_rows).astype(BF16) * ADAPTER_SCALE
        down_out_rows = down_out[0].reshape(here * r, MODEL_WIDTH)
        cot_mid = ADAPTER_SCALE * mm_nt(cot_all[...], down_out_rows)
        for e in range(here):
            rank_in_all[e] = rank_in[:, e * 2 * r : (e + 1) * 2 * r]
            cot_mid_all[e] = cot_mid[:, e * r : (e + 1) * r]

    cot = cot_all[...]
    lane = lax.broadcasted_iota(jnp.int32, gates.shape, 1)
    gate_of = jnp.sum(
        jnp.where(lane == scalars[2] * here + step, gates[...], 0.0), axis=1, keepdims=True
    )
    rank_in2 = rank_in_all[step]
    none = jnp.zeros((r, EXPERT_HIDDEN), BF16)
    out_map = jnp.concatenate(
        [
            jnp.concatenate([up_out[0, 0, 0], none], axis=1),
            jnp.concatenate([none, up_out[0, 0, 1]], axis=1),
        ],
        axis=0,
    )
    pre = mm(x, up_w[0]) + mm(rank_in2, out_map)
    gate_pre, up_pre = pre[:, :EXPERT_HIDDEN], pre[:, EXPERT_HIDDEN:]
    cot_hidden = mm_nt(cot, down_w[0])
    sig = 0.5 * jnp.tanh(0.5 * gate_pre) + 0.5
    silu = gate_pre * sig
    hidden_wide = silu * up_pre
    hidden = hidden_wide.astype(BF16)
    rank_mid = mm_nt(hidden, down_in[0, 0]).astype(BF16).astype(F32)
    cot_mid = cot_mid_all[step]
    gate_grad = jnp.sum(hidden.astype(F32) * cot_hidden, axis=1, keepdims=True) + jnp.sum(
        rank_mid * cot_mid, axis=1, keepdims=True
    )
    gg_lane = lax.broadcasted_iota(jnp.int32, gg_all.shape, 1)
    gg_all[...] += jnp.where(gg_lane == step, gate_grad, 0.0)
    grad_rank_mid = (gate_of * cot_mid).astype(BF16)
    grad_hidden = gate_of * cot_hidden + mm(grad_rank_mid, down_in[0, 0])
    grad_gate = (grad_hidden * up_pre * (sig + silu * (1.0 - sig))).astype(BF16)
    grad_up = (grad_hidden * silu).astype(BF16)
    grad_both = jnp.concatenate([grad_gate, grad_up], axis=1)
    grad_rank_all[step] = (ADAPTER_SCALE * mm_nt(grad_both, out_map)).astype(BF16)
    gated_all[step] = (ADAPTER_SCALE * gate_of * rank_mid).astype(BF16)
    part = mm_nt(grad_both, up_w[0])

    @pl.when(step == 0)
    def _():
        total[...] = part

    @pl.when(step > 0)
    def _():
        total[...] += part

    both = mm_tn(
        jnp.concatenate([rank_in2, grad_rank_mid], axis=1),
        jnp.concatenate([grad_both, hidden], axis=1),
    )
    narrow = jnp.concatenate(
        [
            both[i * r : (i + 1) * r, i * EXPERT_HIDDEN : (i + 1) * EXPERT_HIDDEN]
            for i in range(3)
        ],
        axis=0,
    )
    w, v = MODEL_WIDTH // parts, EXPERT_HIDDEN // parts
    if first:
        narrow_ref[0] = narrow
    else:
        narrow = (narrow + narrow_old[0]).astype(BF16)
        at = pl.ds(pl.multiple_of(step * (3 * r), 16), 3 * r)
        for p in range(parts):
            send_ref[p, at, w:] = narrow[:, p * v : (p + 1) * v]

    @pl.when(step == here - 1)
    def _():
        grad_rank = jnp.concatenate([grad_rank_all[e] for e in range(here)], axis=1)
        gated = jnp.concatenate([gated_all[e] for e in range(here)], axis=1)
        rows = total[...] + mm(grad_rank, up_in_rows)
        high = gg_all[...].astype(BF16).astype(F32)
        both = high + pltpu.roll(gg_all[...] - high, GATE_LANES, 1)
        for b, rows_ref in enumerate(rows_refs):
            at = slice(b * own, (b + 1) * own)
            rows_ref[:, :MODEL_WIDTH] = rows[at].astype(BF16)
            rows_ref[:, MODEL_WIDTH:] = both[at].astype(BF16)
        wide = jnp.concatenate([mm_tn(grad_rank, x), mm_tn(gated, cot)], axis=0)
        if first:
            wide_ref[...] = wide
        else:
            wide = (wide + wide_old[...]).astype(BF16)
            rows = here * 3 * r
            chosen = jnp.full((16, w + v), scalars[0], jnp.int32).astype(F32).astype(BF16)
            for p in range(parts):
                send_ref[p, :rows, :w] = wide[:, p * w : (p + 1) * w]
                send_ref[p, rows:] = chosen


def experts(scalars, parts, cots, x, gates, tables, before):
    up_w, down_w, up_in, up_out, down_in, down_out = tables
    own = cots[0].shape[0]
    rows = own * len(cots)
    here = up_w.shape[0]
    r = ADAPTER_RANK
    per_expert = lambda i, s: (i, 0, 0)
    ins = [whole(c) for c in cots] + [
        whole(x),
        whole(gates),
        (up_w, (1,) + up_w.shape[1:], per_expert),
        (down_w, (1,) + down_w.shape[1:], per_expert),
        chosen_whole(up_in),
        (up_out, (1, 1) + up_out.shape[2:], lambda i, s: (s[0], i, 0, 0, 0)),
        (down_in, (1, 1) + down_in.shape[2:], lambda i, s: (s[0], i, 0, 0)),
        chosen_whole(down_out),
    ]
    outs = [whole_out((own, SENT), BF16) for _ in cots]
    if before is None:
        outs.append(whole_out((here * 3 * r, MODEL_WIDTH), F32))
        outs.append(((here, 3 * r, EXPERT_HIDDEN), F32, (1, 3 * r, EXPERT_HIDDEN), per_expert))
    else:
        wide, narrow = before
        ins += [whole(wide), (narrow, (1,) + narrow.shape[1:], per_expert)]
        width = (MODEL_WIDTH + EXPERT_HIDDEN) // parts
        outs.append(whole_out((parts, here * 3 * r + 16, width), BF16))
    return call(
        functools.partial(expert_kernel, len(cots), parts, before is None),
        scalars,
        here,
        ins,
        outs,
        [
            pltpu.VMEM((rows, MODEL_WIDTH), BF16),
            pltpu.VMEM((rows, MODEL_WIDTH), F32),
            pltpu.VMEM((rows, LANES), F32),
            pltpu.VMEM((here, rows, 2 * r), BF16),
            pltpu.VMEM((here, rows, r), F32),
            pltpu.VMEM((here, rows, 2 * r), BF16),
            pltpu.VMEM((here, rows, r), BF16),
        ],
        here * 2 * rows * MODEL_WIDTH * EXPERT_HIDDEN * 5,
    )


def middle_kernel(blocks, here, scalars, *refs):
    parts, refs = refs[:blocks], refs[blocks:]
    gates, router, middle_ref, inv_ref, gain, cot = refs[:6]
    proj_w, proj_in, proj_out, q_ref, k_ref, v_ref, bias, cosine, sine = refs[6:15]
    grad_middle, branch_ref, lora_ref, gq_ref = refs[15:19]
    gkv_refs, grad_att = refs[19:-1], refs[-1]
    step = pl.program_id(0)
    own = q_ref.shape[0]

    @pl.when(step == 0)
    def _():
        gates_own = gates[...]
        lane = lax.broadcasted_iota(jnp.int32, gates_own.shape, 1)
        gg = jnp.zeros_like(gates_own)
        for j, part in enumerate(parts):
            both = part[:, MODEL_WIDTH:].astype(F32)
            both = both + pltpu.roll(both, LANES - GATE_LANES, 1)
            both = jnp.where(lane < here, both, 0.0)
            gg = gg + pltpu.roll(both, lax.rem(scalars[2] + 1 + j, blocks) * here, 1)
        chosen = gates_own * (gg - jnp.sum(gates_own * gg, axis=-1, keepdims=True))
        grad = mm(chosen.astype(BF16), router[...])
        for part in parts:
            grad = grad + part[:, :MODEL_WIDTH].astype(F32)
        scaled = grad * gain[...]
        middle, inv = middle_ref[...], inv_ref[...]
        grad = (
            cot[...].astype(F32)
            + inv * scaled
            - middle * (inv * inv * inv) * jnp.mean(scaled * middle, axis=-1, keepdims=True)
        )
        grad_middle[...] = grad
        branch = grad.astype(BF16)
        branch_ref[...] = branch
        lora = (ADAPTER_SCALE * mm_nt(branch, proj_out[0])).astype(BF16)
        lora_ref[...] = lora
        attended = (mm_nt(branch, proj_w[...]) + mm(lora, proj_in[0])).astype(BF16)
        for i in range(PAIRS):
            grad_att[i] = attended[:, i * PAIR_QUERY : (i + 1) * PAIR_QUERY]

    keys, values = k_ref[...], v_ref[...]
    low = low_lanes(keys.shape)
    zero = jnp.zeros_like(keys)
    key_of = [jnp.where(low, keys, zero), jnp.where(low, zero, keys)]
    value_of = [jnp.where(low, values, zero), jnp.where(low, zero, values)]
    queries = placed_heads(lane_tiles(q_ref[...]))
    grads = placed_heads(lane_tiles(grad_att[step]))
    low_q = low_lanes(queries[0].shape)
    zero_q = jnp.zeros_like(queries[0])
    probs_all, scores_all, queries_all, grads_all = [], [], [], []
    for h in range(6):
        j = h // 3
        scores = mm_nt(key_of[j], queries[h]) + bias[...]
        shifted = jnp.exp(scores - jnp.max(scores, axis=0, keepdims=True))
        probs = shifted / jnp.sum(shifted, axis=0, keepdims=True)
        grad_probs = mm_nt(value_of[j], grads[h])
        grad_scores = probs * (grad_probs - jnp.sum(probs * grad_probs, axis=0, keepdims=True))
        probs_all.append(probs.astype(BF16))
        scores_all.append(grad_scores.astype(BF16))
        inside = low_q if j == 0 else jnp.logical_not(low_q)
        queries_all.append(jnp.where(inside, queries[h], zero_q))
        grads_all.append(jnp.where(inside, grads[h], zero_q))
    scores_six = jnp.concatenate(scores_all, axis=1)
    grad_key = mm(scores_six, jnp.concatenate(queries_all, axis=0))
    grad_key = turned(grad_key, cosine[...], -sine[...]).astype(BF16)
    grad_value = mm(
        jnp.concatenate(probs_all, axis=1), jnp.concatenate(grads_all, axis=0)
    ).astype(BF16)
    for b, gkv_ref in enumerate(gkv_refs):
        gkv_ref[:, :LANES] = grad_key[b * own : (b + 1) * own]
        gkv_ref[:, LANES:] = grad_value[b * own : (b + 1) * own]
    key_t = [key_of[0].astype(F32).T.astype(BF16), key_of[1].astype(F32).T.astype(BF16)]
    halves = [key_t[0][:HEAD_SIZE], key_t[1][HEAD_SIZE:]]
    cos, sin = cosine[-own:], -sine[-own:]
    for t in range(3):
        pair = [mm(halves[h // 3], scores_all[h]) for h in (2 * t, 2 * t + 1)]
        tile = SCALING * jnp.concatenate(pair, axis=0).T
        gq_ref[:, t * LANES : (t + 1) * LANES] = turned(tile, cos, sin).astype(BF16)


def middle_backward(
    scalars, parts, here, gates, router, middle, inv, gain, cot, proj_w, proj_in, proj_out,
    q, k, v, bias_t, cosine, sine,
):
    own = cot.shape[0]
    span = k.shape[0]
    last = span // own - 1
    gates_last = gates.shape[0] // own - 1
    return call(
        functools.partial(middle_kernel, len(parts), here),
        scalars,
        PAIRS,
        [whole(part) for part in parts]
        + [
            (gates, (own, LANES), lambda i, s: (gates_last, 0)),
            whole(router),
            whole(middle),
            whole(inv),
            whole(gain),
            whole(cot),
            whole(proj_w),
            chosen_whole(proj_in),
            chosen_whole(proj_out),
            (q, (own, PAIR_QUERY), lambda i, s: (last, i)),
            (k, (span, LANES), lambda i, s: (0, i)),
            (v, (span, LANES), lambda i, s: (0, i)),
            whole(bias_t),
            whole(cosine),
            whole(sine),
        ],
        [
            whole_out((own, MODEL_WIDTH), F32),
            whole_out((own, MODEL_WIDTH), BF16),
            whole_out((own, ADAPTER_RANK), BF16),
            ((own, QUERY_FEATURES), BF16, (own, PAIR_QUERY), lambda i, s: (0, i)),
        ]
        + [
            ((own, 2 * KEY_FEATURES), BF16, (own, 2 * LANES), lambda i, s: (0, i))
            for _ in range(span // own)
        ],
        [pltpu.VMEM((PAIRS, own, PAIR_QUERY), BF16)],
        10 * own * span * QUERY_FEATURES + 2 * own * MODEL_WIDTH * QUERY_FEATURES,
    )


def key_and_value(columns):
    return jnp.concatenate(columns[0::2], axis=1), jnp.concatenate(columns[1::2], axis=1)


def adapter_kernel(parts, blocks, scalars, *refs):
    gkvs, refs = refs[:blocks], refs[blocks:]
    gq, query_out, kv_out, normed, lora_in, attended, lora_out, branch, grad_lora = refs[:9]
    send_refs, table = refs[9:-1], refs[-1]
    own = gq.shape[0]
    r = ADAPTER_RANK
    gkv = jnp.concatenate([g[...] for g in gkvs], axis=0)
    gk, gv = key_and_value(lane_tiles(gkv))
    lora_q = (ADAPTER_SCALE * mm_nt(gq[...], query_out[0])).astype(BF16)
    lora_k = (ADAPTER_SCALE * mm_nt(gk, kv_out[0, 0])).astype(BF16)
    lora_v = (ADAPTER_SCALE * mm_nt(gv, kv_out[0, 1])).astype(BF16)
    low2 = lora_in[...] * ADAPTER_SCALE
    wide = [
        mm_tn(lora_q, normed[-own:]),
        mm_tn(lora_k, normed[...]),
        mm_tn(lora_v, normed[...]),
        mm_tn(low2[-own:, :r], gq[...]),
        mm_tn(grad_lora[...], attended[...]),
        mm_tn(lora_out[...] * ADAPTER_SCALE, branch[...]),
    ]
    narrow = [mm_tn(low2[:, r : 2 * r], gk), mm_tn(low2[:, 2 * r :], gv)]
    wide, narrow = jnp.concatenate(wide, axis=0), jnp.concatenate(narrow, axis=0)
    w, v = MODEL_WIDTH // parts, KEY_FEATURES // parts
    count = 6 * r // blocks
    for b in range(blocks):
        at, below = b * count, min((b + 1) * count, 2 * r)
        for p in range(parts):
            table[b, p, :, :w] = wide[at : at + count, p * w : (p + 1) * w]
            if below < at + count:
                table[b, p, :, w:] = jnp.zeros((count, v), F32)
            if at < below:
                table[b, p, : below - at, w:] = narrow[at:below, p * v : (p + 1) * v]
    for j, send in enumerate(send_refs):
        send[...] = table[lax.rem(scalars[2] + 2 * blocks - 1 - j, blocks)].astype(BF16)


def adapters(scalars, parts, gkvs, gq, query_out, kv_out, normed, lora_in, attended, lora_out,
             branch, grad_lora):
    own = gq.shape[0]
    blocks = len(gkvs)
    share = (parts, 6 * ADAPTER_RANK // blocks, (MODEL_WIDTH + KEY_FEATURES) // parts)
    return call(
        functools.partial(adapter_kernel, parts, blocks),
        scalars,
        1,
        [whole(g) for g in gkvs]
        + [
            whole(gq),
            chosen_whole(query_out),
            chosen_whole(kv_out),
            whole(normed),
            whole(lora_in),
            whole(attended),
            whole(lora_out),
            whole(branch),
            whole(grad_lora),
        ],
        [whole_out(share, BF16) for _ in range(blocks)],
        [pltpu.VMEM((blocks,) + share, F32)],
        2 * own * MODEL_WIDTH * QUERY_FEATURES,
    )


def summed(received, choices, adapter, senders):
    total = None
    for n in range(senders):
        rows = jnp.where(choices[n, :1, :1].astype(F32) == adapter, received(n), 0.0)
        total = rows if total is None else total + rows
    return total


def expert_sum_kernel(wide, scalars, got, choices, up_in, up_out, down_in, down_out):
    adapter = pl.program_id(0).astype(F32)
    total = summed(lambda n: got[n].astype(F32), choices, adapter, got.shape[0])
    r = ADAPTER_RANK
    here = up_in.shape[1]
    for e in range(here):
        up_in[0, e] = total[e * 2 * r : (e + 1) * 2 * r, :wide]
        down_out[0, e] = total[(2 * here + e) * r : (2 * here + e + 1) * r, :wide]
        rows = total[e * 3 * r : (e + 1) * 3 * r]
        up_out[0, e, 0] = rows[:r, wide:]
        up_out[0, e, 1] = rows[r : 2 * r, wide:]
        down_in[0, e] = rows[2 * r :, wide:]


def expert_sum(scalars, got, here):
    parts, _, width = got.shape
    r = ADAPTER_RANK
    rows = here * 3 * r
    wide, narrow = MODEL_WIDTH // parts, EXPERT_HIDDEN // parts

    def out(*shape):
        return ((ADAPTER_CHOICES,) + shape, F32, (1,) + shape, lambda i, s: (i,) + (0,) * len(shape))

    return call(
        functools.partial(expert_sum_kernel, wide),
        scalars,
        ADAPTER_CHOICES,
        [
            (got, (parts, rows, width), lambda i, s: (0, 0, 0)),
            (got, (parts, 16, width), lambda i, s: (0, rows // 16, 0)),
        ],
        [
            out(here, 2 * r, wide),
            out(here, 2, r, narrow),
            out(here, r, narrow),
            out(here, r, wide),
        ],
        [],
        2 * ADAPTER_CHOICES * parts * rows * width,
    )


def share_kernel(parts, scalars, got, choices, out_ref):
    each = [got[n].astype(F32) for n in range(parts)]
    for a in range(ADAPTER_CHOICES):
        out_ref[a] = summed(lambda n: each[n], choices, float(a), parts).astype(BF16)


def share_sum(scalars, got, expert_got, rows):
    parts = expert_got.shape[0]
    width = got.shape[2]
    return call(
        functools.partial(share_kernel, parts),
        scalars,
        1,
        [whole(got), (expert_got, (parts, 16, width), lambda i, s: (0, rows // 16, 0))],
        [whole_out((ADAPTER_CHOICES,) + got.shape[1:], BF16)],
        [],
        2 * ADAPTER_CHOICES * got.size,
    )[0]


def place_kernel(blocks, wide, scalars, *refs):
    shares, refs = refs[:blocks], refs[blocks:]
    qkv_in, query_out, kv_out, proj_in, proj_out, placed = refs
    for j, share in enumerate(shares):
        placed[lax.rem(scalars[2] + blocks - j, blocks)] = share[...].astype(F32)
    r = ADAPTER_RANK
    rows = shares[0].shape[1]
    for a in range(ADAPTER_CHOICES):
        table = jnp.concatenate([placed[b, a] for b in range(blocks)], axis=0)
        qkv_in[a] = table[: 3 * r, :wide]
        query_out[a] = table[3 * r : 4 * r, :wide]
        proj_in[a] = table[4 * r : 5 * r, :wide]
        proj_out[a] = table[5 * r :, :wide]
        kv_out[a, 0] = table[:r, wide:]
        kv_out[a, 1] = table[r : 2 * r, wide:]


def place(scalars, shares, parts):
    r = ADAPTER_RANK
    wide, narrow = MODEL_WIDTH // parts, KEY_FEATURES // parts

    def out(*shape):
        return whole_out((ADAPTER_CHOICES,) + shape, F32)

    return call(
        functools.partial(place_kernel, len(shares), wide),
        scalars,
        1,
        [whole(s) for s in shares],
        [
            out(3 * r, wide),
            out(r, wide),
            out(2, r, narrow),
            out(r, wide),
            out(r, wide),
        ],
        [pltpu.VMEM((len(shares),) + shares[0].shape, F32)],
        0,
    )


def input_kernel(blocks, scalars, *refs):
    gkvs, refs = refs[:blocks], refs[blocks:]
    gq, query_w, kv_w, query_out, kv_out, down, x_ref, gain, grad_middle, out_ref = refs
    grad_kv = functools.reduce(lambda a, b: a + b, [g[...].astype(F32) for g in gkvs])
    grad_k, grad_v = key_and_value(lane_tiles(grad_kv.astype(BF16)))
    lora = jnp.concatenate(
        [
            mm_nt(gq[...], query_out[0]),
            mm_nt(grad_k, kv_out[0, 0]),
            mm_nt(grad_v, kv_out[0, 1]),
        ],
        axis=1,
    )
    lora = (ADAPTER_SCALE * lora).astype(BF16)
    grad = (
        mm_nt(gq[...], query_w[...])
        + mm_nt(grad_k, kv_w[:, :KEY_FEATURES])
        + mm_nt(grad_v, kv_w[:, KEY_FEATURES:])
        + mm(lora, down[0])
    )
    x = x_ref[...].astype(F32)
    inv = lax.rsqrt(jnp.mean(x * x, axis=-1, keepdims=True) + EPS)
    scaled = grad * gain[...]
    out_ref[...] = (
        grad_middle[...]
        + inv * scaled
        - x * (inv * inv * inv) * jnp.mean(scaled * x, axis=-1, keepdims=True)
    )


def input_backward(scalars, gkvs, gq, query_w, kv_w, query_out, kv_out, down, x, gain, grad_middle):
    own = x.shape[0]
    return call(
        functools.partial(input_kernel, len(gkvs)),
        scalars,
        1,
        [whole(g) for g in gkvs]
        + [
            whole(gq),
            whole(query_w),
            whole(kv_w),
            chosen_whole(query_out),
            chosen_whole(kv_out),
            chosen_whole(down),
            whole(x),
            whole(gain),
            whole(grad_middle),
        ],
        [whole_out((own, MODEL_WIDTH), F32)],
        [],
        4 * own * MODEL_WIDTH * KEY_FEATURES,
    )[0]


def shards(
    layer_input_rows,
    routes,
    prefix,
    sequence_adapter_index,
    attention_norm_gain,
    expert_norm_gain,
    query_weight,
    key_value_weight,
    projection_weight,
    router_weight,
    gate_up_weight,
    down_weight,
    adapter_query_key_value_input,
    adapter_query_output,
    adapter_key_value_output,
    adapter_projection_input,
    adapter_projection_output,
    adapter_gate_up_input,
    adapter_gate_up_output,
    adapter_down_input,
    adapter_down_output,
    cotangent,
):
    ctx_size = lax.axis_size("ctx")
    dp_size = lax.axis_size("dp")
    rank = lax.axis_index("ctx")
    own = layer_input_rows.shape[1]
    span = own * ctx_size
    experts_here = gate_up_weight.shape[0]
    experts_all = experts_here * ctx_size
    half = ctx_size // 2
    scalars = jnp.stack([sequence_adapter_index[0], prefix[0], rank]).astype(jnp.int32)
    gain_attn = attention_norm_gain[None]
    gain_ffn = expert_norm_gain[None]

    order = (rank - 1 - jnp.arange(ctx_size, dtype=jnp.int32)) % ctx_size
    positions = (order[:, None] * own + jnp.arange(own, dtype=jnp.int32)[None, :]).reshape(-1)
    size = HEAD_SIZE // 2
    frequency = ROPE_BASE ** (-jnp.arange(size, dtype=F32) / size)
    angles = positions.astype(F32)[:, None] * frequency[None, :]
    cosine, sine = jnp.cos(angles), jnp.sin(angles)
    cosine = jnp.concatenate([cosine] * 4, axis=1)
    sine = jnp.concatenate([-sine, sine] * 2, axis=1)
    allowed = (positions[None, :] <= positions[:, None]) | (positions[None, :] < prefix[0])
    bias = jnp.where(allowed, 0.0, MASKED).astype(F32)
    bias_t = bias[-own:].T
    qkv_in_t = adapter_query_key_value_input.transpose(0, 2, 1)
    proj_in_t = adapter_projection_input.transpose(0, 2, 1)
    router_t = jnp.pad(router_weight.T, ((0, LANES - experts_all), (0, 0)))

    x_own, cot_own = layer_input_rows[0], cotangent[0]
    step = functools.partial(lax.ppermute, axis_name="ctx", perm=rotation(ctx_size, 1))
    inputs = [step(x_own)]
    own_routes = after(routes[0], inputs[0])
    inputs.append(step(after(inputs[0], cosine, sine, bias, bias_t, router_t, scalars)))
    route_blocks = rotations(own_routes, ctx_size)
    while len(inputs) < ctx_size - 1:
        inputs.append(step(inputs[-1]))
    inputs.append(x_own)
    cots = rotations(after(cot_own, inputs[-2], *route_blocks[:-1]), ctx_size)
    expert_ids = jnp.arange(LANES, dtype=jnp.int32)
    routes_all = jnp.concatenate(route_blocks, axis=0)
    named = jnp.any(routes_all[:, :, None] == expert_ids[None, None, :], axis=1).astype(F32)

    q, k, v, normed, lora_in = qkv(
        scalars, inputs, gain_attn, qkv_in_t, query_weight, key_value_weight,
        adapter_query_output, adapter_key_value_output, cosine, sine,
    )
    tables = (
        gate_up_weight,
        down_weight,
        adapter_gate_up_input.transpose(0, 1, 3, 2),
        adapter_gate_up_output,
        adapter_down_input.transpose(0, 1, 3, 2),
        adapter_down_output,
    )

    def attend_half(part, with_own):
        return attend(
            scalars, part, with_own, inputs[part * half : (part + 1) * half], q, k, v, bias,
            projection_weight, proj_in_t, adapter_projection_output, gain_ffn, router_t, named,
        )

    normed_first, gates_first = attend_half(0, False)
    *rows_first, wide, narrow = experts(
        scalars, dp_size, cots[:half], normed_first, gates_first, tables, None
    )
    q = after(q, rows_first[0])
    normed_last, gates_last, attended, lora_out, middle, inv = attend_half(1, True)
    *rows_last, send = experts(
        scalars, dp_size, cots[half:], normed_last, gates_last, tables, (wide, narrow)
    )

    got = send_back(rows_first, ctx_size, 0)
    rows_last[0] = after(rows_last[0], *got)
    got += send_back(rows_last[:-1], ctx_size, half) + rows_last[-1:]
    expert_got = lax.all_to_all(send, "dp", 0, 0, tiled=True)

    grad_middle, branch, grad_lora, gq, *gkvs = middle_backward(
        scalars, got, experts_here, gates_last, router_t, middle, inv, gain_ffn, cot_own,
        projection_weight, proj_in_t, adapter_projection_output, q, k, v, bias_t, cosine, sine,
    )
    shares = adapters(
        scalars, dp_size, gkvs, after(gq, expert_got), adapter_query_output,
        adapter_key_value_output, normed, lora_in, attended, lora_out, branch, grad_lora,
    )
    gkvs = send_back(gkvs[:-1], ctx_size, 0) + [gkvs[-1]]
    shares = send_back([after(shares[0], gkvs[0])] + shares[1:-1], ctx_size, 0) + [shares[-1]]
    up_in, up_out, down_in, down_out = expert_sum(scalars, expert_got, experts_here)
    share = functools.reduce(lambda a, b: a + b, [s.astype(F32) for s in shares]).astype(BF16)
    share = after(share, up_in, gkvs[-2])
    attention_got = lax.all_to_all(share, "dp", 0, 0, tiled=True)
    attention_got = after(attention_got, *gkvs[1:-2])
    share = share_sum(scalars, attention_got, expert_got, experts_here * 3 * ADAPTER_RANK)
    shares = rotations(share, ctx_size)
    shares = shares[-1:] + shares[:-1]
    grad_inputs = input_backward(
        scalars, gkvs, after(gq, share), query_weight, key_value_weight, adapter_query_output,
        adapter_key_value_output, qkv_in_t, x_own, gain_attn, grad_middle,
    )
    shares[1] = after(shares[1], grad_inputs)
    qkv_in, query_out, kv_out, proj_in, proj_out = place(scalars, shares, dp_size)
    return (
        grad_inputs[None],
        qkv_in.transpose(0, 2, 1),
        query_out,
        kv_out,
        proj_in.transpose(0, 2, 1),
        proj_out,
        up_in.transpose(0, 1, 3, 2),
        up_out,
        down_in.transpose(0, 1, 3, 2),
        down_out,
    )


def solution(mesh):
    placed = (
        P("dp", "ctx", None),
        P("dp", "ctx", None),
        P("dp"),
        P("dp"),
        P(),
        P(),
        P(),
        P(),
        P(),
        P(),
        P("ctx", None, None),
        P("ctx", None, None),
        P(),
        P(),
        P(),
        P(),
        P(),
        P(None, "ctx", None, None),
        P(None, "ctx", None, None, None),
        P(None, "ctx", None, None),
        P(None, "ctx", None, None),
        P("dp", "ctx", None),
    )
    return jax.shard_map(
        shards,
        mesh=mesh,
        in_specs=placed,
        out_specs=(
            P("dp", "ctx", None),
            P(None, "dp", None),
            P(None, None, "dp"),
            P(None, None, None, "dp"),
            P(None, "dp", None),
            P(None, None, "dp"),
            P(None, "ctx", "dp", None),
            P(None, "ctx", None, None, "dp"),
            P(None, "ctx", "dp", None),
            P(None, "ctx", None, "dp"),
        ),
        check_vma=False,
    )
```

```python
import functools

import jax
import jax.numpy as jnp
from jax import lax
from jax.experimental import pallas as pl
from jax.experimental.pallas import tpu as pltpu
from jax.sharding import PartitionSpec as P

MODEL_WIDTH = 1536
QUERY_HEADS = 24
KEY_HEADS = 8
HEAD_SIZE = 64
EXPERT_HIDDEN = 512
TOPK = 8
ADAPTER_RANK = 16
ADAPTER_CHOICES = 8
QUERY_FEATURES = 1536
KEY_FEATURES = 512
LANES = 128
PAIRS = KEY_HEADS // 2
PAIR_QUERY = QUERY_FEATURES // PAIRS
GATE_LANES = 8
SENT = MODEL_WIDTH + LANES
COLUMNS = 512

EPS = 1e-05
ADAPTER_SCALE = 2.0
ROPE_BASE = 10000.0
MASKED = -1e30
SCALING = HEAD_SIZE ** (-0.5)
F32 = jnp.float32
BF16 = jnp.bfloat16
MIB = 1024 * 1024


def mm(left, right):
    return jnp.dot(left, right, preferred_element_type=F32)


def mm_nt(left, right):
    return lax.dot_general(left, right, (((1,), (1,)), ((), ())), preferred_element_type=F32)


def mm_tn(left, right):
    return lax.dot_general(left, right, (((0,), (0,)), ((), ())), preferred_element_type=F32)


def rotation(size, by):
    return [(i, (i + by) % size) for i in range(size)]


def after(value, *others):
    return lax.optimization_barrier((value, *others))[0]


def rotations(block, size):
    return [lax.ppermute(block, "ctx", rotation(size, j)) for j in range(1, size)] + [block]


def send_back(blocks, size, first):
    return [
        lax.ppermute(b, "ctx", rotation(size, -1 - j)) for j, b in enumerate(blocks, first)
    ]


def low_lanes(shape):
    return lax.broadcasted_iota(jnp.int32, shape, 1) % LANES < HEAD_SIZE


def turned(tile, cosine, sine):
    half = HEAD_SIZE // 2
    lane = lax.broadcasted_iota(jnp.int32, tile.shape, 1)
    other = jnp.where(
        lane % HEAD_SIZE < half, pltpu.roll(tile, LANES - half, 1), pltpu.roll(tile, half, 1)
    )
    return tile * cosine + other * sine


def variants(block, filler):
    tile, exchanged = lane_tiles(block)
    low = low_lanes(tile.shape)
    fill = jnp.full_like(tile, filler)
    return {
        (0, 0): jnp.where(low, tile, fill),
        (0, 1): jnp.where(low, fill, exchanged),
        (1, 0): jnp.where(low, exchanged, fill),
        (1, 1): jnp.where(low, fill, tile),
    }


def joined(refs):
    return jnp.concatenate([ref[...] for ref in refs], axis=0)


def lane_tiles(block):
    return [block[:, t * LANES : (t + 1) * LANES] for t in range(block.shape[1] // LANES)]


def call(kernel, scalars, grid, ins, outs, scratch, vmem=62, flops=0):
    return list(pl.pallas_call(
        kernel,
        grid_spec=pltpu.PrefetchScalarGridSpec(
            num_scalar_prefetch=1,
            grid=(grid,),
            in_specs=[pl.BlockSpec(b, m) for _, b, m in ins],
            out_specs=[pl.BlockSpec(b, m) for _, _, b, m in outs],
            scratch_shapes=scratch,
        ),
        out_shape=[jax.ShapeDtypeStruct(s, d) for s, d, _, _ in outs],
        compiler_params=pltpu.CompilerParams(
            vmem_limit_bytes=vmem * MIB, dimension_semantics=("arbitrary",)
        ),
        cost_estimate=pl.CostEstimate(
            flops=flops, bytes_accessed=0, transcendentals=0
        ),
    )(scalars, *[a for a, _, _ in ins]))


def whole(array):
    return (array, array.shape, lambda i, s, n=array.ndim: (0,) * n)


def whole_out(shape, dtype):
    return (shape, dtype, shape, lambda i, s, n=len(shape): (0,) * n)


def chosen_whole(table):
    rest = table.shape[1:]
    return (table, (1,) + rest, lambda i, s, n=len(rest): (s[0],) + (0,) * n)


def qkv_kernel(blocks, scalars, *refs):
    xs, refs = refs[:blocks], refs[blocks:]
    gain, down, query_w, kv_w, query_out, kv_out = refs[:6]
    cosines, sines, refs = refs[6 : 6 + blocks], refs[6 + blocks : 6 + 2 * blocks], refs[6 + 2 * blocks :]
    q_refs, k_refs, v_refs, normed_refs, lora_refs = [
        refs[n * blocks : (n + 1) * blocks] for n in range(5)
    ]
    normed, lora = refs[5 * blocks :]
    step = pl.program_id(0)
    q_steps = QUERY_FEATURES // COLUMNS
    own = xs[0].shape[0]
    r = ADAPTER_RANK

    @pl.when(step == 0)
    def _():
        for b, x_ref in enumerate(xs):
            x = x_ref[...].astype(F32)
            inv = lax.rsqrt(jnp.mean(x * x, axis=-1, keepdims=True) + EPS)
            rows = (x * inv * gain[...]).astype(BF16)
            normed[b * own : (b + 1) * own] = rows
            normed_refs[b][...] = rows
        lora[...] = mm_nt(normed[...], down[0]).astype(BF16)
        for b, lora_ref in enumerate(lora_refs):
            lora_ref[...] = lora[b * own : (b + 1) * own]

    def with_exchanged(out_ref, t, tile):
        out_ref[:, 2 * t * LANES : (2 * t + 1) * LANES] = tile.astype(BF16)
        out_ref[:, (2 * t + 1) * LANES : (2 * t + 2) * LANES] = pltpu.roll(
            tile, HEAD_SIZE, 1
        ).astype(BF16)

    @pl.when(step < q_steps)
    def _():
        pre = mm(normed[...], query_w[...])
        pre = pre + mm(lora[:, :r] * ADAPTER_SCALE, query_out[0])
        for b, q_ref in enumerate(q_refs):
            cos, sin = cosines[b][...] * SCALING, sines[b][...] * SCALING
            for t, tile in enumerate(lane_tiles(pre[b * own : (b + 1) * own])):
                q_ref[:, t * LANES : (t + 1) * LANES] = turned(tile, cos, sin).astype(BF16)

    @pl.when(step == q_steps)
    def _():
        pre = mm(normed[...], kv_w[...])
        pre = pre + mm(lora[:, r : 2 * r] * ADAPTER_SCALE, kv_out[0, 0])
        for b, k_ref in enumerate(k_refs):
            cos, sin = cosines[b][...], sines[b][...]
            for t, tile in enumerate(lane_tiles(pre[b * own : (b + 1) * own])):
                with_exchanged(k_ref, t, turned(tile, cos, sin))

    @pl.when(step == q_steps + 1)
    def _():
        pre = mm(normed[...], kv_w[...])
        pre = pre + mm(lora[:, 2 * r :] * ADAPTER_SCALE, kv_out[0, 1])
        for b, v_ref in enumerate(v_refs):
            for t, tile in enumerate(lane_tiles(pre[b * own : (b + 1) * own])):
                with_exchanged(v_ref, t, tile)


def qkv(scalars, xs, gain, down, query_w, kv_w, query_out, kv_out, cosine, sine, places):
    own = xs[0].shape[0]
    blocks = len(xs)
    q_steps = QUERY_FEATURES // COLUMNS
    last = q_steps - 1
    outs = call(
        functools.partial(qkv_kernel, blocks),
        scalars,
        q_steps + 2,
        [whole(x) for x in xs]
        + [
            whole(gain),
            chosen_whole(down),
            (query_w, (MODEL_WIDTH, COLUMNS), lambda i, s: (0, jnp.minimum(i, last))),
            (kv_w, (MODEL_WIDTH, COLUMNS), lambda i, s: (0, jnp.maximum(i - q_steps, 0))),
            (query_out, (1, ADAPTER_RANK, COLUMNS), lambda i, s: (s[0], 0, jnp.minimum(i, last))),
            chosen_whole(kv_out),
        ]
        + [
            (table, (own, LANES), lambda i, s, b=b: (b, 0))
            for table in (cosine, sine)
            for b in places
        ],
        [
            ((own, QUERY_FEATURES), BF16, (own, COLUMNS), lambda i, s: (0, jnp.minimum(i, last)))
            for _ in xs
        ]
        + [whole_out((own, 2 * KEY_FEATURES), BF16) for _ in xs + xs]
        + [whole_out((own, MODEL_WIDTH), BF16) for _ in xs]
        + [whole_out((own, 3 * ADAPTER_RANK), BF16) for _ in xs],
        [
            pltpu.VMEM((own * blocks, MODEL_WIDTH), BF16),
            pltpu.VMEM((own * blocks, 3 * ADAPTER_RANK), BF16),
        ],
        flops=10_000_000_000,
    )
    return [outs[n * blocks : (n + 1) * blocks] for n in range(5)]


def attend_kernel(blocks, scalars, *refs):
    xs, qs, ks, vs = [refs[n * blocks : (n + 1) * blocks] for n in range(4)]
    bias, proj_w, proj_in, proj_out, gain = refs[4 * blocks : 4 * blocks + 5]
    refs = refs[4 * blocks + 5 :]
    normed_refs, att_ref, lora_ref, middle_ref, inv_ref, total, rank_total = (
        refs[:2],
        *refs[2:],
    )
    step = pl.program_id(0)
    own = xs[0].shape[0]
    key_of, value_of = variants(joined(ks), 0), variants(joined(vs), 1)
    parts = []
    for n in range(blocks // 2):
        tiles = lane_tiles(joined(qs[2 * n : 2 * n + 2]))
        rows = slice(2 * n * own, (2 * n + 2) * own)
        heads = []
        for h in range(6):
            at = (h // 3, h % 2)
            scores = mm_nt(tiles[h // 2], key_of[at]) + bias[rows]
            shifted = jnp.exp(scores - jnp.max(scores, axis=-1, keepdims=True)).astype(BF16)
            sums = mm(shifted, value_of[at])
            heads.append(sums / pltpu.roll(sums, HEAD_SIZE, 1))
        low = low_lanes(heads[0].shape)
        parts.append(
            jnp.concatenate(
                [jnp.where(low, heads[2 * t], heads[2 * t + 1]) for t in range(3)], axis=1
            ).astype(BF16)
        )
    attended = jnp.concatenate(parts, axis=0)
    att_ref[...] = attended
    part = mm(attended, proj_w[...])
    rank_part = mm_nt(attended, proj_in[0])

    @pl.when(step == 0)
    def _():
        total[...] = part
        rank_total[...] = rank_part

    @pl.when(step > 0)
    def _():
        total[...] += part
        rank_total[...] += rank_part

    @pl.when(step == PAIRS - 1)
    def _():
        lora_out = rank_total[...].astype(BF16)
        branch = total[...] + mm(lora_out * ADAPTER_SCALE, proj_out[0])
        for b, x_ref in enumerate(xs):
            middle = x_ref[...].astype(F32) + branch[b * own : (b + 1) * own]
            inv = lax.rsqrt(jnp.mean(middle * middle, axis=-1, keepdims=True) + EPS)
            at = b % (blocks // 2)
            normed_refs[b // (blocks // 2)][at * own : (at + 1) * own] = (
                middle * inv * gain[...]
            ).astype(BF16)
            if b == blocks - 1:
                middle_ref[...] = middle
                inv_ref[...] = inv
                lora_ref[...] = lora_out[b * own : (b + 1) * own]


def attend(scalars, xs, qs, ks, vs, bias, proj_w, proj_in, proj_out, gain):
    own = xs[0].shape[0]
    rows = own * len(xs)
    return call(
        functools.partial(attend_kernel, len(xs)),
        scalars,
        PAIRS,
        [whole(x) for x in xs]
        + [(q, (own, PAIR_QUERY), lambda i, s: (0, i)) for q in qs]
        + [(k, (own, 2 * LANES), lambda i, s: (0, i)) for k in ks + vs]
        + [
            whole(bias),
            (proj_w, (PAIR_QUERY, MODEL_WIDTH), lambda i, s: (i, 0)),
            (proj_in, (1, ADAPTER_RANK, PAIR_QUERY), lambda i, s: (s[0], 0, i)),
            chosen_whole(proj_out),
            whole(gain),
        ],
        [
            whole_out((rows // 2, MODEL_WIDTH), BF16),
            whole_out((rows // 2, MODEL_WIDTH), BF16),
            ((rows, QUERY_FEATURES), BF16, (rows, PAIR_QUERY), lambda i, s: (0, i)),
            whole_out((own, ADAPTER_RANK), BF16),
            whole_out((own, MODEL_WIDTH), F32),
            whole_out((own, 1), F32),
        ],
        [pltpu.VMEM((rows, MODEL_WIDTH), F32), pltpu.VMEM((rows, ADAPTER_RANK), F32)],
    )


def expert_kernel(blocks, parts, first, scalars, *refs):
    cots, refs = refs[:blocks], refs[blocks:]
    x_ref, router, up_w, down_w, up_in, up_out, down_in, down_out = refs[:8]
    refs = refs[8:]
    if not first:
        (wide_old, narrow_old), refs = refs[:2], refs[2:]
    rows_refs, refs = refs[:blocks], refs[blocks:]
    if first:
        (wide_ref, narrow_ref), refs = refs[:2], refs[2:]
    else:
        (send_ref, gates_ref), refs = refs[:2], refs[2:]
    gates, cot_all, total, gg_all, rank_in_all, cot_mid_all, grad_rank_all, gated_all = refs
    step = pl.program_id(0)
    here = up_in.shape[1]
    own = cots[0].shape[0]
    r = ADAPTER_RANK
    up_in_rows = up_in[0].reshape(here * 2 * r, MODEL_WIDTH)
    x = x_ref[...]

    @pl.when(step == 0)
    def _():
        for b, cot in enumerate(cots):
            cot_all[b * own : (b + 1) * own] = cot[:, :MODEL_WIDTH]
        mask = jnp.concatenate([cot[:, MODEL_WIDTH:] for cot in cots], axis=0).astype(F32) > 0.0
        chosen = jnp.where(mask, mm_nt(x, router[...]), MASKED)
        shifted = jnp.exp(chosen - jnp.max(chosen, axis=-1, keepdims=True))
        shifted = jnp.where(mask, shifted, 0.0)
        gates[...] = shifted / jnp.sum(shifted, axis=-1, keepdims=True)
        if not first:
            gates_ref[...] = gates[-own:]
        gg_all[...] = jnp.zeros_like(gg_all)
        rank_in = mm_nt(x, up_in_rows).astype(BF16) * ADAPTER_SCALE
        down_out_rows = down_out[0].reshape(here * r, MODEL_WIDTH)
        cot_mid = ADAPTER_SCALE * mm_nt(cot_all[...], down_out_rows)
        for e in range(here):
            rank_in_all[e] = rank_in[:, e * 2 * r : (e + 1) * 2 * r]
            cot_mid_all[e] = cot_mid[:, e * r : (e + 1) * r]

    cot = cot_all[...]
    lane = lax.broadcasted_iota(jnp.int32, gates.shape, 1)
    gate_of = jnp.sum(
        jnp.where(lane == scalars[2] * here + step, gates[...], 0.0), axis=1, keepdims=True
    )
    rank_in2 = rank_in_all[step]
    none = jnp.zeros((r, EXPERT_HIDDEN), BF16)
    out_map = jnp.concatenate(
        [
            jnp.concatenate([up_out[0, 0, 0], none], axis=1),
            jnp.concatenate([none, up_out[0, 0, 1]], axis=1),
        ],
        axis=0,
    )
    pre = mm(x, up_w[0]) + mm(rank_in2, out_map)
    gate_pre, up_pre = pre[:, :EXPERT_HIDDEN], pre[:, EXPERT_HIDDEN:]
    cot_hidden = mm_nt(cot, down_w[0])
    sig = 0.5 * jnp.tanh(0.5 * gate_pre) + 0.5
    silu = gate_pre * sig
    hidden_wide = silu * up_pre
    hidden = hidden_wide.astype(BF16)
    rank_mid = mm_nt(hidden, down_in[0, 0]).astype(BF16).astype(F32)
    cot_mid = cot_mid_all[step]
    gate_grad = jnp.sum(hidden.astype(F32) * cot_hidden, axis=1, keepdims=True) + jnp.sum(
        rank_mid * cot_mid, axis=1, keepdims=True
    )
    gg_lane = lax.broadcasted_iota(jnp.int32, gg_all.shape, 1)
    gg_all[...] += jnp.where(gg_lane == step, gate_grad, 0.0)
    grad_rank_mid = (gate_of * cot_mid).astype(BF16)
    grad_hidden = gate_of * cot_hidden + mm(grad_rank_mid, down_in[0, 0])
    grad_gate = (grad_hidden * up_pre * (sig + silu * (1.0 - sig))).astype(BF16)
    grad_up = (grad_hidden * silu).astype(BF16)
    grad_both = jnp.concatenate([grad_gate, grad_up], axis=1)
    grad_rank_all[step] = (ADAPTER_SCALE * mm_nt(grad_both, out_map)).astype(BF16)
    gated_all[step] = (ADAPTER_SCALE * gate_of * rank_mid).astype(BF16)
    part = mm_nt(grad_both, up_w[0])

    @pl.when(step == 0)
    def _():
        total[...] = part

    @pl.when(step > 0)
    def _():
        total[...] += part

    both = mm_tn(
        jnp.concatenate([rank_in2, grad_rank_mid], axis=1),
        jnp.concatenate([grad_both, hidden], axis=1),
    )
    narrow = jnp.concatenate(
        [
            both[i * r : (i + 1) * r, i * EXPERT_HIDDEN : (i + 1) * EXPERT_HIDDEN]
            for i in range(3)
        ],
        axis=0,
    )
    w, v = MODEL_WIDTH // parts, EXPERT_HIDDEN // parts
    if first:
        narrow_ref[0] = narrow
    else:
        narrow = (narrow + narrow_old[0]).astype(BF16)
        at = pl.ds(pl.multiple_of(step * (3 * r), 16), 3 * r)
        for p in range(parts):
            send_ref[p, at, w:] = narrow[:, p * v : (p + 1) * v]

    @pl.when(step == here - 1)
    def _():
        grad_rank = jnp.concatenate([grad_rank_all[e] for e in range(here)], axis=1)
        gated = jnp.concatenate([gated_all[e] for e in range(here)], axis=1)
        rows = total[...] + mm(grad_rank, up_in_rows)
        high = gg_all[...].astype(BF16).astype(F32)
        both = high + pltpu.roll(gg_all[...] - high, GATE_LANES, 1)
        for b, rows_ref in enumerate(rows_refs):
            at = slice(b * own, (b + 1) * own)
            rows_ref[:, :MODEL_WIDTH] = rows[at].astype(BF16)
            rows_ref[:, MODEL_WIDTH:] = both[at].astype(BF16)
        wide = jnp.concatenate([mm_tn(grad_rank, x), mm_tn(gated, cot)], axis=0)
        if first:
            wide_ref[...] = wide
        else:
            wide = (wide + wide_old[...]).astype(BF16)
            rows = here * 3 * r
            chosen = jnp.full((16, w + v), scalars[0], jnp.int32).astype(F32).astype(BF16)
            for p in range(parts):
                send_ref[p, :rows, :w] = wide[:, p * w : (p + 1) * w]
                send_ref[p, rows:] = chosen


def experts(scalars, parts, cots, x, router, tables, before):
    up_w, down_w, up_in, up_out, down_in, down_out = tables
    own = cots[0].shape[0]
    rows = own * len(cots)
    here = up_w.shape[0]
    r = ADAPTER_RANK
    per_expert = lambda i, s: (i, 0, 0)
    ins = [whole(c) for c in cots] + [
        whole(x),
        whole(router),
        (up_w, (1,) + up_w.shape[1:], per_expert),
        (down_w, (1,) + down_w.shape[1:], per_expert),
        chosen_whole(up_in),
        (up_out, (1, 1) + up_out.shape[2:], lambda i, s: (s[0], i, 0, 0, 0)),
        (down_in, (1, 1) + down_in.shape[2:], lambda i, s: (s[0], i, 0, 0)),
        chosen_whole(down_out),
    ]
    outs = [whole_out((own, SENT), BF16) for _ in cots]
    if before is None:
        outs.append(whole_out((here * 3 * r, MODEL_WIDTH), F32))
        outs.append(((here, 3 * r, EXPERT_HIDDEN), F32, (1, 3 * r, EXPERT_HIDDEN), per_expert))
    else:
        wide, narrow = before
        ins += [whole(wide), (narrow, (1,) + narrow.shape[1:], per_expert)]
        width = (MODEL_WIDTH + EXPERT_HIDDEN) // parts
        outs.append(whole_out((parts, here * 3 * r + 16, width), BF16))
        outs.append(whole_out((own, LANES), F32))
    return call(
        functools.partial(expert_kernel, len(cots), parts, before is None),
        scalars,
        here,
        ins,
        outs,
        [
            pltpu.VMEM((rows, LANES), F32),
            pltpu.VMEM((rows, MODEL_WIDTH), BF16),
            pltpu.VMEM((rows, MODEL_WIDTH), F32),
            pltpu.VMEM((rows, LANES), F32),
            pltpu.VMEM((here, rows, 2 * r), BF16),
            pltpu.VMEM((here, rows, r), F32),
            pltpu.VMEM((here, rows, 2 * r), BF16),
            pltpu.VMEM((here, rows, r), BF16),
        ],
    )


def middle_kernel(blocks, here, scalars, *refs):
    parts, ks, vs, refs = refs[:blocks], refs[blocks : 2 * blocks], refs[2 * blocks : 3 * blocks], refs[3 * blocks :]
    gates, router, middle_ref, inv_ref, gain, cot = refs[:6]
    proj_w, proj_in, proj_out, q_ref, bias, cosine, sine = refs[6:13]
    grad_middle, branch_ref, lora_ref, gq_ref = refs[13:17]
    gkv_refs, grad_att = refs[17:-1], refs[-1]
    step = pl.program_id(0)
    own = q_ref.shape[0]

    @pl.when(step == 0)
    def _():
        gates_own = gates[...]
        lane = lax.broadcasted_iota(jnp.int32, gates_own.shape, 1)
        gg = jnp.zeros_like(gates_own)
        for j, part in enumerate(parts):
            both = part[:, MODEL_WIDTH:].astype(F32)
            both = both + pltpu.roll(both, LANES - GATE_LANES, 1)
            both = jnp.where(lane < here, both, 0.0)
            gg = gg + pltpu.roll(both, lax.rem(scalars[2] + 1 + j, blocks) * here, 1)
        chosen = gates_own * (gg - jnp.sum(gates_own * gg, axis=-1, keepdims=True))
        grad = mm(chosen.astype(BF16), router[...])
        for part in parts:
            grad = grad + part[:, :MODEL_WIDTH].astype(F32)
        scaled = grad * gain[...]
        middle, inv = middle_ref[...], inv_ref[...]
        grad = (
            cot[...].astype(F32)
            + inv * scaled
            - middle * (inv * inv * inv) * jnp.mean(scaled * middle, axis=-1, keepdims=True)
        )
        grad_middle[...] = grad
        branch = grad.astype(BF16)
        branch_ref[...] = branch
        lora = (ADAPTER_SCALE * mm_nt(branch, proj_out[0])).astype(BF16)
        lora_ref[...] = lora
        attended = (mm_nt(branch, proj_w[...]) + mm(lora, proj_in[0])).astype(BF16)
        for i in range(PAIRS):
            grad_att[i] = attended[:, i * PAIR_QUERY : (i + 1) * PAIR_QUERY]

    key_of, value_of = variants(joined(ks), 0), variants(joined(vs), 0)
    queries, grads = lane_tiles(q_ref[...]), lane_tiles(grad_att[step])
    low = low_lanes(queries[0].shape)
    none = jnp.zeros_like(queries[0])
    probs_of, scores_of, query_of, grad_of = [], [], [], []
    for h in range(6):
        at = (h // 3, h % 2)
        scores = mm_nt(key_of[at], queries[h // 2]) + bias[...]
        shifted = jnp.exp(scores - jnp.max(scores, axis=0, keepdims=True))
        probs = shifted * (1.0 / jnp.sum(shifted, axis=0, keepdims=True))
        grad_probs = mm_nt(value_of[at], grads[h // 2])
        grad_scores = probs * (grad_probs - jnp.sum(probs * grad_probs, axis=0, keepdims=True))
        probs_of.append(probs.astype(BF16))
        scores_of.append(grad_scores.astype(BF16))
        inside = low if h % 2 == 0 else jnp.logical_not(low)
        query_of.append(jnp.where(inside, queries[h // 2], none))
        grad_of.append(jnp.where(inside, grads[h // 2], none))

    def summed_over(lefts, rights):
        def over(chosen):
            return mm(
                jnp.concatenate([lefts[h] for h in chosen], axis=1),
                jnp.concatenate([rights[h] for h in chosen], axis=0),
            )

        return over([0, 2, 3, 5]) + pltpu.roll(over([1, 4]), HEAD_SIZE, 1)

    grad_key = summed_over(scores_of, query_of)
    grad_key = turned(grad_key, cosine[...], -sine[...]).astype(BF16)
    grad_value = summed_over(probs_of, grad_of).astype(BF16)
    for b, gkv_ref in enumerate(gkv_refs):
        gkv_ref[:, :LANES] = grad_key[b * own : (b + 1) * own]
        gkv_ref[:, LANES:] = grad_value[b * own : (b + 1) * own]
    key_t = {at: key_of[at].astype(F32).T.astype(BF16) for at in key_of}
    cos, sin = cosine[-own:], -sine[-own:]
    for t in range(3):
        pair = (2 * t, 2 * t + 1)
        tile = mm(
            jnp.concatenate([key_t[h // 3, h % 2] for h in pair], axis=1),
            jnp.concatenate([scores_of[h] for h in pair], axis=0),
        )
        gq_ref[:, t * LANES : (t + 1) * LANES] = turned(SCALING * tile.T, cos, sin).astype(BF16)


def middle_backward(
    scalars, parts, here, gates, router, middle, inv, gain, cot, proj_w, proj_in, proj_out,
    q, ks, vs, bias_t, cosine, sine,
):
    own = q.shape[0]
    return call(
        functools.partial(middle_kernel, len(parts), here),
        scalars,
        PAIRS,
        [whole(part) for part in parts]
        + [(k, (own, 2 * LANES), lambda i, s: (0, i)) for k in ks + vs]
        + [
            whole(gates),
            whole(router),
            whole(middle),
            whole(inv),
            whole(gain),
            (cot, (own, MODEL_WIDTH), lambda i, s: (0, 0)),
            whole(proj_w),
            chosen_whole(proj_in),
            chosen_whole(proj_out),
            (q, (own, PAIR_QUERY), lambda i, s: (0, i)),
            whole(bias_t),
            whole(cosine),
            whole(sine),
        ],
        [
            whole_out((own, MODEL_WIDTH), F32),
            whole_out((own, MODEL_WIDTH), BF16),
            whole_out((own, ADAPTER_RANK), BF16),
            ((own, QUERY_FEATURES), BF16, (own, PAIR_QUERY), lambda i, s: (0, i)),
        ]
        + [
            ((own, 2 * KEY_FEATURES), BF16, (own, 2 * LANES), lambda i, s: (0, i))
            for _ in parts
        ],
        [pltpu.VMEM((PAIRS, own, PAIR_QUERY), BF16)],
        flops=20_000_000_000,
    )


def key_and_value(columns):
    return jnp.concatenate(columns[0::2], axis=1), jnp.concatenate(columns[1::2], axis=1)


def package_sizes(parts, blocks):
    width = (MODEL_WIDTH + KEY_FEATURES) // parts
    tiles = -(-width // LANES)
    return width, tiles, parts * tiles + blocks + 1


def partial_kernel(parts, blocks, scalars, *refs):
    gkvs, lora_in = refs[:blocks], refs[blocks : 2 * blocks]
    gq, query_out, kv_out, lora_out, branch, grad_lora, package = refs[2 * blocks :]
    own = gq.shape[0]
    r = ADAPTER_RANK
    width, tiles, entries = package_sizes(parts, blocks)
    low2 = joined(lora_in) * ADAPTER_SCALE
    gk, gv = key_and_value(lane_tiles(joined(gkvs)))
    wide = jnp.concatenate(
        [mm_tn(low2[-own:, :r], gq[...]), mm_tn(lora_out[...] * ADAPTER_SCALE, branch[...])], axis=0
    ).astype(BF16)
    narrow = jnp.concatenate(
        [mm_tn(low2[:, r : 2 * r], gk), mm_tn(low2[:, 2 * r :], gv)], axis=0
    ).astype(BF16)
    w, v = MODEL_WIDTH // parts, KEY_FEATURES // parts
    for p in range(parts):
        block = [wide[:, p * w : (p + 1) * w], narrow[:, p * v : (p + 1) * v]]
        if width < tiles * LANES:
            block.append(jnp.zeros((2 * r, tiles * LANES - width), BF16))
        for t, tile in enumerate(lane_tiles(jnp.concatenate(block, axis=1))):
            package[p * tiles + t] = tile
    grad_kv = jnp.concatenate([mm_nt(kv_out[0, 0], gk), mm_nt(kv_out[0, 1], gv)], axis=0)
    grad_kv = (ADAPTER_SCALE * grad_kv).astype(BF16)
    for j in range(blocks):
        at = parts * tiles + lax.rem(scalars[2] + 2 * blocks - 1 - j, blocks)
        package[at] = grad_kv[:, j * own : (j + 1) * own]
    grad_q = (ADAPTER_SCALE * mm_nt(query_out[0], gq[...])).astype(BF16)
    grad_out = grad_lora[...].astype(F32).T.astype(BF16)
    package[entries - 1] = jnp.concatenate([grad_q, grad_out], axis=0)


def partials(scalars, parts, gkvs, lora_in, gq, query_out, kv_out, lora_out, branch, grad_lora):
    blocks = len(gkvs)
    entries = package_sizes(parts, blocks)[2]
    return call(
        functools.partial(partial_kernel, parts, blocks),
        scalars,
        1,
        [whole(g) for g in list(gkvs) + lora_in]
        + [
            whole(gq),
            chosen_whole(query_out),
            chosen_whole(kv_out),
            whole(lora_out),
            whole(branch),
            whole(grad_lora),
        ],
        [whole_out((entries, 2 * ADAPTER_RANK, LANES), BF16)],
        [],
    )[0]


def sequence_kernel(parts, blocks, scalars, *refs):
    packages, normed = refs[:blocks], refs[blocks : 2 * blocks]
    attended, send, total = refs[2 * blocks :]
    r = ADAPTER_RANK
    width, tiles, entries = package_sizes(parts, blocks)
    total[...] = functools.reduce(lambda a, b: a + b, [p[...].astype(F32) for p in packages])
    ends = [p[entries - 1] for p in packages]
    order = [lax.rem(scalars[2] + 2 * blocks - 1 - j, blocks) for j in range(blocks)]
    grad_kv = [total[parts * tiles + rank].astype(BF16) for rank in order]
    grad_in = jnp.concatenate(
        [jnp.concatenate([end[:r] for end in ends], axis=1), jnp.concatenate(grad_kv, axis=1)],
        axis=0,
    )
    grad_out = jnp.concatenate([end[r:] for end in ends], axis=1)
    wide = jnp.concatenate(
        [mm(grad_in, joined(normed)), mm(grad_out, attended[...])], axis=0
    ).astype(BF16)
    w = MODEL_WIDTH // parts
    for p in range(parts):
        block = jnp.concatenate([total[p * tiles + t] for t in range(tiles)], axis=1).astype(BF16)
        send[p, : 4 * r, :w] = wide[:, p * w : (p + 1) * w]
        send[p, 4 * r :, :w] = block[:, :w]
        send[p, : 2 * r, w:] = block[:, w:width]
        send[p, 2 * r :, w:] = jnp.zeros((4 * r, width - w), BF16)


def sequence_sums(scalars, parts, packages, normed, attended):
    blocks = len(packages)
    width, _, entries = package_sizes(parts, blocks)
    return call(
        functools.partial(sequence_kernel, parts, blocks),
        scalars,
        1,
        [whole(p) for p in packages + normed] + [whole(attended)],
        [whole_out((parts, 6 * ADAPTER_RANK, width), BF16)],
        [pltpu.VMEM((entries, 2 * ADAPTER_RANK, LANES), F32)],
    )[0]


def summed(received, choices, adapter, senders):
    total = None
    for n in range(senders):
        rows = jnp.where(choices[n, :1, :1].astype(F32) == adapter, received(n), 0.0)
        total = rows if total is None else total + rows
    return total


def expert_sum_kernel(wide, scalars, got, choices, up_in, up_out, down_in, down_out):
    adapter = pl.program_id(0).astype(F32)
    total = summed(lambda n: got[n].astype(F32), choices, adapter, got.shape[0])
    r = ADAPTER_RANK
    here = up_in.shape[1]
    for e in range(here):
        up_in[0, e] = total[e * 2 * r : (e + 1) * 2 * r, :wide]
        down_out[0, e] = total[(2 * here + e) * r : (2 * here + e + 1) * r, :wide]
        rows = total[e * 3 * r : (e + 1) * 3 * r]
        up_out[0, e, 0] = rows[:r, wide:]
        up_out[0, e, 1] = rows[r : 2 * r, wide:]
        down_in[0, e] = rows[2 * r :, wide:]


def expert_sum(scalars, got, here):
    parts, _, width = got.shape
    r = ADAPTER_RANK
    rows = here * 3 * r
    wide, narrow = MODEL_WIDTH // parts, EXPERT_HIDDEN // parts

    def out(*shape):
        return ((ADAPTER_CHOICES,) + shape, F32, (1,) + shape, lambda i, s: (i,) + (0,) * len(shape))

    return call(
        functools.partial(expert_sum_kernel, wide),
        scalars,
        ADAPTER_CHOICES,
        [
            (got, (parts, rows, width), lambda i, s: (0, 0, 0)),
            (got, (parts, 16, width), lambda i, s: (0, rows // 16, 0)),
        ],
        [
            out(here, 2 * r, wide),
            out(here, 2, r, narrow),
            out(here, r, narrow),
            out(here, r, wide),
        ],
        [],
    )


def attention_sum_kernel(wide, scalars, got, choices, qkv_in, query_out, kv_out, proj_in, proj_out):
    adapter = pl.program_id(0).astype(F32)
    total = summed(lambda n: got[n].astype(F32), choices, adapter, got.shape[0])
    r = ADAPTER_RANK
    qkv_in[0] = total[: 3 * r, :wide]
    proj_in[0] = total[3 * r : 4 * r, :wide]
    query_out[0] = total[4 * r : 5 * r, :wide]
    proj_out[0] = total[5 * r :, :wide]
    kv_out[0, 0] = total[:r, wide:]
    kv_out[0, 1] = total[r : 2 * r, wide:]


def attention_sum(scalars, got, expert_got, rows):
    parts, _, width = got.shape
    r = ADAPTER_RANK
    wide, narrow = MODEL_WIDTH // parts, KEY_FEATURES // parts

    def out(*shape):
        return ((ADAPTER_CHOICES,) + shape, F32, (1,) + shape, lambda i, s: (i,) + (0,) * len(shape))

    return call(
        functools.partial(attention_sum_kernel, wide),
        scalars,
        ADAPTER_CHOICES,
        [whole(got), (expert_got, (parts, 16, width), lambda i, s: (0, rows // 16, 0))],
        [
            out(3 * r, wide),
            out(r, wide),
            out(2, r, narrow),
            out(r, wide),
            out(r, wide),
        ],
        [],
    )


def query_kernel(scalars, gq, query_w, out_ref):
    out_ref[...] = mm_nt(gq[...], query_w[...])


def query_backward(scalars, gq, query_w):
    steps = 3
    return call(
        query_kernel,
        scalars,
        steps,
        [whole(gq), (query_w, (MODEL_WIDTH // steps, QUERY_FEATURES), lambda i, s: (i, 0))],
        [(gq.shape, F32, (gq.shape[0], MODEL_WIDTH // steps), lambda i, s: (0, i))],
        [],
    )[0]


def input_kernel(blocks, scalars, *refs):
    gkvs, refs = refs[:blocks], refs[blocks:]
    gq, first, kv_w, query_out, kv_out, down, x_ref, gain, grad_middle, out_ref = refs
    grad_kv = functools.reduce(lambda a, b: a + b, [g[...].astype(F32) for g in gkvs])
    grad_k, grad_v = key_and_value(lane_tiles(grad_kv.astype(BF16)))
    lora = jnp.concatenate(
        [
            mm_nt(gq[...], query_out[0]),
            mm_nt(grad_k, kv_out[0, 0]),
            mm_nt(grad_v, kv_out[0, 1]),
        ],
        axis=1,
    )
    lora = (ADAPTER_SCALE * lora).astype(BF16)
    grad = (
        first[...]
        + mm_nt(grad_k, kv_w[:, :KEY_FEATURES])
        + mm_nt(grad_v, kv_w[:, KEY_FEATURES:])
        + mm(lora, down[0])
    )
    x = x_ref[...].astype(F32)
    inv = lax.rsqrt(jnp.mean(x * x, axis=-1, keepdims=True) + EPS)
    scaled = grad * gain[...]
    out_ref[...] = (
        grad_middle[...]
        + inv * scaled
        - x * (inv * inv * inv) * jnp.mean(scaled * x, axis=-1, keepdims=True)
    )


def input_backward(scalars, gkvs, gq, first, kv_w, query_out, kv_out, down, x, gain, grad_middle):
    own = x.shape[0]
    return call(
        functools.partial(input_kernel, len(gkvs)),
        scalars,
        1,
        [whole(g) for g in gkvs]
        + [
            whole(gq),
            whole(first),
            whole(kv_w),
            chosen_whole(query_out),
            chosen_whole(kv_out),
            chosen_whole(down),
            whole(x),
            whole(gain),
            whole(grad_middle),
        ],
        [whole_out((own, MODEL_WIDTH), F32)],
        [],
        flops=20_000_000_000,
    )[0]


def shards(
    layer_input_rows,
    routes,
    prefix,
    sequence_adapter_index,
    attention_norm_gain,
    expert_norm_gain,
    query_weight,
    key_value_weight,
    projection_weight,
    router_weight,
    gate_up_weight,
    down_weight,
    adapter_query_key_value_input,
    adapter_query_output,
    adapter_key_value_output,
    adapter_projection_input,
    adapter_projection_output,
    adapter_gate_up_input,
    adapter_gate_up_output,
    adapter_down_input,
    adapter_down_output,
    cotangent,
):
    ctx_size = lax.axis_size("ctx")
    dp_size = lax.axis_size("dp")
    rank = lax.axis_index("ctx")
    own = layer_input_rows.shape[1]
    span = own * ctx_size
    experts_here = gate_up_weight.shape[0]
    experts_all = experts_here * ctx_size
    half = ctx_size // 2
    scalars = jnp.stack([sequence_adapter_index[0], prefix[0], rank]).astype(jnp.int32)
    gain_attn = attention_norm_gain[None]
    gain_ffn = expert_norm_gain[None]

    order = (rank - 1 - jnp.arange(ctx_size, dtype=jnp.int32)) % ctx_size
    positions = (order[:, None] * own + jnp.arange(own, dtype=jnp.int32)[None, :]).reshape(-1)
    size = HEAD_SIZE // 2
    frequency = ROPE_BASE ** (-jnp.arange(size, dtype=F32) / size)
    angles = positions.astype(F32)[:, None] * frequency[None, :]
    cosine, sine = jnp.cos(angles), jnp.sin(angles)
    cosine = jnp.concatenate([cosine] * 4, axis=1)
    sine = jnp.concatenate([-sine, sine] * 2, axis=1)
    allowed = (positions[None, :] <= positions[:, None]) | (positions[None, :] < prefix[0])
    bias = jnp.where(allowed, 0.0, MASKED).astype(F32)
    bias_t = bias[-own:].T
    qkv_in_t = adapter_query_key_value_input.transpose(0, 2, 1)
    proj_in_t = adapter_projection_input.transpose(0, 2, 1)
    router_t = jnp.pad(router_weight.T, ((0, LANES - experts_all), (0, 0)))

    expert_ids = jnp.arange(LANES, dtype=jnp.int32)
    named = jnp.any(routes[0][:, :, None] == expert_ids[None, None, :], axis=1).astype(BF16)
    cot_own = jnp.concatenate([cotangent[0], named], axis=1)
    x_own = layer_input_rows[0]
    step = functools.partial(lax.ppermute, axis_name="ctx", perm=rotation(ctx_size, 1))
    inputs = [step(x_own)]
    inputs.append(step(after(inputs[0], cosine, sine, bias, bias_t, router_t, scalars, cot_own)))
    while len(inputs) < ctx_size - 1:
        inputs.append(step(inputs[-1]))
    inputs.append(x_own)
    cots = None
    q, k, v, normed, lora_in = [], [], [], [], []
    now = scalars
    for some in ([ctx_size - 1] + list(range(ctx_size - 2)), [ctx_size - 2]):
        made = qkv(
            now, [inputs[b] for b in some], gain_attn, qkv_in_t, query_weight, key_value_weight,
            adapter_query_output, adapter_key_value_output, cosine, sine, some,
        )
        for all_of, some_of in zip((q, k, v, normed, lora_in), made):
            all_of += some_of
        now = after(scalars, q[0])
        if cots is None:
            cots = rotations(after(cot_own, q[0]), ctx_size)
    q, k, v, normed, lora_in = [a[1:] + a[:1] for a in (q, k, v, normed, lora_in)]
    tables = (
        gate_up_weight,
        down_weight,
        adapter_gate_up_input.transpose(0, 1, 3, 2),
        adapter_gate_up_output,
        adapter_down_input.transpose(0, 1, 3, 2),
        adapter_down_output,
    )

    normed_first, normed_last, attended, lora_out, middle, inv = attend(
        scalars, inputs, q, k, v, bias, projection_weight, proj_in_t, adapter_projection_output,
        gain_ffn,
    )
    *rows_first, wide, narrow = experts(
        scalars, dp_size, cots[:half], normed_first, router_t, tables, None
    )
    *rows_last, send, gates = experts(
        scalars, dp_size, cots[half:], normed_last, router_t, tables, (wide, narrow)
    )

    got = send_back(rows_first, ctx_size, 0)
    rows_last[0] = after(rows_last[0], *got)
    got += send_back(rows_last[:-1], ctx_size, half) + rows_last[-1:]
    grad_middle, branch, grad_lora, gq, *gkvs = middle_backward(
        scalars, got, experts_here, gates, router_t, middle, inv, gain_ffn, cot_own,
        projection_weight, proj_in_t, adapter_projection_output, q[-1], k, v, bias_t, cosine, sine,
    )
    expert_got = lax.all_to_all(send, "dp", 0, 0, tiled=True)
    package = partials(
        scalars, dp_size, gkvs, lora_in, after(gq, expert_got), adapter_query_output, adapter_key_value_output,
        lora_out, branch, grad_lora,
    )
    gkvs = list(gkvs)
    gkvs[0] = send_back(gkvs[:1], ctx_size, 0)[0]
    packages = rotations(after(package, gkvs[0]), ctx_size)
    first = query_backward(scalars, after(gq, package), query_weight)
    up_in, up_out, down_in, down_out = expert_sum(
        scalars, after(expert_got, first), experts_here
    )
    later = [after(g, first, up_in, *packages[:-1]) for g in gkvs[1:-1]]
    gkvs[1:-1] = send_back(later, ctx_size, 1)
    packages[1] = after(packages[1], first, up_in)
    attention_send = sequence_sums(scalars, dp_size, packages, normed, attended)
    attention_got = lax.all_to_all(attention_send, "dp", 0, 0, tiled=True)
    grad_inputs = input_backward(
        scalars, gkvs, after(gq, attention_send), first, key_value_weight, adapter_query_output,
        adapter_key_value_output, qkv_in_t, x_own, gain_attn, grad_middle,
    )
    attention_got = after(attention_got, grad_inputs)
    qkv_in, query_out, kv_out, proj_in, proj_out = attention_sum(
        scalars, attention_got, expert_got, experts_here * 3 * ADAPTER_RANK
    )
    return (
        grad_inputs[None],
        qkv_in.transpose(0, 2, 1),
        query_out,
        kv_out,
        proj_in.transpose(0, 2, 1),
        proj_out,
        up_in.transpose(0, 1, 3, 2),
        up_out,
        down_in.transpose(0, 1, 3, 2),
        down_out,
    )


def solution(mesh):
    placed = (
        P("dp", "ctx", None),
        P("dp", "ctx", None),
        P("dp"),
        P("dp"),
        P(),
        P(),
        P(),
        P(),
        P(),
        P(),
        P("ctx", None, None),
        P("ctx", None, None),
        P(),
        P(),
        P(),
        P(),
        P(),
        P(None, "ctx", None, None),
        P(None, "ctx", None, None, None),
        P(None, "ctx", None, None),
        P(None, "ctx", None, None),
        P("dp", "ctx", None),
    )
    return jax.shard_map(
        shards,
        mesh=mesh,
        in_specs=placed,
        out_specs=(
            P("dp", "ctx", None),
            P(None, "dp", None),
            P(None, None, "dp"),
            P(None, None, None, "dp"),
            P(None, "dp", None),
            P(None, None, "dp"),
            P(None, "ctx", "dp", None),
            P(None, "ctx", None, None, "dp"),
            P(None, "ctx", "dp", None),
            P(None, "ctx", None, "dp"),
        ),
        check_vma=False,
    )
```

```python
import functools

import jax
import jax.numpy as jnp
from jax import lax
from jax.experimental import pallas as pl
from jax.experimental.pallas import tpu as pltpu
from jax.sharding import PartitionSpec as P

MODEL_WIDTH = 1536
QUERY_HEADS = 24
KEY_HEADS = 8
HEAD_SIZE = 64
EXPERT_HIDDEN = 512
TOPK = 8
ADAPTER_RANK = 16
ADAPTER_CHOICES = 8
QUERY_FEATURES = 1536
KEY_FEATURES = 512
LANES = 128
PAIRS = KEY_HEADS // 2
PAIR_QUERY = QUERY_FEATURES // PAIRS
GATE_LANES = 8
SENT = MODEL_WIDTH + LANES
AHEAD = 2
COLUMNS = 512

EPS = 1e-05
ADAPTER_SCALE = 2.0
ROPE_BASE = 10000.0
MASKED = -1e30
SCALING = HEAD_SIZE ** (-0.5)
F32 = jnp.float32
BF16 = jnp.bfloat16
MIB = 1024 * 1024


def mm(left, right):
    return jnp.dot(left, right, preferred_element_type=F32)


def mm_nt(left, right):
    return lax.dot_general(left, right, (((1,), (1,)), ((), ())), preferred_element_type=F32)


def mm_tn(left, right):
    return lax.dot_general(left, right, (((0,), (0,)), ((), ())), preferred_element_type=F32)


def rotation(size, by):
    return [(i, (i + by) % size) for i in range(size)]


def after(value, *others):
    return lax.optimization_barrier((value, *others))[0]


def rotations(block, size):
    return [lax.ppermute(block, "ctx", rotation(size, j)) for j in range(1, size)] + [block]


def send_back(blocks, size, first):
    return [
        lax.ppermute(b, "ctx", rotation(size, -1 - j)) for j, b in enumerate(blocks, first)
    ]


def low_lanes(shape):
    return lax.broadcasted_iota(jnp.int32, shape, 1) % LANES < HEAD_SIZE


def turned(tile, cosine, sine):
    half = HEAD_SIZE // 2
    lane = lax.broadcasted_iota(jnp.int32, tile.shape, 1)
    other = jnp.where(
        lane % HEAD_SIZE < half, pltpu.roll(tile, LANES - half, 1), pltpu.roll(tile, half, 1)
    )
    return tile * cosine + other * sine


def variants(block, filler):
    tile, exchanged = lane_tiles(block)
    low = low_lanes(tile.shape)
    fill = jnp.full_like(tile, filler)
    return {
        (0, 0): jnp.where(low, tile, fill),
        (0, 1): jnp.where(low, fill, exchanged),
        (1, 0): jnp.where(low, exchanged, fill),
        (1, 1): jnp.where(low, fill, tile),
    }


def joined(refs):
    return jnp.concatenate([ref[...] for ref in refs], axis=0)


def lane_tiles(block):
    return [block[:, t * LANES : (t + 1) * LANES] for t in range(block.shape[1] // LANES)]


def call(kernel, scalars, grid, ins, outs, scratch, vmem=62, flops=0):
    return list(pl.pallas_call(
        kernel,
        grid_spec=pltpu.PrefetchScalarGridSpec(
            num_scalar_prefetch=1,
            grid=(grid,),
            in_specs=[pl.BlockSpec(b, m) for _, b, m in ins],
            out_specs=[pl.BlockSpec(b, m) for _, _, b, m in outs],
            scratch_shapes=scratch,
        ),
        out_shape=[jax.ShapeDtypeStruct(s, d) for s, d, _, _ in outs],
        compiler_params=pltpu.CompilerParams(
            vmem_limit_bytes=vmem * MIB, dimension_semantics=("arbitrary",)
        ),
        cost_estimate=pl.CostEstimate(
            flops=flops, bytes_accessed=0, transcendentals=0
        ),
    )(scalars, *[a for a, _, _ in ins]))


def whole(array):
    return (array, array.shape, lambda i, s, n=array.ndim: (0,) * n)


def whole_out(shape, dtype):
    return (shape, dtype, shape, lambda i, s, n=len(shape): (0,) * n)


def chosen_whole(table):
    rest = table.shape[1:]
    return (table, (1,) + rest, lambda i, s, n=len(rest): (s[0],) + (0,) * n)


def qkv_kernel(blocks, scalars, *refs):
    xs, refs = refs[:blocks], refs[blocks:]
    gain, down, query_w, kv_w, query_out, kv_out = refs[:6]
    cosines, sines, refs = refs[6 : 6 + blocks], refs[6 + blocks : 6 + 2 * blocks], refs[6 + 2 * blocks :]
    q_refs, k_refs, v_refs, normed_refs, lora_refs = [
        refs[n * blocks : (n + 1) * blocks] for n in range(5)
    ]
    normed, lora = refs[5 * blocks :]
    step = pl.program_id(0)
    q_steps = QUERY_FEATURES // COLUMNS
    own = xs[0].shape[0]
    r = ADAPTER_RANK

    @pl.when(step == 0)
    def _():
        for b, x_ref in enumerate(xs):
            x = x_ref[...].astype(F32)
            inv = lax.rsqrt(jnp.mean(x * x, axis=-1, keepdims=True) + EPS)
            rows = (x * inv * gain[...]).astype(BF16)
            normed[b * own : (b + 1) * own] = rows
            normed_refs[b][...] = rows
        lora[...] = mm_nt(normed[...], down[0]).astype(BF16)
        for b, lora_ref in enumerate(lora_refs):
            lora_ref[...] = lora[b * own : (b + 1) * own]

    def with_exchanged(out_ref, t, tile):
        out_ref[:, 2 * t * LANES : (2 * t + 1) * LANES] = tile.astype(BF16)
        out_ref[:, (2 * t + 1) * LANES : (2 * t + 2) * LANES] = pltpu.roll(
            tile, HEAD_SIZE, 1
        ).astype(BF16)

    @pl.when(step < q_steps)
    def _():
        pre = mm(normed[...], query_w[...])
        pre = pre + mm(lora[:, :r] * ADAPTER_SCALE, query_out[0])
        for b, q_ref in enumerate(q_refs):
            cos, sin = cosines[b][...] * SCALING, sines[b][...] * SCALING
            for t, tile in enumerate(lane_tiles(pre[b * own : (b + 1) * own])):
                q_ref[:, t * LANES : (t + 1) * LANES] = turned(tile, cos, sin).astype(BF16)

    @pl.when(step == q_steps)
    def _():
        pre = mm(normed[...], kv_w[...])
        pre = pre + mm(lora[:, r : 2 * r] * ADAPTER_SCALE, kv_out[0, 0])
        for b, k_ref in enumerate(k_refs):
            cos, sin = cosines[b][...], sines[b][...]
            for t, tile in enumerate(lane_tiles(pre[b * own : (b + 1) * own])):
                with_exchanged(k_ref, t, turned(tile, cos, sin))

    @pl.when(step == q_steps + 1)
    def _():
        pre = mm(normed[...], kv_w[...])
        pre = pre + mm(lora[:, 2 * r :] * ADAPTER_SCALE, kv_out[0, 1])
        for b, v_ref in enumerate(v_refs):
            for t, tile in enumerate(lane_tiles(pre[b * own : (b + 1) * own])):
                with_exchanged(v_ref, t, tile)


def qkv(scalars, xs, gain, down, query_w, kv_w, query_out, kv_out, cosine, sine, places):
    own = xs[0].shape[0]
    blocks = len(xs)
    q_steps = QUERY_FEATURES // COLUMNS
    last = q_steps - 1
    outs = call(
        functools.partial(qkv_kernel, blocks),
        scalars,
        q_steps + 2,
        [whole(x) for x in xs]
        + [
            whole(gain),
            chosen_whole(down),
            (query_w, (MODEL_WIDTH, COLUMNS), lambda i, s: (0, jnp.minimum(i, last))),
            (kv_w, (MODEL_WIDTH, COLUMNS), lambda i, s: (0, jnp.maximum(i - q_steps, 0))),
            (query_out, (1, ADAPTER_RANK, COLUMNS), lambda i, s: (s[0], 0, jnp.minimum(i, last))),
            chosen_whole(kv_out),
        ]
        + [
            (table, (own, LANES), lambda i, s, b=b: (b, 0))
            for table in (cosine, sine)
            for b in places
        ],
        [
            ((own, QUERY_FEATURES), BF16, (own, COLUMNS), lambda i, s: (0, jnp.minimum(i, last)))
            for _ in xs
        ]
        + [whole_out((own, 2 * KEY_FEATURES), BF16) for _ in xs + xs]
        + [whole_out((own, MODEL_WIDTH), BF16) for _ in xs]
        + [whole_out((own, 3 * ADAPTER_RANK), BF16) for _ in xs],
        [
            pltpu.VMEM((own * blocks, MODEL_WIDTH), BF16),
            pltpu.VMEM((own * blocks, 3 * ADAPTER_RANK), BF16),
        ],
        flops=10_000_000_000,
    )
    return [outs[n * blocks : (n + 1) * blocks] for n in range(5)]


def attend_kernel(blocks, scalars, *refs):
    xs, qs, ks, vs = [refs[n * blocks : (n + 1) * blocks] for n in range(4)]
    bias, proj_w, proj_in, proj_out, gain = refs[4 * blocks : 4 * blocks + 5]
    refs = refs[4 * blocks + 5 :]
    normed_refs, att_ref, lora_ref, middle_ref, inv_ref, total, rank_total = (
        refs[:2],
        *refs[2:],
    )
    step = pl.program_id(0)
    own = xs[0].shape[0]
    key_of, value_of = variants(joined(ks), 0), variants(joined(vs), 1)
    tiles = [lane_tiles(joined(qs[2 * n : 2 * n + 2])) for n in range(blocks // 2)]

    def scores_of(n, h):
        rows = slice(2 * n * own, (2 * n + 2) * own)
        return mm_nt(tiles[n][h // 2], key_of[h // 3, h % 2]) + bias[rows]

    todo = [(n, h) for n in range(blocks // 2) for h in range(6)]
    waiting = [scores_of(*item) for item in todo[:AHEAD]]
    heads = []
    for i, (n, h) in enumerate(todo):
        scores = waiting.pop(0)
        if i + AHEAD < len(todo):
            waiting.append(scores_of(*todo[i + AHEAD]))
        shifted = jnp.exp(scores - jnp.max(scores, axis=-1, keepdims=True)).astype(BF16)
        sums = mm(shifted, value_of[h // 3, h % 2])
        heads.append(sums / pltpu.roll(sums, HEAD_SIZE, 1))
    low = low_lanes(heads[0].shape)
    parts = []
    for n in range(blocks // 2):
        some = heads[6 * n : 6 * n + 6]
        pairs = [jnp.where(low, some[2 * t], some[2 * t + 1]) for t in range(3)]
        parts.append(jnp.concatenate(pairs, axis=1).astype(BF16))
    attended = jnp.concatenate(parts, axis=0)
    att_ref[...] = attended
    part = mm(attended, proj_w[...])
    rank_part = mm_nt(attended, proj_in[0])

    @pl.when(step == 0)
    def _():
        total[...] = part
        rank_total[...] = rank_part

    @pl.when(step > 0)
    def _():
        total[...] += part
        rank_total[...] += rank_part

    @pl.when(step == PAIRS - 1)
    def _():
        lora_out = rank_total[...].astype(BF16)
        branch = total[...] + mm(lora_out * ADAPTER_SCALE, proj_out[0])
        for b, x_ref in enumerate(xs):
            middle = x_ref[...].astype(F32) + branch[b * own : (b + 1) * own]
            inv = lax.rsqrt(jnp.mean(middle * middle, axis=-1, keepdims=True) + EPS)
            at = b % (blocks // 2)
            normed_refs[b // (blocks // 2)][at * own : (at + 1) * own] = (
                middle * inv * gain[...]
            ).astype(BF16)
            if b == blocks - 1:
                middle_ref[...] = middle
                inv_ref[...] = inv
                lora_ref[...] = lora_out[b * own : (b + 1) * own]


def attend(scalars, xs, qs, ks, vs, bias, proj_w, proj_in, proj_out, gain):
    own = xs[0].shape[0]
    rows = own * len(xs)
    return call(
        functools.partial(attend_kernel, len(xs)),
        scalars,
        PAIRS,
        [whole(x) for x in xs]
        + [(q, (own, PAIR_QUERY), lambda i, s: (0, i)) for q in qs]
        + [(k, (own, 2 * LANES), lambda i, s: (0, i)) for k in ks + vs]
        + [
            whole(bias),
            (proj_w, (PAIR_QUERY, MODEL_WIDTH), lambda i, s: (i, 0)),
            (proj_in, (1, ADAPTER_RANK, PAIR_QUERY), lambda i, s: (s[0], 0, i)),
            chosen_whole(proj_out),
            whole(gain),
        ],
        [
            whole_out((rows // 2, MODEL_WIDTH), BF16),
            whole_out((rows // 2, MODEL_WIDTH), BF16),
            ((rows, QUERY_FEATURES), BF16, (rows, PAIR_QUERY), lambda i, s: (0, i)),
            whole_out((own, ADAPTER_RANK), BF16),
            whole_out((own, MODEL_WIDTH), F32),
            whole_out((own, 1), F32),
        ],
        [pltpu.VMEM((rows, MODEL_WIDTH), F32), pltpu.VMEM((rows, ADAPTER_RANK), F32)],
    )


def expert_kernel(blocks, parts, first, scalars, *refs):
    cots, refs = refs[:blocks], refs[blocks:]
    x_ref, router, up_w, down_w, up_in, up_out, down_in, down_out = refs[:8]
    refs = refs[8:]
    if not first:
        (wide_old, narrow_old), refs = refs[:2], refs[2:]
    rows_refs, refs = refs[:blocks], refs[blocks:]
    if first:
        (wide_ref, narrow_ref), refs = refs[:2], refs[2:]
    else:
        (send_ref, gates_ref), refs = refs[:2], refs[2:]
    gates, cot_all, total, gg_all, rank_in_all, cot_mid_all, grad_rank_all, gated_all = refs
    step = pl.program_id(0)
    here = up_in.shape[1]
    own = cots[0].shape[0]
    r = ADAPTER_RANK
    up_in_rows = up_in[0].reshape(here * 2 * r, MODEL_WIDTH)
    x = x_ref[...]

    @pl.when(step == 0)
    def _():
        for b, cot in enumerate(cots):
            cot_all[b * own : (b + 1) * own] = cot[:, :MODEL_WIDTH]
        mask = jnp.concatenate([cot[:, MODEL_WIDTH:] for cot in cots], axis=0).astype(F32) > 0.0
        chosen = jnp.where(mask, mm_nt(x, router[...]), MASKED)
        shifted = jnp.exp(chosen - jnp.max(chosen, axis=-1, keepdims=True))
        shifted = jnp.where(mask, shifted, 0.0)
        gates[...] = shifted / jnp.sum(shifted, axis=-1, keepdims=True)
        if not first:
            gates_ref[...] = gates[-own:]
        gg_all[...] = jnp.zeros_like(gg_all)
        rank_in = mm_nt(x, up_in_rows).astype(BF16) * ADAPTER_SCALE
        down_out_rows = down_out[0].reshape(here * r, MODEL_WIDTH)
        cot_mid = ADAPTER_SCALE * mm_nt(cot_all[...], down_out_rows)
        for e in range(here):
            rank_in_all[e] = rank_in[:, e * 2 * r : (e + 1) * 2 * r]
            cot_mid_all[e] = cot_mid[:, e * r : (e + 1) * r]

    cot = cot_all[...]
    lane = lax.broadcasted_iota(jnp.int32, gates.shape, 1)
    gate_of = jnp.sum(
        jnp.where(lane == scalars[2] * here + step, gates[...], 0.0), axis=1, keepdims=True
    )
    rank_in2 = rank_in_all[step]
    none = jnp.zeros((r, EXPERT_HIDDEN), BF16)
    out_map = jnp.concatenate(
        [
            jnp.concatenate([up_out[0, 0, 0], none], axis=1),
            jnp.concatenate([none, up_out[0, 0, 1]], axis=1),
        ],
        axis=0,
    )
    pre = mm(x, up_w[0]) + mm(rank_in2, out_map)
    gate_pre, up_pre = pre[:, :EXPERT_HIDDEN], pre[:, EXPERT_HIDDEN:]
    cot_hidden = mm_nt(cot, down_w[0])
    sig = 0.5 * jnp.tanh(0.5 * gate_pre) + 0.5
    silu = gate_pre * sig
    hidden_wide = silu * up_pre
    hidden = hidden_wide.astype(BF16)
    rank_mid = mm_nt(hidden, down_in[0, 0]).astype(BF16).astype(F32)
    cot_mid = cot_mid_all[step]
    gate_grad = jnp.sum(hidden.astype(F32) * cot_hidden, axis=1, keepdims=True) + jnp.sum(
        rank_mid * cot_mid, axis=1, keepdims=True
    )
    gg_lane = lax.broadcasted_iota(jnp.int32, gg_all.shape, 1)
    gg_all[...] += jnp.where(gg_lane == step, gate_grad, 0.0)
    grad_rank_mid = (gate_of * cot_mid).astype(BF16)
    grad_hidden = gate_of * cot_hidden + mm(grad_rank_mid, down_in[0, 0])
    grad_gate = (grad_hidden * up_pre * (sig + silu * (1.0 - sig))).astype(BF16)
    grad_up = (grad_hidden * silu).astype(BF16)
    grad_both = jnp.concatenate([grad_gate, grad_up], axis=1)
    grad_rank_all[step] = (ADAPTER_SCALE * mm_nt(grad_both, out_map)).astype(BF16)
    gated_all[step] = (ADAPTER_SCALE * gate_of * rank_mid).astype(BF16)
    part = mm_nt(grad_both, up_w[0])

    @pl.when(step == 0)
    def _():
        total[...] = part

    @pl.when(step > 0)
    def _():
        total[...] += part

    both = mm_tn(
        jnp.concatenate([rank_in2, grad_rank_mid], axis=1),
        jnp.concatenate([grad_both, hidden], axis=1),
    )
    narrow = jnp.concatenate(
        [
            both[i * r : (i + 1) * r, i * EXPERT_HIDDEN : (i + 1) * EXPERT_HIDDEN]
            for i in range(3)
        ],
        axis=0,
    )
    w, v = MODEL_WIDTH // parts, EXPERT_HIDDEN // parts
    if first:
        narrow_ref[0] = narrow
    else:
        narrow = (narrow + narrow_old[0]).astype(BF16)
        at = pl.ds(pl.multiple_of(step * (3 * r), 16), 3 * r)
        for p in range(parts):
            send_ref[p, at, w:] = narrow[:, p * v : (p + 1) * v]

    @pl.when(step == here - 1)
    def _():
        grad_rank = jnp.concatenate([grad_rank_all[e] for e in range(here)], axis=1)
        gated = jnp.concatenate([gated_all[e] for e in range(here)], axis=1)
        rows = total[...] + mm(grad_rank, up_in_rows)
        high = gg_all[...].astype(BF16).astype(F32)
        both = high + pltpu.roll(gg_all[...] - high, GATE_LANES, 1)
        for b, rows_ref in enumerate(rows_refs):
            at = slice(b * own, (b + 1) * own)
            rows_ref[:, :MODEL_WIDTH] = rows[at].astype(BF16)
            rows_ref[:, MODEL_WIDTH:] = both[at].astype(BF16)
        wide = jnp.concatenate([mm_tn(grad_rank, x), mm_tn(gated, cot)], axis=0)
        if first:
            wide_ref[...] = wide
        else:
            wide = (wide + wide_old[...]).astype(BF16)
            rows = here * 3 * r
            chosen = jnp.full((16, w + v), scalars[0], jnp.int32).astype(F32).astype(BF16)
            for p in range(parts):
                send_ref[p, :rows, :w] = wide[:, p * w : (p + 1) * w]
                send_ref[p, rows:] = chosen


def experts(scalars, parts, cots, x, router, tables, before):
    up_w, down_w, up_in, up_out, down_in, down_out = tables
    own = cots[0].shape[0]
    rows = own * len(cots)
    here = up_w.shape[0]
    r = ADAPTER_RANK
    per_expert = lambda i, s: (i, 0, 0)
    ins = [whole(c) for c in cots] + [
        whole(x),
        whole(router),
        (up_w, (1,) + up_w.shape[1:], per_expert),
        (down_w, (1,) + down_w.shape[1:], per_expert),
        chosen_whole(up_in),
        (up_out, (1, 1) + up_out.shape[2:], lambda i, s: (s[0], i, 0, 0, 0)),
        (down_in, (1, 1) + down_in.shape[2:], lambda i, s: (s[0], i, 0, 0)),
        chosen_whole(down_out),
    ]
    outs = [whole_out((own, SENT), BF16) for _ in cots]
    if before is None:
        outs.append(whole_out((here * 3 * r, MODEL_WIDTH), F32))
        outs.append(((here, 3 * r, EXPERT_HIDDEN), F32, (1, 3 * r, EXPERT_HIDDEN), per_expert))
    else:
        wide, narrow = before
        ins += [whole(wide), (narrow, (1,) + narrow.shape[1:], per_expert)]
        width = (MODEL_WIDTH + EXPERT_HIDDEN) // parts
        outs.append(whole_out((parts, here * 3 * r + 16, width), BF16))
        outs.append(whole_out((own, LANES), F32))
    return call(
        functools.partial(expert_kernel, len(cots), parts, before is None),
        scalars,
        here,
        ins,
        outs,
        [
            pltpu.VMEM((rows, LANES), F32),
            pltpu.VMEM((rows, MODEL_WIDTH), BF16),
            pltpu.VMEM((rows, MODEL_WIDTH), F32),
            pltpu.VMEM((rows, LANES), F32),
            pltpu.VMEM((here, rows, 2 * r), BF16),
            pltpu.VMEM((here, rows, r), F32),
            pltpu.VMEM((here, rows, 2 * r), BF16),
            pltpu.VMEM((here, rows, r), BF16),
        ],
    )


def middle_kernel(blocks, here, scalars, *refs):
    parts, ks, vs, refs = refs[:blocks], refs[blocks : 2 * blocks], refs[2 * blocks : 3 * blocks], refs[3 * blocks :]
    gates, router, middle_ref, inv_ref, gain, cot = refs[:6]
    proj_w, proj_in, proj_out, q_ref, bias, cosine, sine = refs[6:13]
    grad_middle, branch_ref, lora_ref, gq_ref = refs[13:17]
    gkv_refs, grad_att = refs[17:-1], refs[-1]
    step = pl.program_id(0)
    own = q_ref.shape[0]

    @pl.when(step == 0)
    def _():
        gates_own = gates[...]
        lane = lax.broadcasted_iota(jnp.int32, gates_own.shape, 1)
        gg = jnp.zeros_like(gates_own)
        for j, part in enumerate(parts):
            both = part[:, MODEL_WIDTH:].astype(F32)
            both = both + pltpu.roll(both, LANES - GATE_LANES, 1)
            both = jnp.where(lane < here, both, 0.0)
            gg = gg + pltpu.roll(both, lax.rem(scalars[2] + 1 + j, blocks) * here, 1)
        chosen = gates_own * (gg - jnp.sum(gates_own * gg, axis=-1, keepdims=True))
        grad = mm(chosen.astype(BF16), router[...])
        for part in parts:
            grad = grad + part[:, :MODEL_WIDTH].astype(F32)
        scaled = grad * gain[...]
        middle, inv = middle_ref[...], inv_ref[...]
        grad = (
            cot[...].astype(F32)
            + inv * scaled
            - middle * (inv * inv * inv) * jnp.mean(scaled * middle, axis=-1, keepdims=True)
        )
        grad_middle[...] = grad
        branch = grad.astype(BF16)
        branch_ref[...] = branch
        lora = (ADAPTER_SCALE * mm_nt(branch, proj_out[0])).astype(BF16)
        lora_ref[...] = lora
        attended = (mm_nt(branch, proj_w[...]) + mm(lora, proj_in[0])).astype(BF16)
        for i in range(PAIRS):
            grad_att[i] = attended[:, i * PAIR_QUERY : (i + 1) * PAIR_QUERY]

    key_of, value_of = variants(joined(ks), 0), variants(joined(vs), 0)
    queries, grads = lane_tiles(q_ref[...]), lane_tiles(grad_att[step])
    low = low_lanes(queries[0].shape)
    none = jnp.zeros_like(queries[0])
    probs_of, scores_of, query_of, grad_of = [], [], [], []

    def products(h):
        at = (h // 3, h % 2)
        scores = mm_nt(key_of[at], queries[h // 2]) + bias[...]
        return scores, mm_nt(value_of[at], grads[h // 2])

    waiting = [products(h) for h in range(AHEAD)]
    for h in range(6):
        scores, grad_probs = waiting.pop(0)
        if h + AHEAD < 6:
            waiting.append(products(h + AHEAD))
        shifted = jnp.exp(scores - jnp.max(scores, axis=0, keepdims=True))
        probs = shifted * (1.0 / jnp.sum(shifted, axis=0, keepdims=True))
        grad_scores = probs * (grad_probs - jnp.sum(probs * grad_probs, axis=0, keepdims=True))
        probs_of.append(probs.astype(BF16))
        scores_of.append(grad_scores.astype(BF16))
        inside = low if h % 2 == 0 else jnp.logical_not(low)
        query_of.append(jnp.where(inside, queries[h // 2], none))
        grad_of.append(jnp.where(inside, grads[h // 2], none))

    def summed_over(lefts, rights):
        def over(chosen):
            return mm(
                jnp.concatenate([lefts[h] for h in chosen], axis=1),
                jnp.concatenate([rights[h] for h in chosen], axis=0),
            )

        return over([0, 2, 3, 5]) + pltpu.roll(over([1, 4]), HEAD_SIZE, 1)

    grad_key = summed_over(scores_of, query_of)
    grad_key = turned(grad_key, cosine[...], -sine[...]).astype(BF16)
    grad_value = summed_over(probs_of, grad_of).astype(BF16)
    for b, gkv_ref in enumerate(gkv_refs):
        gkv_ref[:, :LANES] = grad_key[b * own : (b + 1) * own]
        gkv_ref[:, LANES:] = grad_value[b * own : (b + 1) * own]
    key_t = {at: key_of[at].astype(F32).T.astype(BF16) for at in key_of}
    cos, sin = cosine[-own:], -sine[-own:]
    for t in range(3):
        pair = (2 * t, 2 * t + 1)
        tile = mm(
            jnp.concatenate([key_t[h // 3, h % 2] for h in pair], axis=1),
            jnp.concatenate([scores_of[h] for h in pair], axis=0),
        )
        gq_ref[:, t * LANES : (t + 1) * LANES] = turned(SCALING * tile.T, cos, sin).astype(BF16)


def middle_backward(
    scalars, parts, here, gates, router, middle, inv, gain, cot, proj_w, proj_in, proj_out,
    q, ks, vs, bias_t, cosine, sine,
):
    own = q.shape[0]
    return call(
        functools.partial(middle_kernel, len(parts), here),
        scalars,
        PAIRS,
        [whole(part) for part in parts]
        + [(k, (own, 2 * LANES), lambda i, s: (0, i)) for k in ks + vs]
        + [
            whole(gates),
            whole(router),
            whole(middle),
            whole(inv),
            whole(gain),
            (cot, (own, MODEL_WIDTH), lambda i, s: (0, 0)),
            whole(proj_w),
            chosen_whole(proj_in),
            chosen_whole(proj_out),
            (q, (own, PAIR_QUERY), lambda i, s: (0, i)),
            whole(bias_t),
            whole(cosine),
            whole(sine),
        ],
        [
            whole_out((own, MODEL_WIDTH), F32),
            whole_out((own, MODEL_WIDTH), BF16),
            whole_out((own, ADAPTER_RANK), BF16),
            ((own, QUERY_FEATURES), BF16, (own, PAIR_QUERY), lambda i, s: (0, i)),
        ]
        + [
            ((own, 2 * KEY_FEATURES), BF16, (own, 2 * LANES), lambda i, s: (0, i))
            for _ in parts
        ],
        [pltpu.VMEM((PAIRS, own, PAIR_QUERY), BF16)],
        flops=20_000_000_000,
    )


def key_and_value(columns):
    return jnp.concatenate(columns[0::2], axis=1), jnp.concatenate(columns[1::2], axis=1)


def package_sizes(parts, blocks):
    width = (MODEL_WIDTH + KEY_FEATURES) // parts
    tiles = -(-width // LANES)
    return width, tiles, parts * tiles + blocks + 1


def partial_kernel(parts, blocks, scalars, *refs):
    gkvs, lora_in = refs[:blocks], refs[blocks : 2 * blocks]
    gq, query_out, kv_out, lora_out, branch, grad_lora, package = refs[2 * blocks :]
    own = gq.shape[0]
    r = ADAPTER_RANK
    width, tiles, entries = package_sizes(parts, blocks)
    low2 = joined(lora_in) * ADAPTER_SCALE
    gk, gv = key_and_value(lane_tiles(joined(gkvs)))
    wide = jnp.concatenate(
        [mm_tn(low2[-own:, :r], gq[...]), mm_tn(lora_out[...] * ADAPTER_SCALE, branch[...])], axis=0
    ).astype(BF16)
    narrow = jnp.concatenate(
        [mm_tn(low2[:, r : 2 * r], gk), mm_tn(low2[:, 2 * r :], gv)], axis=0
    ).astype(BF16)
    w, v = MODEL_WIDTH // parts, KEY_FEATURES // parts
    for p in range(parts):
        block = [wide[:, p * w : (p + 1) * w], narrow[:, p * v : (p + 1) * v]]
        if width < tiles * LANES:
            block.append(jnp.zeros((2 * r, tiles * LANES - width), BF16))
        for t, tile in enumerate(lane_tiles(jnp.concatenate(block, axis=1))):
            package[p * tiles + t] = tile
    grad_kv = jnp.concatenate([mm_nt(kv_out[0, 0], gk), mm_nt(kv_out[0, 1], gv)], axis=0)
    grad_kv = (ADAPTER_SCALE * grad_kv).astype(BF16)
    for j in range(blocks):
        at = parts * tiles + lax.rem(scalars[2] + 2 * blocks - 1 - j, blocks)
        package[at] = grad_kv[:, j * own : (j + 1) * own]
    grad_q = (ADAPTER_SCALE * mm_nt(query_out[0], gq[...])).astype(BF16)
    grad_out = grad_lora[...].astype(F32).T.astype(BF16)
    package[entries - 1] = jnp.concatenate([grad_q, grad_out], axis=0)


def partials(scalars, parts, gkvs, lora_in, gq, query_out, kv_out, lora_out, branch, grad_lora):
    blocks = len(gkvs)
    entries = package_sizes(parts, blocks)[2]
    return call(
        functools.partial(partial_kernel, parts, blocks),
        scalars,
        1,
        [whole(g) for g in list(gkvs) + lora_in]
        + [
            whole(gq),
            chosen_whole(query_out),
            chosen_whole(kv_out),
            whole(lora_out),
            whole(branch),
            whole(grad_lora),
        ],
        [whole_out((entries, 2 * ADAPTER_RANK, LANES), BF16)],
        [],
    )[0]


def sequence_kernel(parts, blocks, scalars, *refs):
    packages, normed = refs[:blocks], refs[blocks : 2 * blocks]
    attended, send, total = refs[2 * blocks :]
    r = ADAPTER_RANK
    width, tiles, entries = package_sizes(parts, blocks)
    total[...] = functools.reduce(lambda a, b: a + b, [p[...].astype(F32) for p in packages])
    ends = [p[entries - 1] for p in packages]
    order = [lax.rem(scalars[2] + 2 * blocks - 1 - j, blocks) for j in range(blocks)]
    grad_kv = [total[parts * tiles + rank].astype(BF16) for rank in order]
    grad_in = jnp.concatenate(
        [jnp.concatenate([end[:r] for end in ends], axis=1), jnp.concatenate(grad_kv, axis=1)],
        axis=0,
    )
    grad_out = jnp.concatenate([end[r:] for end in ends], axis=1)
    wide = jnp.concatenate(
        [mm(grad_in, joined(normed)), mm(grad_out, attended[...])], axis=0
    ).astype(BF16)
    w = MODEL_WIDTH // parts
    for p in range(parts):
        block = jnp.concatenate([total[p * tiles + t] for t in range(tiles)], axis=1).astype(BF16)
        send[p, : 4 * r, :w] = wide[:, p * w : (p + 1) * w]
        send[p, 4 * r :, :w] = block[:, :w]
        send[p, : 2 * r, w:] = block[:, w:width]
        send[p, 2 * r :, w:] = jnp.zeros((4 * r, width - w), BF16)


def sequence_sums(scalars, parts, packages, normed, attended):
    blocks = len(packages)
    width, _, entries = package_sizes(parts, blocks)
    return call(
        functools.partial(sequence_kernel, parts, blocks),
        scalars,
        1,
        [whole(p) for p in packages + normed] + [whole(attended)],
        [whole_out((parts, 6 * ADAPTER_RANK, width), BF16)],
        [pltpu.VMEM((entries, 2 * ADAPTER_RANK, LANES), F32)],
    )[0]


def summed(received, choices, adapter, senders):
    total = None
    for n in range(senders):
        rows = jnp.where(choices[n, :1, :1].astype(F32) == adapter, received(n), 0.0)
        total = rows if total is None else total + rows
    return total


def expert_sum_kernel(wide, scalars, got, choices, up_in, up_out, down_in, down_out):
    adapter = pl.program_id(0).astype(F32)
    total = summed(lambda n: got[n].astype(F32), choices, adapter, got.shape[0])
    r = ADAPTER_RANK
    here = up_in.shape[1]
    for e in range(here):
        up_in[0, e] = total[e * 2 * r : (e + 1) * 2 * r, :wide]
        down_out[0, e] = total[(2 * here + e) * r : (2 * here + e + 1) * r, :wide]
        rows = total[e * 3 * r : (e + 1) * 3 * r]
        up_out[0, e, 0] = rows[:r, wide:]
        up_out[0, e, 1] = rows[r : 2 * r, wide:]
        down_in[0, e] = rows[2 * r :, wide:]


def expert_sum(scalars, got, here):
    parts, _, width = got.shape
    r = ADAPTER_RANK
    rows = here * 3 * r
    wide, narrow = MODEL_WIDTH // parts, EXPERT_HIDDEN // parts

    def out(*shape):
        return ((ADAPTER_CHOICES,) + shape, F32, (1,) + shape, lambda i, s: (i,) + (0,) * len(shape))

    return call(
        functools.partial(expert_sum_kernel, wide),
        scalars,
        ADAPTER_CHOICES,
        [
            (got, (parts, rows, width), lambda i, s: (0, 0, 0)),
            (got, (parts, 16, width), lambda i, s: (0, rows // 16, 0)),
        ],
        [
            out(here, 2 * r, wide),
            out(here, 2, r, narrow),
            out(here, r, narrow),
            out(here, r, wide),
        ],
        [],
    )


def attention_sum_kernel(wide, scalars, got, choices, qkv_in, query_out, kv_out, proj_in, proj_out):
    adapter = pl.program_id(0).astype(F32)
    total = summed(lambda n: got[n].astype(F32), choices, adapter, got.shape[0])
    r = ADAPTER_RANK
    qkv_in[0] = total[: 3 * r, :wide]
    proj_in[0] = total[3 * r : 4 * r, :wide]
    query_out[0] = total[4 * r : 5 * r, :wide]
    proj_out[0] = total[5 * r :, :wide]
    kv_out[0, 0] = total[:r, wide:]
    kv_out[0, 1] = total[r : 2 * r, wide:]


def attention_sum(scalars, got, expert_got, rows):
    parts, _, width = got.shape
    r = ADAPTER_RANK
    wide, narrow = MODEL_WIDTH // parts, KEY_FEATURES // parts

    def out(*shape):
        return ((ADAPTER_CHOICES,) + shape, F32, (1,) + shape, lambda i, s: (i,) + (0,) * len(shape))

    return call(
        functools.partial(attention_sum_kernel, wide),
        scalars,
        ADAPTER_CHOICES,
        [whole(got), (expert_got, (parts, 16, width), lambda i, s: (0, rows // 16, 0))],
        [
            out(3 * r, wide),
            out(r, wide),
            out(2, r, narrow),
            out(r, wide),
            out(r, wide),
        ],
        [],
    )


def query_kernel(scalars, gq, query_w, out_ref):
    out_ref[...] = mm_nt(gq[...], query_w[...])


def query_backward(scalars, gq, query_w):
    steps = 3
    return call(
        query_kernel,
        scalars,
        steps,
        [whole(gq), (query_w, (MODEL_WIDTH // steps, QUERY_FEATURES), lambda i, s: (i, 0))],
        [(gq.shape, F32, (gq.shape[0], MODEL_WIDTH // steps), lambda i, s: (0, i))],
        [],
    )[0]


def input_kernel(blocks, scalars, *refs):
    gkvs, refs = refs[:blocks], refs[blocks:]
    gq, first, kv_w, query_out, kv_out, down, x_ref, gain, grad_middle, out_ref = refs
    grad_kv = functools.reduce(lambda a, b: a + b, [g[...].astype(F32) for g in gkvs])
    grad_k, grad_v = key_and_value(lane_tiles(grad_kv.astype(BF16)))
    lora = jnp.concatenate(
        [
            mm_nt(gq[...], query_out[0]),
            mm_nt(grad_k, kv_out[0, 0]),
            mm_nt(grad_v, kv_out[0, 1]),
        ],
        axis=1,
    )
    lora = (ADAPTER_SCALE * lora).astype(BF16)
    grad = (
        first[...]
        + mm_nt(grad_k, kv_w[:, :KEY_FEATURES])
        + mm_nt(grad_v, kv_w[:, KEY_FEATURES:])
        + mm(lora, down[0])
    )
    x = x_ref[...].astype(F32)
    inv = lax.rsqrt(jnp.mean(x * x, axis=-1, keepdims=True) + EPS)
    scaled = grad * gain[...]
    out_ref[...] = (
        grad_middle[...]
        + inv * scaled
        - x * (inv * inv * inv) * jnp.mean(scaled * x, axis=-1, keepdims=True)
    )


def input_backward(scalars, gkvs, gq, first, kv_w, query_out, kv_out, down, x, gain, grad_middle):
    own = x.shape[0]
    return call(
        functools.partial(input_kernel, len(gkvs)),
        scalars,
        1,
        [whole(g) for g in gkvs]
        + [
            whole(gq),
            whole(first),
            whole(kv_w),
            chosen_whole(query_out),
            chosen_whole(kv_out),
            chosen_whole(down),
            whole(x),
            whole(gain),
            whole(grad_middle),
        ],
        [whole_out((own, MODEL_WIDTH), F32)],
        [],
        flops=20_000_000_000,
    )[0]


def shards(
    layer_input_rows,
    routes,
    prefix,
    sequence_adapter_index,
    attention_norm_gain,
    expert_norm_gain,
    query_weight,
    key_value_weight,
    projection_weight,
    router_weight,
    gate_up_weight,
    down_weight,
    adapter_query_key_value_input,
    adapter_query_output,
    adapter_key_value_output,
    adapter_projection_input,
    adapter_projection_output,
    adapter_gate_up_input,
    adapter_gate_up_output,
    adapter_down_input,
    adapter_down_output,
    cotangent,
):
    ctx_size = lax.axis_size("ctx")
    dp_size = lax.axis_size("dp")
    rank = lax.axis_index("ctx")
    own = layer_input_rows.shape[1]
    span = own * ctx_size
    experts_here = gate_up_weight.shape[0]
    experts_all = experts_here * ctx_size
    half = ctx_size // 2
    scalars = jnp.stack([sequence_adapter_index[0], prefix[0], rank]).astype(jnp.int32)
    gain_attn = attention_norm_gain[None]
    gain_ffn = expert_norm_gain[None]

    order = (rank - 1 - jnp.arange(ctx_size, dtype=jnp.int32)) % ctx_size
    positions = (order[:, None] * own + jnp.arange(own, dtype=jnp.int32)[None, :]).reshape(-1)
    size = HEAD_SIZE // 2
    frequency = ROPE_BASE ** (-jnp.arange(size, dtype=F32) / size)
    angles = positions.astype(F32)[:, None] * frequency[None, :]
    cosine, sine = jnp.cos(angles), jnp.sin(angles)
    cosine = jnp.concatenate([cosine] * 4, axis=1)
    sine = jnp.concatenate([-sine, sine] * 2, axis=1)
    allowed = (positions[None, :] <= positions[:, None]) | (positions[None, :] < prefix[0])
    bias = jnp.where(allowed, 0.0, MASKED).astype(F32)
    bias_t = bias[-own:].T
    qkv_in_t = adapter_query_key_value_input.transpose(0, 2, 1)
    proj_in_t = adapter_projection_input.transpose(0, 2, 1)
    router_t = jnp.pad(router_weight.T, ((0, LANES - experts_all), (0, 0)))

    expert_ids = jnp.arange(LANES, dtype=jnp.int32)
    named = jnp.any(routes[0][:, :, None] == expert_ids[None, None, :], axis=1).astype(BF16)
    cot_own = jnp.concatenate([cotangent[0], named], axis=1)
    x_own = layer_input_rows[0]
    step = functools.partial(lax.ppermute, axis_name="ctx", perm=rotation(ctx_size, 1))
    inputs = [step(x_own)]
    inputs.append(step(after(inputs[0], cosine, sine, bias, bias_t, router_t, scalars, cot_own)))
    while len(inputs) < ctx_size - 1:
        inputs.append(step(inputs[-1]))
    inputs.append(x_own)
    cots = None
    q, k, v, normed, lora_in = [], [], [], [], []
    now = scalars
    for some in ([ctx_size - 1] + list(range(ctx_size - 2)), [ctx_size - 2]):
        made = qkv(
            now, [inputs[b] for b in some], gain_attn, qkv_in_t, query_weight, key_value_weight,
            adapter_query_output, adapter_key_value_output, cosine, sine, some,
        )
        for all_of, some_of in zip((q, k, v, normed, lora_in), made):
            all_of += some_of
        now = after(scalars, q[0])
        if cots is None:
            cots = rotations(after(cot_own, q[0]), ctx_size)
    q, k, v, normed, lora_in = [a[1:] + a[:1] for a in (q, k, v, normed, lora_in)]
    tables = (
        gate_up_weight,
        down_weight,
        adapter_gate_up_input.transpose(0, 1, 3, 2),
        adapter_gate_up_output,
        adapter_down_input.transpose(0, 1, 3, 2),
        adapter_down_output,
    )

    normed_first, normed_last, attended, lora_out, middle, inv = attend(
        scalars, inputs, q, k, v, bias, projection_weight, proj_in_t, adapter_projection_output,
        gain_ffn,
    )
    *rows_first, wide, narrow = experts(
        scalars, dp_size, cots[:half], normed_first, router_t, tables, None
    )
    *rows_last, send, gates = experts(
        scalars, dp_size, cots[half:], normed_last, router_t, tables, (wide, narrow)
    )

    got = send_back(rows_first, ctx_size, 0)
    rows_last[0] = after(rows_last[0], *got)
    got += send_back(rows_last[:-1], ctx_size, half) + rows_last[-1:]
    grad_middle, branch, grad_lora, gq, *gkvs = middle_backward(
        scalars, got, experts_here, gates, router_t, middle, inv, gain_ffn, cot_own,
        projection_weight, proj_in_t, adapter_projection_output, q[-1], k, v, bias_t, cosine, sine,
    )
    expert_got = lax.all_to_all(send, "dp", 0, 0, tiled=True)
    package = partials(
        scalars, dp_size, gkvs, lora_in, after(gq, expert_got), adapter_query_output, adapter_key_value_output,
        lora_out, branch, grad_lora,
    )
    gkvs = list(gkvs)
    gkvs[0] = send_back(gkvs[:1], ctx_size, 0)[0]
    packages = rotations(after(package, gkvs[0]), ctx_size)
    first = query_backward(scalars, after(gq, package), query_weight)
    up_in, up_out, down_in, down_out = expert_sum(
        scalars, after(expert_got, first), experts_here
    )
    later = [after(g, first, up_in, *packages[:-1]) for g in gkvs[1:-1]]
    gkvs[1:-1] = send_back(later, ctx_size, 1)
    packages[1] = after(packages[1], first, up_in)
    attention_send = sequence_sums(scalars, dp_size, packages, normed, attended)
    attention_got = lax.all_to_all(attention_send, "dp", 0, 0, tiled=True)
    grad_inputs = input_backward(
        scalars, gkvs, after(gq, attention_send), first, key_value_weight, adapter_query_output,
        adapter_key_value_output, qkv_in_t, x_own, gain_attn, grad_middle,
    )
    attention_got = after(attention_got, grad_inputs)
    qkv_in, query_out, kv_out, proj_in, proj_out = attention_sum(
        scalars, attention_got, expert_got, experts_here * 3 * ADAPTER_RANK
    )
    return (
        grad_inputs[None],
        qkv_in.transpose(0, 2, 1),
        query_out,
        kv_out,
        proj_in.transpose(0, 2, 1),
        proj_out,
        up_in.transpose(0, 1, 3, 2),
        up_out,
        down_in.transpose(0, 1, 3, 2),
        down_out,
    )


def solution(mesh):
    placed = (
        P("dp", "ctx", None),
        P("dp", "ctx", None),
        P("dp"),
        P("dp"),
        P(),
        P(),
        P(),
        P(),
        P(),
        P(),
        P("ctx", None, None),
        P("ctx", None, None),
        P(),
        P(),
        P(),
        P(),
        P(),
        P(None, "ctx", None, None),
        P(None, "ctx", None, None, None),
        P(None, "ctx", None, None),
        P(None, "ctx", None, None),
        P("dp", "ctx", None),
    )
    return jax.shard_map(
        shards,
        mesh=mesh,
        in_specs=placed,
        out_specs=(
            P("dp", "ctx", None),
            P(None, "dp", None),
            P(None, None, "dp"),
            P(None, None, None, "dp"),
            P(None, "dp", None),
            P(None, None, "dp"),
            P(None, "ctx", "dp", None),
            P(None, "ctx", None, None, "dp"),
            P(None, "ctx", "dp", None),
            P(None, "ctx", None, "dp"),
        ),
        check_vma=False,
    )
```

```python
import functools

import jax
import jax.numpy as jnp
from jax import lax
from jax.experimental import pallas as pl
from jax.experimental.pallas import tpu as pltpu
from jax.sharding import PartitionSpec as P

MODEL_WIDTH = 1536
QUERY_HEADS = 24
KEY_HEADS = 8
HEAD_SIZE = 64
EXPERT_HIDDEN = 512
TOPK = 8
ADAPTER_RANK = 16
ADAPTER_CHOICES = 8
QUERY_FEATURES = 1536
KEY_FEATURES = 512
LANES = 128
PAIRS = KEY_HEADS // 2
PAIR_QUERY = QUERY_FEATURES // PAIRS
GATE_LANES = 8
SENT = MODEL_WIDTH + LANES
AHEAD = 2
COLUMNS = 512

EPS = 1e-05
ADAPTER_SCALE = 2.0
ROPE_BASE = 10000.0
MASKED = -1e30
SCALING = HEAD_SIZE ** (-0.5)
F32 = jnp.float32
BF16 = jnp.bfloat16
MIB = 1024 * 1024


def mm(left, right):
    return jnp.dot(left, right, preferred_element_type=F32)


def mm_nt(left, right):
    return lax.dot_general(left, right, (((1,), (1,)), ((), ())), preferred_element_type=F32)


def mm_tn(left, right):
    return lax.dot_general(left, right, (((0,), (0,)), ((), ())), preferred_element_type=F32)


def rotation(size, by):
    return [(i, (i + by) % size) for i in range(size)]


def after(value, *others):
    return lax.optimization_barrier((value, *others))[0]


def rotations(block, size):
    return [lax.ppermute(block, "ctx", rotation(size, j)) for j in range(1, size)] + [block]


def send_back(blocks, size, first):
    return [
        lax.ppermute(b, "ctx", rotation(size, -1 - j)) for j, b in enumerate(blocks, first)
    ]


def low_lanes(shape):
    return lax.broadcasted_iota(jnp.int32, shape, 1) % LANES < HEAD_SIZE


def turned(tile, cosine, sine):
    half = HEAD_SIZE // 2
    lane = lax.broadcasted_iota(jnp.int32, tile.shape, 1)
    other = jnp.where(
        lane % HEAD_SIZE < half, pltpu.roll(tile, LANES - half, 1), pltpu.roll(tile, half, 1)
    )
    return tile * cosine + other * sine


def variants(block, filler):
    tile, exchanged = lane_tiles(block)
    low = low_lanes(tile.shape)
    fill = jnp.full_like(tile, filler)
    return {
        (0, 0): jnp.where(low, tile, fill),
        (0, 1): jnp.where(low, fill, exchanged),
        (1, 0): jnp.where(low, exchanged, fill),
        (1, 1): jnp.where(low, fill, tile),
    }


def joined(refs):
    return jnp.concatenate([ref[...] for ref in refs], axis=0)


def lane_tiles(block):
    return [block[:, t * LANES : (t + 1) * LANES] for t in range(block.shape[1] // LANES)]


def call(kernel, scalars, grid, ins, outs, scratch, vmem=62, flops=0):
    return list(pl.pallas_call(
        kernel,
        grid_spec=pltpu.PrefetchScalarGridSpec(
            num_scalar_prefetch=1,
            grid=(grid,),
            in_specs=[pl.BlockSpec(b, m) for _, b, m in ins],
            out_specs=[pl.BlockSpec(b, m) for _, _, b, m in outs],
            scratch_shapes=scratch,
        ),
        out_shape=[jax.ShapeDtypeStruct(s, d) for s, d, _, _ in outs],
        compiler_params=pltpu.CompilerParams(
            vmem_limit_bytes=vmem * MIB, dimension_semantics=("arbitrary",)
        ),
        cost_estimate=pl.CostEstimate(
            flops=flops, bytes_accessed=0, transcendentals=0
        ),
    )(scalars, *[a for a, _, _ in ins]))


def whole(array):
    return (array, array.shape, lambda i, s, n=array.ndim: (0,) * n)


def whole_out(shape, dtype):
    return (shape, dtype, shape, lambda i, s, n=len(shape): (0,) * n)


def chosen_whole(table):
    rest = table.shape[1:]
    return (table, (1,) + rest, lambda i, s, n=len(rest): (s[0],) + (0,) * n)


def qkv_kernel(blocks, scalars, *refs):
    xs, refs = refs[:blocks], refs[blocks:]
    gain, down, query_w, kv_w, query_out, kv_out = refs[:6]
    cosines, sines, refs = refs[6 : 6 + blocks], refs[6 + blocks : 6 + 2 * blocks], refs[6 + 2 * blocks :]
    q_refs, k_refs, v_refs, normed_refs, lora_refs = [
        refs[n * blocks : (n + 1) * blocks] for n in range(5)
    ]
    normed, lora = refs[5 * blocks :]
    step = pl.program_id(0)
    q_steps = QUERY_FEATURES // COLUMNS
    own = xs[0].shape[0]
    r = ADAPTER_RANK

    @pl.when(step == 0)
    def _():
        for b, x_ref in enumerate(xs):
            x = x_ref[...].astype(F32)
            inv = lax.rsqrt(jnp.mean(x * x, axis=-1, keepdims=True) + EPS)
            rows = (x * inv * gain[...]).astype(BF16)
            normed[b * own : (b + 1) * own] = rows
            normed_refs[b][...] = rows
        lora[...] = mm_nt(normed[...], down[0]).astype(BF16)
        for b, lora_ref in enumerate(lora_refs):
            lora_ref[...] = lora[b * own : (b + 1) * own]

    def with_exchanged(out_ref, t, tile):
        out_ref[:, 2 * t * LANES : (2 * t + 1) * LANES] = tile.astype(BF16)
        out_ref[:, (2 * t + 1) * LANES : (2 * t + 2) * LANES] = pltpu.roll(
            tile, HEAD_SIZE, 1
        ).astype(BF16)

    @pl.when(step < q_steps)
    def _():
        pre = mm(normed[...], query_w[...])
        pre = pre + mm(lora[:, :r] * ADAPTER_SCALE, query_out[0])
        for b, q_ref in enumerate(q_refs):
            cos, sin = cosines[b][...] * SCALING, sines[b][...] * SCALING
            for t, tile in enumerate(lane_tiles(pre[b * own : (b + 1) * own])):
                q_ref[:, t * LANES : (t + 1) * LANES] = turned(tile, cos, sin).astype(BF16)

    @pl.when(step == q_steps)
    def _():
        pre = mm(normed[...], kv_w[...])
        pre = pre + mm(lora[:, r : 2 * r] * ADAPTER_SCALE, kv_out[0, 0])
        for b, k_ref in enumerate(k_refs):
            cos, sin = cosines[b][...], sines[b][...]
            for t, tile in enumerate(lane_tiles(pre[b * own : (b + 1) * own])):
                with_exchanged(k_ref, t, turned(tile, cos, sin))

    @pl.when(step == q_steps + 1)
    def _():
        pre = mm(normed[...], kv_w[...])
        pre = pre + mm(lora[:, 2 * r :] * ADAPTER_SCALE, kv_out[0, 1])
        for b, v_ref in enumerate(v_refs):
            for t, tile in enumerate(lane_tiles(pre[b * own : (b + 1) * own])):
                with_exchanged(v_ref, t, tile)


def qkv(scalars, xs, gain, down, query_w, kv_w, query_out, kv_out, cosine, sine, places):
    own = xs[0].shape[0]
    blocks = len(xs)
    q_steps = QUERY_FEATURES // COLUMNS
    last = q_steps - 1
    outs = call(
        functools.partial(qkv_kernel, blocks),
        scalars,
        q_steps + 2,
        [whole(x) for x in xs]
        + [
            whole(gain),
            chosen_whole(down),
            (query_w, (MODEL_WIDTH, COLUMNS), lambda i, s: (0, jnp.minimum(i, last))),
            (kv_w, (MODEL_WIDTH, COLUMNS), lambda i, s: (0, jnp.maximum(i - q_steps, 0))),
            (query_out, (1, ADAPTER_RANK, COLUMNS), lambda i, s: (s[0], 0, jnp.minimum(i, last))),
            chosen_whole(kv_out),
        ]
        + [
            (table, (own, LANES), lambda i, s, b=b: (b, 0))
            for table in (cosine, sine)
            for b in places
        ],
        [
            ((own, QUERY_FEATURES), BF16, (own, COLUMNS), lambda i, s: (0, jnp.minimum(i, last)))
            for _ in xs
        ]
        + [whole_out((own, 2 * KEY_FEATURES), BF16) for _ in xs + xs]
        + [whole_out((own, MODEL_WIDTH), BF16) for _ in xs]
        + [whole_out((own, 3 * ADAPTER_RANK), BF16) for _ in xs],
        [
            pltpu.VMEM((own * blocks, MODEL_WIDTH), BF16),
            pltpu.VMEM((own * blocks, 3 * ADAPTER_RANK), BF16),
        ],
        flops=10_000_000_000,
    )
    return [outs[n * blocks : (n + 1) * blocks] for n in range(5)]


def attend_kernel(blocks, scalars, *refs):
    xs, qs, ks, vs = [refs[n * blocks : (n + 1) * blocks] for n in range(4)]
    bias, proj_w, proj_in, proj_out, gain = refs[4 * blocks : 4 * blocks + 5]
    refs = refs[4 * blocks + 5 :]
    normed_refs, att_ref, lora_ref, middle_ref, inv_ref, total, rank_total = (
        refs[:2],
        *refs[2:],
    )
    step = pl.program_id(0)
    own = xs[0].shape[0]
    key_of, value_of = variants(joined(ks), 0), variants(joined(vs), 1)
    tiles = [lane_tiles(joined(qs[2 * n : 2 * n + 2])) for n in range(blocks // 2)]

    def scores_of(n, h):
        rows = slice(2 * n * own, (2 * n + 2) * own)
        return mm_nt(tiles[n][h // 2], key_of[h // 3, h % 2]) + bias[rows]

    todo = [(n, h) for n in range(blocks // 2) for h in range(6)]
    waiting = [scores_of(*item) for item in todo[:AHEAD]]
    heads = []
    for i, (n, h) in enumerate(todo):
        scores = waiting.pop(0)
        if i + AHEAD < len(todo):
            waiting.append(scores_of(*todo[i + AHEAD]))
        shifted = jnp.exp(scores - jnp.max(scores, axis=-1, keepdims=True)).astype(BF16)
        sums = mm(shifted, value_of[h // 3, h % 2])
        heads.append(sums / pltpu.roll(sums, HEAD_SIZE, 1))
    low = low_lanes(heads[0].shape)
    parts = []
    for n in range(blocks // 2):
        some = heads[6 * n : 6 * n + 6]
        pairs = [jnp.where(low, some[2 * t], some[2 * t + 1]) for t in range(3)]
        parts.append(jnp.concatenate(pairs, axis=1).astype(BF16))
    attended = jnp.concatenate(parts, axis=0)
    att_ref[...] = attended
    part = mm(attended, proj_w[...])
    rank_part = mm_nt(attended, proj_in[0])

    @pl.when(step == 0)
    def _():
        total[...] = part
        rank_total[...] = rank_part

    @pl.when(step > 0)
    def _():
        total[...] += part
        rank_total[...] += rank_part

    @pl.when(step == PAIRS - 1)
    def _():
        lora_out = rank_total[...].astype(BF16)
        branch = total[...] + mm(lora_out * ADAPTER_SCALE, proj_out[0])
        for b, x_ref in enumerate(xs):
            middle = x_ref[...].astype(F32) + branch[b * own : (b + 1) * own]
            inv = lax.rsqrt(jnp.mean(middle * middle, axis=-1, keepdims=True) + EPS)
            at = b % (blocks // 2)
            normed_refs[b // (blocks // 2)][at * own : (at + 1) * own] = (
                middle * inv * gain[...]
            ).astype(BF16)
            if b == blocks - 1:
                middle_ref[...] = middle
                inv_ref[...] = inv
                lora_ref[...] = lora_out[b * own : (b + 1) * own]


def attend(scalars, xs, qs, ks, vs, bias, proj_w, proj_in, proj_out, gain):
    own = xs[0].shape[0]
    rows = own * len(xs)
    return call(
        functools.partial(attend_kernel, len(xs)),
        scalars,
        PAIRS,
        [whole(x) for x in xs]
        + [(q, (own, PAIR_QUERY), lambda i, s: (0, i)) for q in qs]
        + [(k, (own, 2 * LANES), lambda i, s: (0, i)) for k in ks + vs]
        + [
            whole(bias),
            (proj_w, (PAIR_QUERY, MODEL_WIDTH), lambda i, s: (i, 0)),
            (proj_in, (1, ADAPTER_RANK, PAIR_QUERY), lambda i, s: (s[0], 0, i)),
            chosen_whole(proj_out),
            whole(gain),
        ],
        [
            whole_out((rows // 2, MODEL_WIDTH), BF16),
            whole_out((rows // 2, MODEL_WIDTH), BF16),
            ((rows, QUERY_FEATURES), BF16, (rows, PAIR_QUERY), lambda i, s: (0, i)),
            whole_out((own, ADAPTER_RANK), BF16),
            whole_out((own, MODEL_WIDTH), F32),
            whole_out((own, 1), F32),
        ],
        [pltpu.VMEM((rows, MODEL_WIDTH), F32), pltpu.VMEM((rows, ADAPTER_RANK), F32)],
    )


def expert_kernel(blocks, parts, first, scalars, *refs):
    cots, refs = refs[:blocks], refs[blocks:]
    x_ref, router, up_w, down_w, up_in, up_out, down_in, down_out = refs[:8]
    refs = refs[8:]
    if not first:
        (wide_old, narrow_old), refs = refs[:2], refs[2:]
    rows_refs, refs = refs[:blocks], refs[blocks:]
    if first:
        (wide_ref, narrow_ref), refs = refs[:2], refs[2:]
    else:
        (send_ref, gates_ref), refs = refs[:2], refs[2:]
    gates, cot_all, total, gg_all, rank_in_all, cot_mid_all, grad_rank_all, gated_all = refs
    step = pl.program_id(0)
    here = up_in.shape[1]
    own = cots[0].shape[0]
    r = ADAPTER_RANK
    up_in_rows = up_in[0].reshape(here * 2 * r, MODEL_WIDTH)
    x = x_ref[...]

    @pl.when(step == 0)
    def _():
        for b, cot in enumerate(cots):
            cot_all[b * own : (b + 1) * own] = cot[:, :MODEL_WIDTH]
        mask = jnp.concatenate([cot[:, MODEL_WIDTH:] for cot in cots], axis=0).astype(F32) > 0.0
        chosen = jnp.where(mask, mm_nt(x, router[...]), MASKED)
        shifted = jnp.exp(chosen - jnp.max(chosen, axis=-1, keepdims=True))
        shifted = jnp.where(mask, shifted, 0.0)
        gates[...] = shifted / jnp.sum(shifted, axis=-1, keepdims=True)
        if not first:
            gates_ref[...] = gates[-own:]
        gg_all[...] = jnp.zeros_like(gg_all)
        rank_in = mm_nt(x, up_in_rows).astype(BF16) * ADAPTER_SCALE
        down_out_rows = down_out[0].reshape(here * r, MODEL_WIDTH)
        cot_mid = ADAPTER_SCALE * mm_nt(cot_all[...], down_out_rows)
        for e in range(here):
            rank_in_all[e] = rank_in[:, e * 2 * r : (e + 1) * 2 * r]
            cot_mid_all[e] = cot_mid[:, e * r : (e + 1) * r]

    cot = cot_all[...]
    lane = lax.broadcasted_iota(jnp.int32, gates.shape, 1)
    gate_of = jnp.sum(
        jnp.where(lane == scalars[2] * here + step, gates[...], 0.0), axis=1, keepdims=True
    )
    rank_in2 = rank_in_all[step]
    none = jnp.zeros((r, EXPERT_HIDDEN), BF16)
    out_map = jnp.concatenate(
        [
            jnp.concatenate([up_out[0, 0, 0], none], axis=1),
            jnp.concatenate([none, up_out[0, 0, 1]], axis=1),
        ],
        axis=0,
    )
    pre = mm(x, up_w[0]) + mm(rank_in2, out_map)
    gate_pre, up_pre = pre[:, :EXPERT_HIDDEN], pre[:, EXPERT_HIDDEN:]
    cot_hidden = mm_nt(cot, down_w[0])
    sig = 0.5 * jnp.tanh(0.5 * gate_pre) + 0.5
    silu = gate_pre * sig
    hidden_wide = silu * up_pre
    hidden = hidden_wide.astype(BF16)
    rank_mid = mm_nt(hidden, down_in[0, 0]).astype(BF16).astype(F32)
    cot_mid = cot_mid_all[step]
    gate_grad = jnp.sum(hidden.astype(F32) * cot_hidden, axis=1, keepdims=True) + jnp.sum(
        rank_mid * cot_mid, axis=1, keepdims=True
    )
    gg_lane = lax.broadcasted_iota(jnp.int32, gg_all.shape, 1)
    gg_all[...] += jnp.where(gg_lane == step, gate_grad, 0.0)
    grad_rank_mid = (gate_of * cot_mid).astype(BF16)
    grad_hidden = gate_of * cot_hidden + mm(grad_rank_mid, down_in[0, 0])
    grad_gate = (grad_hidden * up_pre * (sig + silu * (1.0 - sig))).astype(BF16)
    grad_up = (grad_hidden * silu).astype(BF16)
    grad_both = jnp.concatenate([grad_gate, grad_up], axis=1)
    grad_rank_all[step] = (ADAPTER_SCALE * mm_nt(grad_both, out_map)).astype(BF16)
    gated_all[step] = (ADAPTER_SCALE * gate_of * rank_mid).astype(BF16)
    part = mm_nt(grad_both, up_w[0])

    @pl.when(step == 0)
    def _():
        total[...] = part

    @pl.when(step > 0)
    def _():
        total[...] += part

    both = mm_tn(
        jnp.concatenate([rank_in2, grad_rank_mid], axis=1),
        jnp.concatenate([grad_both, hidden], axis=1),
    )
    narrow = jnp.concatenate(
        [
            both[i * r : (i + 1) * r, i * EXPERT_HIDDEN : (i + 1) * EXPERT_HIDDEN]
            for i in range(3)
        ],
        axis=0,
    )
    w, v = MODEL_WIDTH // parts, EXPERT_HIDDEN // parts
    if first:
        narrow_ref[0] = narrow
    else:
        narrow = (narrow + narrow_old[0]).astype(BF16)
        at = pl.ds(pl.multiple_of(step * (3 * r), 16), 3 * r)
        for p in range(parts):
            send_ref[p, at, w:] = narrow[:, p * v : (p + 1) * v]

    @pl.when(step == here - 1)
    def _():
        grad_rank = jnp.concatenate([grad_rank_all[e] for e in range(here)], axis=1)
        gated = jnp.concatenate([gated_all[e] for e in range(here)], axis=1)
        rows = total[...] + mm(grad_rank, up_in_rows)
        high = gg_all[...].astype(BF16).astype(F32)
        both = high + pltpu.roll(gg_all[...] - high, GATE_LANES, 1)
        for b, rows_ref in enumerate(rows_refs):
            at = slice(b * own, (b + 1) * own)
            rows_ref[:, :MODEL_WIDTH] = rows[at].astype(BF16)
            rows_ref[:, MODEL_WIDTH:] = both[at].astype(BF16)
        wide = jnp.concatenate([mm_tn(grad_rank, x), mm_tn(gated, cot)], axis=0)
        if first:
            wide_ref[...] = wide
        else:
            wide = (wide + wide_old[...]).astype(BF16)
            rows = here * 3 * r
            chosen = jnp.full((16, w + v), scalars[0], jnp.int32).astype(F32).astype(BF16)
            for p in range(parts):
                send_ref[p, :rows, :w] = wide[:, p * w : (p + 1) * w]
                send_ref[p, rows:] = chosen


def experts(scalars, parts, cots, x, router, tables, before):
    up_w, down_w, up_in, up_out, down_in, down_out = tables
    own = cots[0].shape[0]
    rows = own * len(cots)
    here = up_w.shape[0]
    r = ADAPTER_RANK
    per_expert = lambda i, s: (i, 0, 0)
    ins = [whole(c) for c in cots] + [
        whole(x),
        whole(router),
        (up_w, (1,) + up_w.shape[1:], per_expert),
        (down_w, (1,) + down_w.shape[1:], per_expert),
        chosen_whole(up_in),
        (up_out, (1, 1) + up_out.shape[2:], lambda i, s: (s[0], i, 0, 0, 0)),
        (down_in, (1, 1) + down_in.shape[2:], lambda i, s: (s[0], i, 0, 0)),
        chosen_whole(down_out),
    ]
    outs = [whole_out((own, SENT), BF16) for _ in cots]
    if before is None:
        outs.append(whole_out((here * 3 * r, MODEL_WIDTH), F32))
        outs.append(((here, 3 * r, EXPERT_HIDDEN), F32, (1, 3 * r, EXPERT_HIDDEN), per_expert))
    else:
        wide, narrow = before
        ins += [whole(wide), (narrow, (1,) + narrow.shape[1:], per_expert)]
        width = (MODEL_WIDTH + EXPERT_HIDDEN) // parts
        outs.append(whole_out((parts, here * 3 * r + 16, width), BF16))
        outs.append(whole_out((own, LANES), F32))
    return call(
        functools.partial(expert_kernel, len(cots), parts, before is None),
        scalars,
        here,
        ins,
        outs,
        [
            pltpu.VMEM((rows, LANES), F32),
            pltpu.VMEM((rows, MODEL_WIDTH), BF16),
            pltpu.VMEM((rows, MODEL_WIDTH), F32),
            pltpu.VMEM((rows, LANES), F32),
            pltpu.VMEM((here, rows, 2 * r), BF16),
            pltpu.VMEM((here, rows, r), F32),
            pltpu.VMEM((here, rows, 2 * r), BF16),
            pltpu.VMEM((here, rows, r), BF16),
        ],
    )


def middle_kernel(blocks, here, scalars, *refs):
    parts, ks, vs, refs = refs[:blocks], refs[blocks : 2 * blocks], refs[2 * blocks : 3 * blocks], refs[3 * blocks :]
    gates, router, middle_ref, inv_ref, gain, cot = refs[:6]
    proj_w, proj_in, proj_out, q_ref, bias, cosine, sine = refs[6:13]
    grad_middle, branch_ref, lora_ref, gq_ref = refs[13:17]
    gkv_refs, grad_att = refs[17:-1], refs[-1]
    step = pl.program_id(0)
    own = q_ref.shape[0]

    @pl.when(step == 0)
    def _():
        gates_own = gates[...]
        lane = lax.broadcasted_iota(jnp.int32, gates_own.shape, 1)
        gg = jnp.zeros_like(gates_own)
        for j, part in enumerate(parts):
            both = part[:, MODEL_WIDTH:].astype(F32)
            both = both + pltpu.roll(both, LANES - GATE_LANES, 1)
            both = jnp.where(lane < here, both, 0.0)
            gg = gg + pltpu.roll(both, lax.rem(scalars[2] + 1 + j, blocks) * here, 1)
        chosen = gates_own * (gg - jnp.sum(gates_own * gg, axis=-1, keepdims=True))
        grad = mm(chosen.astype(BF16), router[...])
        for part in parts:
            grad = grad + part[:, :MODEL_WIDTH].astype(F32)
        scaled = grad * gain[...]
        middle, inv = middle_ref[...], inv_ref[...]
        grad = (
            cot[...].astype(F32)
            + inv * scaled
            - middle * (inv * inv * inv) * jnp.mean(scaled * middle, axis=-1, keepdims=True)
        )
        grad_middle[...] = grad
        branch = grad.astype(BF16)
        branch_ref[...] = branch
        lora = (ADAPTER_SCALE * mm_nt(branch, proj_out[0])).astype(BF16)
        lora_ref[...] = lora
        attended = (mm_nt(branch, proj_w[...]) + mm(lora, proj_in[0])).astype(BF16)
        for i in range(PAIRS):
            grad_att[i] = attended[:, i * PAIR_QUERY : (i + 1) * PAIR_QUERY]

    key_of, value_of = variants(joined(ks), 0), variants(joined(vs), 0)
    queries, grads = lane_tiles(q_ref[...]), lane_tiles(grad_att[step])
    low = low_lanes(queries[0].shape)
    none = jnp.zeros_like(queries[0])
    probs_of, scores_of, query_of, grad_of = [], [], [], []

    def products(h):
        at = (h // 3, h % 2)
        scores = mm_nt(key_of[at], queries[h // 2]) + bias[...]
        return scores, mm_nt(value_of[at], grads[h // 2])

    waiting = [products(h) for h in range(AHEAD)]
    for h in range(6):
        scores, grad_probs = waiting.pop(0)
        if h + AHEAD < 6:
            waiting.append(products(h + AHEAD))
        shifted = jnp.exp(scores - jnp.max(scores, axis=0, keepdims=True))
        probs = shifted * (1.0 / jnp.sum(shifted, axis=0, keepdims=True))
        grad_scores = probs * (grad_probs - jnp.sum(probs * grad_probs, axis=0, keepdims=True))
        probs_of.append(probs.astype(BF16))
        scores_of.append(grad_scores.astype(BF16))
        inside = low if h % 2 == 0 else jnp.logical_not(low)
        query_of.append(jnp.where(inside, queries[h // 2], none))
        grad_of.append(jnp.where(inside, grads[h // 2], none))

    def summed_over(lefts, rights):
        def over(chosen):
            return mm(
                jnp.concatenate([lefts[h] for h in chosen], axis=1),
                jnp.concatenate([rights[h] for h in chosen], axis=0),
            )

        return over([0, 2, 3, 5]) + pltpu.roll(over([1, 4]), HEAD_SIZE, 1)

    grad_key = summed_over(scores_of, query_of)
    grad_key = turned(grad_key, cosine[...], -sine[...]).astype(BF16)
    grad_value = summed_over(probs_of, grad_of).astype(BF16)
    for b, gkv_ref in enumerate(gkv_refs):
        gkv_ref[:, :LANES] = grad_key[b * own : (b + 1) * own]
        gkv_ref[:, LANES:] = grad_value[b * own : (b + 1) * own]
    key_t = {at: key_of[at].astype(F32).T.astype(BF16) for at in key_of}
    cos, sin = cosine[-own:], -sine[-own:]
    for t in range(3):
        pair = (2 * t, 2 * t + 1)
        tile = mm(
            jnp.concatenate([key_t[h // 3, h % 2] for h in pair], axis=1),
            jnp.concatenate([scores_of[h] for h in pair], axis=0),
        )
        gq_ref[:, t * LANES : (t + 1) * LANES] = turned(SCALING * tile.T, cos, sin).astype(BF16)


def middle_backward(
    scalars, parts, here, gates, router, middle, inv, gain, cot, proj_w, proj_in, proj_out,
    q, ks, vs, bias_t, cosine, sine,
):
    own = q.shape[0]
    return call(
        functools.partial(middle_kernel, len(parts), here),
        scalars,
        PAIRS,
        [whole(part) for part in parts]
        + [(k, (own, 2 * LANES), lambda i, s: (0, i)) for k in ks + vs]
        + [
            whole(gates),
            whole(router),
            whole(middle),
            whole(inv),
            whole(gain),
            (cot, (own, MODEL_WIDTH), lambda i, s: (0, 0)),
            whole(proj_w),
            chosen_whole(proj_in),
            chosen_whole(proj_out),
            (q, (own, PAIR_QUERY), lambda i, s: (0, i)),
            whole(bias_t),
            whole(cosine),
            whole(sine),
        ],
        [
            whole_out((own, MODEL_WIDTH), F32),
            whole_out((own, MODEL_WIDTH), BF16),
            whole_out((own, ADAPTER_RANK), BF16),
            ((own, QUERY_FEATURES), BF16, (own, PAIR_QUERY), lambda i, s: (0, i)),
        ]
        + [
            ((own, 2 * KEY_FEATURES), BF16, (own, 2 * LANES), lambda i, s: (0, i))
            for _ in parts
        ],
        [pltpu.VMEM((PAIRS, own, PAIR_QUERY), BF16)],
        flops=20_000_000_000,
    )


def key_and_value(columns):
    return jnp.concatenate(columns[0::2], axis=1), jnp.concatenate(columns[1::2], axis=1)


def package_sizes(parts, blocks):
    width = (MODEL_WIDTH + KEY_FEATURES) // parts
    tiles = -(-width // LANES)
    return width, tiles, parts * tiles + blocks + 1


def partial_kernel(parts, blocks, scalars, *refs):
    gkvs, lora_in = refs[:blocks], refs[blocks : 2 * blocks]
    gq, query_out, kv_out, lora_out, branch, grad_lora, package = refs[2 * blocks :]
    own = gq.shape[0]
    r = ADAPTER_RANK
    width, tiles, entries = package_sizes(parts, blocks)
    low2 = joined(lora_in) * ADAPTER_SCALE
    gk, gv = key_and_value(lane_tiles(joined(gkvs)))
    wide = jnp.concatenate(
        [mm_tn(low2[-own:, :r], gq[...]), mm_tn(lora_out[...] * ADAPTER_SCALE, branch[...])], axis=0
    ).astype(BF16)
    narrow = jnp.concatenate(
        [mm_tn(low2[:, r : 2 * r], gk), mm_tn(low2[:, 2 * r :], gv)], axis=0
    ).astype(BF16)
    w, v = MODEL_WIDTH // parts, KEY_FEATURES // parts
    for p in range(parts):
        block = [wide[:, p * w : (p + 1) * w], narrow[:, p * v : (p + 1) * v]]
        if width < tiles * LANES:
            block.append(jnp.zeros((2 * r, tiles * LANES - width), BF16))
        for t, tile in enumerate(lane_tiles(jnp.concatenate(block, axis=1))):
            package[p * tiles + t] = tile
    grad_kv = jnp.concatenate([mm_nt(kv_out[0, 0], gk), mm_nt(kv_out[0, 1], gv)], axis=0)
    grad_kv = (ADAPTER_SCALE * grad_kv).astype(BF16)
    for j in range(blocks):
        at = parts * tiles + lax.rem(scalars[2] + 2 * blocks - 1 - j, blocks)
        package[at] = grad_kv[:, j * own : (j + 1) * own]
    grad_q = (ADAPTER_SCALE * mm_nt(query_out[0], gq[...])).astype(BF16)
    grad_out = grad_lora[...].astype(F32).T.astype(BF16)
    package[entries - 1] = jnp.concatenate([grad_q, grad_out], axis=0)


def partials(scalars, parts, gkvs, lora_in, gq, query_out, kv_out, lora_out, branch, grad_lora):
    blocks = len(gkvs)
    entries = package_sizes(parts, blocks)[2]
    return call(
        functools.partial(partial_kernel, parts, blocks),
        scalars,
        1,
        [whole(g) for g in list(gkvs) + lora_in]
        + [
            whole(gq),
            chosen_whole(query_out),
            chosen_whole(kv_out),
            whole(lora_out),
            whole(branch),
            whole(grad_lora),
        ],
        [whole_out((entries, 2 * ADAPTER_RANK, LANES), BF16)],
        [],
    )[0]


def sequence_kernel(parts, blocks, scalars, *refs):
    packages, normed = refs[:blocks], refs[blocks : 2 * blocks]
    attended, send, total = refs[2 * blocks :]
    r = ADAPTER_RANK
    width, tiles, entries = package_sizes(parts, blocks)
    total[...] = functools.reduce(lambda a, b: a + b, [p[...].astype(F32) for p in packages])
    ends = [p[entries - 1] for p in packages]
    order = [lax.rem(scalars[2] + 2 * blocks - 1 - j, blocks) for j in range(blocks)]
    grad_kv = [total[parts * tiles + rank].astype(BF16) for rank in order]
    grad_in = jnp.concatenate(
        [jnp.concatenate([end[:r] for end in ends], axis=1), jnp.concatenate(grad_kv, axis=1)],
        axis=0,
    )
    grad_out = jnp.concatenate([end[r:] for end in ends], axis=1)
    wide = jnp.concatenate(
        [mm(grad_in, joined(normed)), mm(grad_out, attended[...])], axis=0
    ).astype(BF16)
    w = MODEL_WIDTH // parts
    for p in range(parts):
        block = jnp.concatenate([total[p * tiles + t] for t in range(tiles)], axis=1).astype(BF16)
        send[p, : 4 * r, :w] = wide[:, p * w : (p + 1) * w]
        send[p, 4 * r :, :w] = block[:, :w]
        send[p, : 2 * r, w:] = block[:, w:width]
        send[p, 2 * r :, w:] = jnp.zeros((4 * r, width - w), BF16)


def sequence_sums(scalars, parts, packages, normed, attended):
    blocks = len(packages)
    width, _, entries = package_sizes(parts, blocks)
    return call(
        functools.partial(sequence_kernel, parts, blocks),
        scalars,
        1,
        [whole(p) for p in packages + normed] + [whole(attended)],
        [whole_out((parts, 6 * ADAPTER_RANK, width), BF16)],
        [pltpu.VMEM((entries, 2 * ADAPTER_RANK, LANES), F32)],
    )[0]


def expert_sum_kernel(wide, scalars, got, up_in, up_out, down_in, down_out):
    for out in (up_in, up_out, down_in, down_out):
        out[...] = jnp.zeros_like(out)
    r = ADAPTER_RANK
    here = up_in.shape[1]
    for n in range(got.shape[0]):
        a = scalars[3 + n]
        rows = got[n].astype(F32)
        for e in range(here):
            up_in[a, e] += rows[e * 2 * r : (e + 1) * 2 * r, :wide]
            down_out[a, e] += rows[(2 * here + e) * r : (2 * here + e + 1) * r, :wide]
            at = e * 3 * r
            up_out[a, e, 0] += rows[at : at + r, wide:]
            up_out[a, e, 1] += rows[at + r : at + 2 * r, wide:]
            down_in[a, e] += rows[at + 2 * r : at + 3 * r, wide:]


def expert_sum(scalars, got, here):
    parts = got.shape[0]
    r = ADAPTER_RANK
    wide, narrow = MODEL_WIDTH // parts, EXPERT_HIDDEN // parts

    def out(*shape):
        return whole_out((ADAPTER_CHOICES,) + shape, F32)

    return call(
        functools.partial(expert_sum_kernel, wide),
        scalars,
        1,
        [whole(got)],
        [
            out(here, 2 * r, wide),
            out(here, 2, r, narrow),
            out(here, r, narrow),
            out(here, r, wide),
        ],
        [],
    )


def attention_sum_kernel(wide, scalars, got, qkv_in, query_out, kv_out, proj_in, proj_out):
    for out in (qkv_in, query_out, kv_out, proj_in, proj_out):
        out[...] = jnp.zeros_like(out)
    r = ADAPTER_RANK
    for n in range(got.shape[0]):
        a = scalars[3 + n]
        rows = got[n].astype(F32)
        qkv_in[a] += rows[: 3 * r, :wide]
        proj_in[a] += rows[3 * r : 4 * r, :wide]
        query_out[a] += rows[4 * r : 5 * r, :wide]
        proj_out[a] += rows[5 * r :, :wide]
        kv_out[a, 0] += rows[:r, wide:]
        kv_out[a, 1] += rows[r : 2 * r, wide:]


def attention_sum(scalars, got):
    parts = got.shape[0]
    r = ADAPTER_RANK
    wide, narrow = MODEL_WIDTH // parts, KEY_FEATURES // parts

    def out(*shape):
        return whole_out((ADAPTER_CHOICES,) + shape, F32)

    return call(
        functools.partial(attention_sum_kernel, wide),
        scalars,
        1,
        [whole(got)],
        [
            out(3 * r, wide),
            out(r, wide),
            out(2, r, narrow),
            out(r, wide),
            out(r, wide),
        ],
        [],
    )


def query_kernel(scalars, gq, query_w, out_ref):
    out_ref[...] = mm_nt(gq[...], query_w[...])


def query_backward(scalars, gq, query_w):
    steps = 3
    return call(
        query_kernel,
        scalars,
        steps,
        [whole(gq), (query_w, (MODEL_WIDTH // steps, QUERY_FEATURES), lambda i, s: (i, 0))],
        [(gq.shape, F32, (gq.shape[0], MODEL_WIDTH // steps), lambda i, s: (0, i))],
        [],
    )[0]


def input_kernel(blocks, scalars, *refs):
    gkvs, refs = refs[:blocks], refs[blocks:]
    gq, first, kv_w, query_out, kv_out, down, x_ref, gain, grad_middle, out_ref = refs
    grad_kv = functools.reduce(lambda a, b: a + b, [g[...].astype(F32) for g in gkvs])
    grad_k, grad_v = key_and_value(lane_tiles(grad_kv.astype(BF16)))
    lora = jnp.concatenate(
        [
            mm_nt(gq[...], query_out[0]),
            mm_nt(grad_k, kv_out[0, 0]),
            mm_nt(grad_v, kv_out[0, 1]),
        ],
        axis=1,
    )
    lora = (ADAPTER_SCALE * lora).astype(BF16)
    grad = (
        first[...]
        + mm_nt(grad_k, kv_w[:, :KEY_FEATURES])
        + mm_nt(grad_v, kv_w[:, KEY_FEATURES:])
        + mm(lora, down[0])
    )
    x = x_ref[...].astype(F32)
    inv = lax.rsqrt(jnp.mean(x * x, axis=-1, keepdims=True) + EPS)
    scaled = grad * gain[...]
    out_ref[...] = (
        grad_middle[...]
        + inv * scaled
        - x * (inv * inv * inv) * jnp.mean(scaled * x, axis=-1, keepdims=True)
    )


def input_backward(scalars, gkvs, gq, first, kv_w, query_out, kv_out, down, x, gain, grad_middle):
    own = x.shape[0]
    return call(
        functools.partial(input_kernel, len(gkvs)),
        scalars,
        1,
        [whole(g) for g in gkvs]
        + [
            whole(gq),
            whole(first),
            whole(kv_w),
            chosen_whole(query_out),
            chosen_whole(kv_out),
            chosen_whole(down),
            whole(x),
            whole(gain),
            whole(grad_middle),
        ],
        [whole_out((own, MODEL_WIDTH), F32)],
        [],
        flops=20_000_000_000,
    )[0]


def shards(
    layer_input_rows,
    routes,
    prefix,
    sequence_adapter_index,
    attention_norm_gain,
    expert_norm_gain,
    query_weight,
    key_value_weight,
    projection_weight,
    router_weight,
    gate_up_weight,
    down_weight,
    adapter_query_key_value_input,
    adapter_query_output,
    adapter_key_value_output,
    adapter_projection_input,
    adapter_projection_output,
    adapter_gate_up_input,
    adapter_gate_up_output,
    adapter_down_input,
    adapter_down_output,
    cotangent,
):
    ctx_size = lax.axis_size("ctx")
    dp_size = lax.axis_size("dp")
    rank = lax.axis_index("ctx")
    own = layer_input_rows.shape[1]
    span = own * ctx_size
    experts_here = gate_up_weight.shape[0]
    experts_all = experts_here * ctx_size
    half = ctx_size // 2
    scalars = jnp.concatenate([sequence_adapter_index, prefix, rank[None]])
    gain_attn = attention_norm_gain[None]
    gain_ffn = expert_norm_gain[None]

    order = (rank - 1 - jnp.arange(ctx_size, dtype=jnp.int32)) % ctx_size
    positions = (order[:, None] * own + jnp.arange(own, dtype=jnp.int32)[None, :]).reshape(-1)
    size = HEAD_SIZE // 2
    frequency = ROPE_BASE ** (-jnp.arange(size, dtype=F32) / size)
    angles = positions.astype(F32)[:, None] * frequency[None, :]
    cosine, sine = jnp.cos(angles), jnp.sin(angles)
    cosine = jnp.concatenate([cosine] * 4, axis=1)
    sine = jnp.concatenate([-sine, sine] * 2, axis=1)
    allowed = (positions[None, :] <= positions[:, None]) | (positions[None, :] < prefix[0])
    bias = jnp.where(allowed, 0.0, MASKED).astype(F32)
    bias_t = bias[-own:].T
    qkv_in_t = adapter_query_key_value_input.transpose(0, 2, 1)
    proj_in_t = adapter_projection_input.transpose(0, 2, 1)
    router_t = jnp.pad(router_weight.T, ((0, LANES - experts_all), (0, 0)))

    expert_ids = jnp.arange(LANES, dtype=jnp.int32)
    named = jnp.any(routes[0][:, :, None] == expert_ids[None, None, :], axis=1).astype(BF16)
    cot_own = jnp.concatenate([cotangent[0], named], axis=1)
    x_own = layer_input_rows[0]
    step = functools.partial(lax.ppermute, axis_name="ctx", perm=rotation(ctx_size, 1))
    inputs = [step(x_own)]
    inputs.append(step(after(inputs[0], cosine, sine, bias, bias_t, router_t, scalars, cot_own)))
    while len(inputs) < ctx_size - 1:
        inputs.append(step(inputs[-1]))
    inputs.append(x_own)
    cots = None
    q, k, v, normed, lora_in = [], [], [], [], []
    now = scalars
    for some in ([ctx_size - 1] + list(range(ctx_size - 2)), [ctx_size - 2]):
        made = qkv(
            now, [inputs[b] for b in some], gain_attn, qkv_in_t, query_weight, key_value_weight,
            adapter_query_output, adapter_key_value_output, cosine, sine, some,
        )
        for all_of, some_of in zip((q, k, v, normed, lora_in), made):
            all_of += some_of
        now = after(scalars, q[0])
        if cots is None:
            cots = rotations(after(cot_own, q[0]), ctx_size)
    q, k, v, normed, lora_in = [a[1:] + a[:1] for a in (q, k, v, normed, lora_in)]
    tables = (
        gate_up_weight,
        down_weight,
        adapter_gate_up_input.transpose(0, 1, 3, 2),
        adapter_gate_up_output,
        adapter_down_input.transpose(0, 1, 3, 2),
        adapter_down_output,
    )

    normed_first, normed_last, attended, lora_out, middle, inv = attend(
        scalars, inputs, q, k, v, bias, projection_weight, proj_in_t, adapter_projection_output,
        gain_ffn,
    )
    *rows_first, wide, narrow = experts(
        scalars, dp_size, cots[:half], normed_first, router_t, tables, None
    )
    *rows_last, send, gates = experts(
        scalars, dp_size, cots[half:], normed_last, router_t, tables, (wide, narrow)
    )

    got = send_back(rows_first, ctx_size, 0)
    rows_last[0] = after(rows_last[0], *got)
    got += send_back(rows_last[:-1], ctx_size, half) + rows_last[-1:]
    grad_middle, branch, grad_lora, gq, *gkvs = middle_backward(
        scalars, got, experts_here, gates, router_t, middle, inv, gain_ffn, cot_own,
        projection_weight, proj_in_t, adapter_projection_output, q[-1], k, v, bias_t, cosine, sine,
    )
    expert_got = lax.all_to_all(send, "dp", 0, 0, tiled=True)
    package = partials(
        scalars, dp_size, gkvs, lora_in, after(gq, expert_got), adapter_query_output, adapter_key_value_output,
        lora_out, branch, grad_lora,
    )
    gkvs = list(gkvs)
    gkvs[0] = send_back(gkvs[:1], ctx_size, 0)[0]
    packages = rotations(after(package, gkvs[0]), ctx_size)
    choices = expert_got[:, experts_here * 3 * ADAPTER_RANK, 0].astype(jnp.int32)
    with_choices = jnp.concatenate([scalars, choices])
    first = query_backward(scalars, after(gq, package, gkvs[0], with_choices), query_weight)
    up_in, up_out, down_in, down_out = expert_sum(
        with_choices, after(expert_got, first), experts_here
    )
    later = [after(g, first, up_in, *packages[:-1]) for g in gkvs[1:-1]]
    gkvs[1:-1] = send_back(later, ctx_size, 1)
    packages[1] = after(packages[1], first, up_in)
    attention_send = sequence_sums(scalars, dp_size, packages, normed, attended)
    attention_got = lax.all_to_all(attention_send, "dp", 0, 0, tiled=True)
    grad_inputs = input_backward(
        scalars, gkvs, after(gq, attention_send), first, key_value_weight, adapter_query_output,
        adapter_key_value_output, qkv_in_t, x_own, gain_attn, grad_middle,
    )
    attention_got = after(attention_got, grad_inputs)
    qkv_in, query_out, kv_out, proj_in, proj_out = attention_sum(
        with_choices, attention_got
    )
    return (
        grad_inputs[None],
        qkv_in.transpose(0, 2, 1),
        query_out,
        kv_out,
        proj_in.transpose(0, 2, 1),
        proj_out,
        up_in.transpose(0, 1, 3, 2),
        up_out,
        down_in.transpose(0, 1, 3, 2),
        down_out,
    )


def solution(mesh):
    placed = (
        P("dp", "ctx", None),
        P("dp", "ctx", None),
        P("dp"),
        P("dp"),
        P(),
        P(),
        P(),
        P(),
        P(),
        P(),
        P("ctx", None, None),
        P("ctx", None, None),
        P(),
        P(),
        P(),
        P(),
        P(),
        P(None, "ctx", None, None),
        P(None, "ctx", None, None, None),
        P(None, "ctx", None, None),
        P(None, "ctx", None, None),
        P("dp", "ctx", None),
    )
    return jax.shard_map(
        shards,
        mesh=mesh,
        in_specs=placed,
        out_specs=(
            P("dp", "ctx", None),
            P(None, "dp", None),
            P(None, None, "dp"),
            P(None, None, None, "dp"),
            P(None, "dp", None),
            P(None, None, "dp"),
            P(None, "ctx", "dp", None),
            P(None, "ctx", None, None, "dp"),
            P(None, "ctx", "dp", None),
            P(None, "ctx", None, "dp"),
        ),
        check_vma=False,
    )
```

```python
import functools

import jax
import jax.numpy as jnp
from jax import lax
from jax.experimental import pallas as pl
from jax.experimental.pallas import tpu as pltpu
from jax.sharding import PartitionSpec as P

MODEL_WIDTH = 1536
QUERY_HEADS = 24
KEY_HEADS = 8
HEAD_SIZE = 64
EXPERT_HIDDEN = 512
TOPK = 8
ADAPTER_RANK = 16
ADAPTER_CHOICES = 8
QUERY_FEATURES = 1536
KEY_FEATURES = 512
LANES = 128
PAIRS = KEY_HEADS // 2
PAIR_QUERY = QUERY_FEATURES // PAIRS
GATE_LANES = 8
SENT = MODEL_WIDTH + LANES
AHEAD = 2
COLUMNS = 512

EPS = 1e-05
ADAPTER_SCALE = 2.0
ROPE_BASE = 10000.0
MASKED = -1e30
SCALING = HEAD_SIZE ** (-0.5)
F32 = jnp.float32
BF16 = jnp.bfloat16
MIB = 1024 * 1024


def mm(left, right):
    return jnp.dot(left, right, preferred_element_type=F32)


def mm_nt(left, right):
    return lax.dot_general(left, right, (((1,), (1,)), ((), ())), preferred_element_type=F32)


def mm_tn(left, right):
    return lax.dot_general(left, right, (((0,), (0,)), ((), ())), preferred_element_type=F32)


def rotation(size, by):
    return [(i, (i + by) % size) for i in range(size)]


def after(value, *others):
    return lax.optimization_barrier((value, *others))[0]


def rotations(block, size, count=None, first=1):
    if count is not None:
        return [lax.ppermute(block, "ctx", rotation(size, first + j)) for j in range(count)]
    return [lax.ppermute(block, "ctx", rotation(size, j)) for j in range(1, size)] + [block]


def send_back(blocks, size, first):
    return [
        lax.ppermute(b, "ctx", rotation(size, -1 - j)) for j, b in enumerate(blocks, first)
    ]


def low_lanes(shape):
    return lax.broadcasted_iota(jnp.int32, shape, 1) % LANES < HEAD_SIZE


def turned(tile, cosine, sine):
    half = HEAD_SIZE // 2
    lane = lax.broadcasted_iota(jnp.int32, tile.shape, 1)
    other = jnp.where(
        lane % HEAD_SIZE < half, pltpu.roll(tile, LANES - half, 1), pltpu.roll(tile, half, 1)
    )
    return tile * cosine + other * sine


def variants(block, filler):
    tile, exchanged = lane_tiles(block)
    low = low_lanes(tile.shape)
    fill = jnp.full_like(tile, filler)
    return {
        (0, 0): jnp.where(low, tile, fill),
        (0, 1): jnp.where(low, fill, exchanged),
        (1, 0): jnp.where(low, exchanged, fill),
        (1, 1): jnp.where(low, fill, tile),
    }


def joined(refs):
    return jnp.concatenate([ref[...] for ref in refs], axis=0)


def lane_tiles(block):
    return [block[:, t * LANES : (t + 1) * LANES] for t in range(block.shape[1] // LANES)]


def call(kernel, scalars, grid, ins, outs, scratch, vmem=62, flops=0):
    return list(pl.pallas_call(
        kernel,
        grid_spec=pltpu.PrefetchScalarGridSpec(
            num_scalar_prefetch=1,
            grid=(grid,),
            in_specs=[pl.BlockSpec(b, m) for _, b, m in ins],
            out_specs=[pl.BlockSpec(b, m) for _, _, b, m in outs],
            scratch_shapes=scratch,
        ),
        out_shape=[jax.ShapeDtypeStruct(s, d) for s, d, _, _ in outs],
        compiler_params=pltpu.CompilerParams(
            vmem_limit_bytes=vmem * MIB, dimension_semantics=("arbitrary",)
        ),
        cost_estimate=pl.CostEstimate(
            flops=flops, bytes_accessed=0, transcendentals=0
        ),
    )(scalars, *[a for a, _, _ in ins]))


def whole(array):
    return (array, array.shape, lambda i, s, n=array.ndim: (0,) * n)


def whole_out(shape, dtype):
    return (shape, dtype, shape, lambda i, s, n=len(shape): (0,) * n)


def chosen_whole(table):
    rest = table.shape[1:]
    return (table, (1,) + rest, lambda i, s, n=len(rest): (s[0],) + (0,) * n)


def qkv_kernel(blocks, scalars, *refs):
    xs, refs = refs[:blocks], refs[blocks:]
    gain, down, query_w, kv_w, query_out, kv_out = refs[:6]
    cosines, sines, refs = refs[6 : 6 + blocks], refs[6 + blocks : 6 + 2 * blocks], refs[6 + 2 * blocks :]
    q_refs, k_refs, v_refs, normed_refs, lora_refs = [
        refs[n * blocks : (n + 1) * blocks] for n in range(5)
    ]
    normed, lora = refs[5 * blocks :]
    step = pl.program_id(0)
    q_steps = QUERY_FEATURES // COLUMNS
    own = xs[0].shape[0]
    r = ADAPTER_RANK

    @pl.when(step == 0)
    def _():
        for b, x_ref in enumerate(xs):
            x = x_ref[...].astype(F32)
            inv = lax.rsqrt(jnp.mean(x * x, axis=-1, keepdims=True) + EPS)
            rows = (x * inv * gain[...]).astype(BF16)
            normed[b * own : (b + 1) * own] = rows
            normed_refs[b][...] = rows
        lora[...] = mm_nt(normed[...], down[0]).astype(BF16)
        for b, lora_ref in enumerate(lora_refs):
            lora_ref[...] = lora[b * own : (b + 1) * own]

    def with_exchanged(out_ref, t, tile):
        out_ref[:, 2 * t * LANES : (2 * t + 1) * LANES] = tile.astype(BF16)
        out_ref[:, (2 * t + 1) * LANES : (2 * t + 2) * LANES] = pltpu.roll(
            tile, HEAD_SIZE, 1
        ).astype(BF16)

    @pl.when(step < q_steps)
    def _():
        pre = mm(normed[...], query_w[...])
        pre = pre + mm(lora[:, :r] * ADAPTER_SCALE, query_out[0])
        for b, q_ref in enumerate(q_refs):
            cos, sin = cosines[b][...] * SCALING, sines[b][...] * SCALING
            for t, tile in enumerate(lane_tiles(pre[b * own : (b + 1) * own])):
                q_ref[:, t * LANES : (t + 1) * LANES] = turned(tile, cos, sin).astype(BF16)

    @pl.when(step == q_steps)
    def _():
        pre = mm(normed[...], kv_w[...])
        pre = pre + mm(lora[:, r : 2 * r] * ADAPTER_SCALE, kv_out[0, 0])
        for b, k_ref in enumerate(k_refs):
            cos, sin = cosines[b][...], sines[b][...]
            for t, tile in enumerate(lane_tiles(pre[b * own : (b + 1) * own])):
                with_exchanged(k_ref, t, turned(tile, cos, sin))

    @pl.when(step == q_steps + 1)
    def _():
        pre = mm(normed[...], kv_w[...])
        pre = pre + mm(lora[:, 2 * r :] * ADAPTER_SCALE, kv_out[0, 1])
        for b, v_ref in enumerate(v_refs):
            for t, tile in enumerate(lane_tiles(pre[b * own : (b + 1) * own])):
                with_exchanged(v_ref, t, tile)


def qkv(scalars, xs, gain, down, query_w, kv_w, query_out, kv_out, cosine, sine, places):
    own = xs[0].shape[0]
    blocks = len(xs)
    q_steps = QUERY_FEATURES // COLUMNS
    last = q_steps - 1
    outs = call(
        functools.partial(qkv_kernel, blocks),
        scalars,
        q_steps + 2,
        [whole(x) for x in xs]
        + [
            whole(gain),
            chosen_whole(down),
            (query_w, (MODEL_WIDTH, COLUMNS), lambda i, s: (0, jnp.minimum(i, last))),
            (kv_w, (MODEL_WIDTH, COLUMNS), lambda i, s: (0, jnp.maximum(i - q_steps, 0))),
            (query_out, (1, ADAPTER_RANK, COLUMNS), lambda i, s: (s[0], 0, jnp.minimum(i, last))),
            chosen_whole(kv_out),
        ]
        + [
            (table, (own, LANES), lambda i, s, b=b: (b, 0))
            for table in (cosine, sine)
            for b in places
        ],
        [
            ((own, QUERY_FEATURES), BF16, (own, COLUMNS), lambda i, s: (0, jnp.minimum(i, last)))
            for _ in xs
        ]
        + [whole_out((own, 2 * KEY_FEATURES), BF16) for _ in xs + xs]
        + [whole_out((own, MODEL_WIDTH), BF16) for _ in xs]
        + [whole_out((own, 3 * ADAPTER_RANK), BF16) for _ in xs],
        [
            pltpu.VMEM((own * blocks, MODEL_WIDTH), BF16),
            pltpu.VMEM((own * blocks, 3 * ADAPTER_RANK), BF16),
        ],
        flops=10_000_000_000,
    )
    return [outs[n * blocks : (n + 1) * blocks] for n in range(5)]


def attend_kernel(blocks, scalars, *refs):
    xs, qs, ks, vs = [refs[n * blocks : (n + 1) * blocks] for n in range(4)]
    bias, proj_w, proj_in, proj_out, gain = refs[4 * blocks : 4 * blocks + 5]
    refs = refs[4 * blocks + 5 :]
    normed_refs, att_ref, lora_ref, middle_ref, inv_ref, total, rank_total = (
        refs[:2],
        *refs[2:],
    )
    step = pl.program_id(0)
    own = xs[0].shape[0]
    key_of, value_of = variants(joined(ks), 0), variants(joined(vs), 1)
    tiles = [lane_tiles(joined(qs[2 * n : 2 * n + 2])) for n in range(blocks // 2)]

    def scores_of(n, h):
        rows = slice(2 * n * own, (2 * n + 2) * own)
        return mm_nt(tiles[n][h // 2], key_of[h // 3, h % 2]) + bias[rows]

    todo = [(n, h) for n in range(blocks // 2) for h in range(6)]
    waiting = [scores_of(*item) for item in todo[:AHEAD]]
    heads = []
    for i, (n, h) in enumerate(todo):
        scores = waiting.pop(0)
        if i + AHEAD < len(todo):
            waiting.append(scores_of(*todo[i + AHEAD]))
        shifted = jnp.exp(scores - jnp.max(scores, axis=-1, keepdims=True)).astype(BF16)
        sums = mm(shifted, value_of[h // 3, h % 2])
        heads.append(sums / pltpu.roll(sums, HEAD_SIZE, 1))
    low = low_lanes(heads[0].shape)
    parts = []
    for n in range(blocks // 2):
        some = heads[6 * n : 6 * n + 6]
        pairs = [jnp.where(low, some[2 * t], some[2 * t + 1]) for t in range(3)]
        parts.append(jnp.concatenate(pairs, axis=1).astype(BF16))
    attended = jnp.concatenate(parts, axis=0)
    att_ref[...] = attended
    part = mm(attended, proj_w[...])
    rank_part = mm_nt(attended, proj_in[0])

    @pl.when(step == 0)
    def _():
        total[...] = part
        rank_total[...] = rank_part

    @pl.when(step > 0)
    def _():
        total[...] += part
        rank_total[...] += rank_part

    @pl.when(step == PAIRS - 1)
    def _():
        lora_out = rank_total[...].astype(BF16)
        branch = total[...] + mm(lora_out * ADAPTER_SCALE, proj_out[0])
        for b, x_ref in enumerate(xs):
            middle = x_ref[...].astype(F32) + branch[b * own : (b + 1) * own]
            inv = lax.rsqrt(jnp.mean(middle * middle, axis=-1, keepdims=True) + EPS)
            at = b % (blocks // 2)
            normed_refs[b // (blocks // 2)][at * own : (at + 1) * own] = (
                middle * inv * gain[...]
            ).astype(BF16)
            if b == blocks - 1:
                middle_ref[...] = middle
                inv_ref[...] = inv
                lora_ref[...] = lora_out[b * own : (b + 1) * own]


def attend(scalars, xs, qs, ks, vs, bias, proj_w, proj_in, proj_out, gain):
    own = xs[0].shape[0]
    rows = own * len(xs)
    return call(
        functools.partial(attend_kernel, len(xs)),
        scalars,
        PAIRS,
        [whole(x) for x in xs]
        + [(q, (own, PAIR_QUERY), lambda i, s: (0, i)) for q in qs]
        + [(k, (own, 2 * LANES), lambda i, s: (0, i)) for k in ks + vs]
        + [
            whole(bias),
            (proj_w, (PAIR_QUERY, MODEL_WIDTH), lambda i, s: (i, 0)),
            (proj_in, (1, ADAPTER_RANK, PAIR_QUERY), lambda i, s: (s[0], 0, i)),
            chosen_whole(proj_out),
            whole(gain),
        ],
        [
            whole_out((rows // 2, MODEL_WIDTH), BF16),
            whole_out((rows // 2, MODEL_WIDTH), BF16),
            ((rows, QUERY_FEATURES), BF16, (rows, PAIR_QUERY), lambda i, s: (0, i)),
            whole_out((own, ADAPTER_RANK), BF16),
            whole_out((own, MODEL_WIDTH), F32),
            whole_out((own, 1), F32),
        ],
        [pltpu.VMEM((rows, MODEL_WIDTH), F32), pltpu.VMEM((rows, ADAPTER_RANK), F32)],
    )


def expert_kernel(blocks, parts, first, scalars, *refs):
    cots, refs = refs[:blocks], refs[blocks:]
    x_ref, router, up_w, down_w, up_in, up_out, down_in, down_out = refs[:8]
    refs = refs[8:]
    if not first:
        (wide_old, narrow_old), refs = refs[:2], refs[2:]
    rows_refs, refs = refs[:blocks], refs[blocks:]
    if first:
        (wide_ref, narrow_ref), refs = refs[:2], refs[2:]
    else:
        (send_ref, gates_ref), refs = refs[:2], refs[2:]
    gates, cot_all, total, gg_all, rank_in_all, cot_mid_all, grad_rank_all, gated_all = refs
    step = pl.program_id(0)
    here = up_in.shape[1]
    own = cots[0].shape[0]
    r = ADAPTER_RANK
    up_in_rows = up_in[0].reshape(here * 2 * r, MODEL_WIDTH)
    x = x_ref[...]

    @pl.when(step == 0)
    def _():
        for b, cot in enumerate(cots):
            cot_all[b * own : (b + 1) * own] = cot[:, :MODEL_WIDTH]
        mask = jnp.concatenate([cot[:, MODEL_WIDTH:] for cot in cots], axis=0).astype(F32) > 0.0
        chosen = jnp.where(mask, mm_nt(x, router[...]), MASKED)
        shifted = jnp.exp(chosen - jnp.max(chosen, axis=-1, keepdims=True))
        shifted = jnp.where(mask, shifted, 0.0)
        gates[...] = shifted / jnp.sum(shifted, axis=-1, keepdims=True)
        if not first:
            gates_ref[...] = gates[-own:]
        gg_all[...] = jnp.zeros_like(gg_all)
        rank_in = mm_nt(x, up_in_rows).astype(BF16) * ADAPTER_SCALE
        down_out_rows = down_out[0].reshape(here * r, MODEL_WIDTH)
        cot_mid = ADAPTER_SCALE * mm_nt(cot_all[...], down_out_rows)
        for e in range(here):
            rank_in_all[e] = rank_in[:, e * 2 * r : (e + 1) * 2 * r]
            cot_mid_all[e] = cot_mid[:, e * r : (e + 1) * r]

    cot = cot_all[...]
    lane = lax.broadcasted_iota(jnp.int32, gates.shape, 1)
    gate_of = jnp.sum(
        jnp.where(lane == scalars[2] * here + step, gates[...], 0.0), axis=1, keepdims=True
    )
    rank_in2 = rank_in_all[step]
    none = jnp.zeros((r, EXPERT_HIDDEN), BF16)
    out_map = jnp.concatenate(
        [
            jnp.concatenate([up_out[0, 0, 0], none], axis=1),
            jnp.concatenate([none, up_out[0, 0, 1]], axis=1),
        ],
        axis=0,
    )
    pre = mm(x, up_w[0]) + mm(rank_in2, out_map)
    gate_pre, up_pre = pre[:, :EXPERT_HIDDEN], pre[:, EXPERT_HIDDEN:]
    cot_hidden = mm_nt(cot, down_w[0])
    sig = 0.5 * jnp.tanh(0.5 * gate_pre) + 0.5
    silu = gate_pre * sig
    hidden_wide = silu * up_pre
    hidden = hidden_wide.astype(BF16)
    rank_mid = mm_nt(hidden, down_in[0, 0]).astype(BF16).astype(F32)
    cot_mid = cot_mid_all[step]
    gate_grad = jnp.sum(hidden.astype(F32) * cot_hidden, axis=1, keepdims=True) + jnp.sum(
        rank_mid * cot_mid, axis=1, keepdims=True
    )
    gg_lane = lax.broadcasted_iota(jnp.int32, gg_all.shape, 1)
    gg_all[...] += jnp.where(gg_lane == step, gate_grad, 0.0)
    grad_rank_mid = (gate_of * cot_mid).astype(BF16)
    grad_hidden = gate_of * cot_hidden + mm(grad_rank_mid, down_in[0, 0])
    grad_gate = (grad_hidden * up_pre * (sig + silu * (1.0 - sig))).astype(BF16)
    grad_up = (grad_hidden * silu).astype(BF16)
    grad_both = jnp.concatenate([grad_gate, grad_up], axis=1)
    grad_rank_all[step] = (ADAPTER_SCALE * mm_nt(grad_both, out_map)).astype(BF16)
    gated_all[step] = (ADAPTER_SCALE * gate_of * rank_mid).astype(BF16)
    part = mm_nt(grad_both, up_w[0])

    @pl.when(step == 0)
    def _():
        total[...] = part

    @pl.when(step > 0)
    def _():
        total[...] += part

    both = mm_tn(
        jnp.concatenate([rank_in2, grad_rank_mid], axis=1),
        jnp.concatenate([grad_both, hidden], axis=1),
    )
    narrow = jnp.concatenate(
        [
            both[i * r : (i + 1) * r, i * EXPERT_HIDDEN : (i + 1) * EXPERT_HIDDEN]
            for i in range(3)
        ],
        axis=0,
    )
    w, v = MODEL_WIDTH // parts, EXPERT_HIDDEN // parts
    if first:
        narrow_ref[0] = narrow
    else:
        narrow = (narrow + narrow_old[0]).astype(BF16)
        at = pl.ds(pl.multiple_of(step * (3 * r), 16), 3 * r)
        for p in range(parts):
            send_ref[p, at, w:] = narrow[:, p * v : (p + 1) * v]

    @pl.when(step == here - 1)
    def _():
        grad_rank = jnp.concatenate([grad_rank_all[e] for e in range(here)], axis=1)
        gated = jnp.concatenate([gated_all[e] for e in range(here)], axis=1)
        rows = total[...] + mm(grad_rank, up_in_rows)
        high = gg_all[...].astype(BF16).astype(F32)
        both = high + pltpu.roll(gg_all[...] - high, GATE_LANES, 1)
        for b, rows_ref in enumerate(rows_refs):
            at = slice(b * own, (b + 1) * own)
            rows_ref[:, :MODEL_WIDTH] = rows[at].astype(BF16)
            rows_ref[:, MODEL_WIDTH:] = both[at].astype(BF16)
        wide = jnp.concatenate([mm_tn(grad_rank, x), mm_tn(gated, cot)], axis=0)
        if first:
            wide_ref[...] = wide
        else:
            wide = (wide + wide_old[...]).astype(BF16)
            rows = here * 3 * r
            chosen = jnp.full((16, w + v), scalars[0], jnp.int32).astype(F32).astype(BF16)
            for p in range(parts):
                send_ref[p, :rows, :w] = wide[:, p * w : (p + 1) * w]
                send_ref[p, rows:] = chosen


def experts(scalars, parts, cots, x, router, tables, before):
    up_w, down_w, up_in, up_out, down_in, down_out = tables
    own = cots[0].shape[0]
    rows = own * len(cots)
    here = up_w.shape[0]
    r = ADAPTER_RANK
    per_expert = lambda i, s: (i, 0, 0)
    ins = [whole(c) for c in cots] + [
        whole(x),
        whole(router),
        (up_w, (1,) + up_w.shape[1:], per_expert),
        (down_w, (1,) + down_w.shape[1:], per_expert),
        chosen_whole(up_in),
        (up_out, (1, 1) + up_out.shape[2:], lambda i, s: (s[0], i, 0, 0, 0)),
        (down_in, (1, 1) + down_in.shape[2:], lambda i, s: (s[0], i, 0, 0)),
        chosen_whole(down_out),
    ]
    outs = [whole_out((own, SENT), BF16) for _ in cots]
    if before is None:
        outs.append(whole_out((here * 3 * r, MODEL_WIDTH), F32))
        outs.append(((here, 3 * r, EXPERT_HIDDEN), F32, (1, 3 * r, EXPERT_HIDDEN), per_expert))
    else:
        wide, narrow = before
        ins += [whole(wide), (narrow, (1,) + narrow.shape[1:], per_expert)]
        width = (MODEL_WIDTH + EXPERT_HIDDEN) // parts
        outs.append(whole_out((parts, here * 3 * r + 16, width), BF16))
        outs.append(whole_out((own, LANES), F32))
    return call(
        functools.partial(expert_kernel, len(cots), parts, before is None),
        scalars,
        here,
        ins,
        outs,
        [
            pltpu.VMEM((rows, LANES), F32),
            pltpu.VMEM((rows, MODEL_WIDTH), BF16),
            pltpu.VMEM((rows, MODEL_WIDTH), F32),
            pltpu.VMEM((rows, LANES), F32),
            pltpu.VMEM((here, rows, 2 * r), BF16),
            pltpu.VMEM((here, rows, r), F32),
            pltpu.VMEM((here, rows, 2 * r), BF16),
            pltpu.VMEM((here, rows, r), BF16),
        ],
    )


def middle_kernel(blocks, here, scalars, *refs):
    parts, ks, vs, refs = refs[:blocks], refs[blocks : 2 * blocks], refs[2 * blocks : 3 * blocks], refs[3 * blocks :]
    gates, router, middle_ref, inv_ref, gain, cot = refs[:6]
    proj_w, proj_in, proj_out, q_ref, bias, cosine, sine = refs[6:13]
    grad_middle, branch_ref, lora_ref, gq_ref = refs[13:17]
    gkv_refs, grad_att = refs[17:-1], refs[-1]
    step = pl.program_id(0)
    own = q_ref.shape[0]

    @pl.when(step == 0)
    def _():
        gates_own = gates[...]
        lane = lax.broadcasted_iota(jnp.int32, gates_own.shape, 1)
        gg = jnp.zeros_like(gates_own)
        for j, part in enumerate(parts):
            both = part[:, MODEL_WIDTH:].astype(F32)
            both = both + pltpu.roll(both, LANES - GATE_LANES, 1)
            both = jnp.where(lane < here, both, 0.0)
            gg = gg + pltpu.roll(both, lax.rem(scalars[2] + 1 + j, blocks) * here, 1)
        chosen = gates_own * (gg - jnp.sum(gates_own * gg, axis=-1, keepdims=True))
        grad = mm(chosen.astype(BF16), router[...])
        for part in parts:
            grad = grad + part[:, :MODEL_WIDTH].astype(F32)
        scaled = grad * gain[...]
        middle, inv = middle_ref[...], inv_ref[...]
        grad = (
            cot[...].astype(F32)
            + inv * scaled
            - middle * (inv * inv * inv) * jnp.mean(scaled * middle, axis=-1, keepdims=True)
        )
        grad_middle[...] = grad
        branch = grad.astype(BF16)
        branch_ref[...] = branch
        lora = (ADAPTER_SCALE * mm_nt(branch, proj_out[0])).astype(BF16)
        lora_ref[...] = lora
        attended = (mm_nt(branch, proj_w[...]) + mm(lora, proj_in[0])).astype(BF16)
        for i in range(PAIRS):
            grad_att[i] = attended[:, i * PAIR_QUERY : (i + 1) * PAIR_QUERY]

    key_of, value_of = variants(joined(ks), 0), variants(joined(vs), 0)
    queries, grads = lane_tiles(q_ref[...]), lane_tiles(grad_att[step])
    low = low_lanes(queries[0].shape)
    none = jnp.zeros_like(queries[0])
    probs_of, scores_of, query_of, grad_of = [], [], [], []

    def products(h):
        at = (h // 3, h % 2)
        scores = mm_nt(key_of[at], queries[h // 2]) + bias[...]
        return scores, mm_nt(value_of[at], grads[h // 2])

    waiting = [products(h) for h in range(AHEAD)]
    for h in range(6):
        scores, grad_probs = waiting.pop(0)
        if h + AHEAD < 6:
            waiting.append(products(h + AHEAD))
        shifted = jnp.exp(scores - jnp.max(scores, axis=0, keepdims=True))
        probs = shifted * (1.0 / jnp.sum(shifted, axis=0, keepdims=True))
        grad_scores = probs * (grad_probs - jnp.sum(probs * grad_probs, axis=0, keepdims=True))
        probs_of.append(probs.astype(BF16))
        scores_of.append(grad_scores.astype(BF16))
        inside = low if h % 2 == 0 else jnp.logical_not(low)
        query_of.append(jnp.where(inside, queries[h // 2], none))
        grad_of.append(jnp.where(inside, grads[h // 2], none))

    def summed_over(lefts, rights):
        def over(chosen):
            return mm(
                jnp.concatenate([lefts[h] for h in chosen], axis=1),
                jnp.concatenate([rights[h] for h in chosen], axis=0),
            )

        return over([0, 2, 3, 5]) + pltpu.roll(over([1, 4]), HEAD_SIZE, 1)

    grad_key = summed_over(scores_of, query_of)
    grad_key = turned(grad_key, cosine[...], -sine[...]).astype(BF16)
    grad_value = summed_over(probs_of, grad_of).astype(BF16)
    for b, gkv_ref in enumerate(gkv_refs):
        gkv_ref[:, :LANES] = grad_key[b * own : (b + 1) * own]
        gkv_ref[:, LANES:] = grad_value[b * own : (b + 1) * own]
    key_t = {at: key_of[at].astype(F32).T.astype(BF16) for at in key_of}
    cos, sin = cosine[-own:], -sine[-own:]
    for t in range(3):
        pair = (2 * t, 2 * t + 1)
        tile = mm(
            jnp.concatenate([key_t[h // 3, h % 2] for h in pair], axis=1),
            jnp.concatenate([scores_of[h] for h in pair], axis=0),
        )
        gq_ref[:, t * LANES : (t + 1) * LANES] = turned(SCALING * tile.T, cos, sin).astype(BF16)


def middle_backward(
    scalars, parts, here, gates, router, middle, inv, gain, cot, proj_w, proj_in, proj_out,
    q, ks, vs, bias_t, cosine, sine,
):
    own = q.shape[0]
    return call(
        functools.partial(middle_kernel, len(parts), here),
        scalars,
        PAIRS,
        [whole(part) for part in parts]
        + [(k, (own, 2 * LANES), lambda i, s: (0, i)) for k in ks + vs]
        + [
            whole(gates),
            whole(router),
            whole(middle),
            whole(inv),
            whole(gain),
            (cot, (own, MODEL_WIDTH), lambda i, s: (0, 0)),
            whole(proj_w),
            chosen_whole(proj_in),
            chosen_whole(proj_out),
            (q, (own, PAIR_QUERY), lambda i, s: (0, i)),
            whole(bias_t),
            whole(cosine),
            whole(sine),
        ],
        [
            whole_out((own, MODEL_WIDTH), F32),
            whole_out((own, MODEL_WIDTH), BF16),
            whole_out((own, ADAPTER_RANK), BF16),
            ((own, QUERY_FEATURES), BF16, (own, PAIR_QUERY), lambda i, s: (0, i)),
        ]
        + [
            ((own, 2 * KEY_FEATURES), BF16, (own, 2 * LANES), lambda i, s: (0, i))
            for _ in parts
        ],
        [pltpu.VMEM((PAIRS, own, PAIR_QUERY), BF16)],
        flops=20_000_000_000,
    )


def key_and_value(columns):
    return jnp.concatenate(columns[0::2], axis=1), jnp.concatenate(columns[1::2], axis=1)


def package_sizes(parts, blocks):
    width = (MODEL_WIDTH + KEY_FEATURES) // parts
    tiles = -(-width // LANES)
    return width, tiles, parts * tiles + blocks + 1


def partial_kernel(parts, blocks, scalars, *refs):
    gkvs, lora_in = refs[:blocks], refs[blocks : 2 * blocks]
    gq, query_out, kv_out, lora_out, branch, grad_lora, package = refs[2 * blocks :]
    own = gq.shape[0]
    r = ADAPTER_RANK
    width, tiles, entries = package_sizes(parts, blocks)
    low2 = joined(lora_in) * ADAPTER_SCALE
    gk, gv = key_and_value(lane_tiles(joined(gkvs)))
    wide = jnp.concatenate(
        [mm_tn(low2[-own:, :r], gq[...]), mm_tn(lora_out[...] * ADAPTER_SCALE, branch[...])], axis=0
    ).astype(BF16)
    narrow = jnp.concatenate(
        [mm_tn(low2[:, r : 2 * r], gk), mm_tn(low2[:, 2 * r :], gv)], axis=0
    ).astype(BF16)
    w, v = MODEL_WIDTH // parts, KEY_FEATURES // parts
    for p in range(parts):
        block = [wide[:, p * w : (p + 1) * w], narrow[:, p * v : (p + 1) * v]]
        if width < tiles * LANES:
            block.append(jnp.zeros((2 * r, tiles * LANES - width), BF16))
        for t, tile in enumerate(lane_tiles(jnp.concatenate(block, axis=1))):
            package[p * tiles + t] = tile
    grad_kv = jnp.concatenate([mm_nt(kv_out[0, 0], gk), mm_nt(kv_out[0, 1], gv)], axis=0)
    grad_kv = (ADAPTER_SCALE * grad_kv).astype(BF16)
    for j in range(blocks):
        at = parts * tiles + lax.rem(scalars[2] + 2 * blocks - 1 - j, blocks)
        package[at] = grad_kv[:, j * own : (j + 1) * own]
    grad_q = (ADAPTER_SCALE * mm_nt(query_out[0], gq[...])).astype(BF16)
    grad_out = grad_lora[...].astype(F32).T.astype(BF16)
    package[entries - 1] = jnp.concatenate([grad_q, grad_out], axis=0)


def partials(scalars, parts, gkvs, lora_in, gq, query_out, kv_out, lora_out, branch, grad_lora):
    blocks = len(gkvs)
    entries = package_sizes(parts, blocks)[2]
    return call(
        functools.partial(partial_kernel, parts, blocks),
        scalars,
        1,
        [whole(g) for g in list(gkvs) + lora_in]
        + [
            whole(gq),
            chosen_whole(query_out),
            chosen_whole(kv_out),
            whole(lora_out),
            whole(branch),
            whole(grad_lora),
        ],
        [whole_out((entries, 2 * ADAPTER_RANK, LANES), BF16)],
        [],
    )[0]


def sequence_kernel(parts, blocks, scalars, *refs):
    packages, normed = refs[:blocks], refs[blocks : 2 * blocks]
    attended, send, total = refs[2 * blocks :]
    r = ADAPTER_RANK
    width, tiles, entries = package_sizes(parts, blocks)
    total[...] = functools.reduce(lambda a, b: a + b, [p[...].astype(F32) for p in packages])
    ends = [p[entries - 1] for p in packages]
    order = [lax.rem(scalars[2] + 2 * blocks - 1 - j, blocks) for j in range(blocks)]
    grad_kv = [total[parts * tiles + rank].astype(BF16) for rank in order]
    grad_in = jnp.concatenate(
        [jnp.concatenate([end[:r] for end in ends], axis=1), jnp.concatenate(grad_kv, axis=1)],
        axis=0,
    )
    grad_out = jnp.concatenate([end[r:] for end in ends], axis=1)
    wide = jnp.concatenate(
        [mm(grad_in, joined(normed)), mm(grad_out, attended[...])], axis=0
    ).astype(BF16)
    w = MODEL_WIDTH // parts
    for p in range(parts):
        block = jnp.concatenate([total[p * tiles + t] for t in range(tiles)], axis=1).astype(BF16)
        send[p, : 4 * r, :w] = wide[:, p * w : (p + 1) * w]
        send[p, 4 * r :, :w] = block[:, :w]
        send[p, : 2 * r, w:] = block[:, w:width]
        send[p, 2 * r :, w:] = jnp.zeros((4 * r, width - w), BF16)


def sequence_sums(scalars, parts, packages, normed, attended):
    blocks = len(packages)
    width, _, entries = package_sizes(parts, blocks)
    return call(
        functools.partial(sequence_kernel, parts, blocks),
        scalars,
        1,
        [whole(p) for p in packages + normed] + [whole(attended)],
        [whole_out((parts, 6 * ADAPTER_RANK, width), BF16)],
        [pltpu.VMEM((entries, 2 * ADAPTER_RANK, LANES), F32)],
    )[0]


def expert_sum_kernel(wide, scalars, got, up_in, up_out, down_in, down_out):
    for out in (up_in, up_out, down_in, down_out):
        out[...] = jnp.zeros_like(out)
    r = ADAPTER_RANK
    here = up_in.shape[1]
    for n in range(got.shape[0]):
        a = scalars[3 + n]
        rows = got[n].astype(F32)
        for e in range(here):
            up_in[a, e] += rows[e * 2 * r : (e + 1) * 2 * r, :wide]
            down_out[a, e] += rows[(2 * here + e) * r : (2 * here + e + 1) * r, :wide]
            at = e * 3 * r
            up_out[a, e, 0] += rows[at : at + r, wide:]
            up_out[a, e, 1] += rows[at + r : at + 2 * r, wide:]
            down_in[a, e] += rows[at + 2 * r : at + 3 * r, wide:]


def expert_sum(scalars, got, here):
    parts = got.shape[0]
    r = ADAPTER_RANK
    wide, narrow = MODEL_WIDTH // parts, EXPERT_HIDDEN // parts

    def out(*shape):
        return whole_out((ADAPTER_CHOICES,) + shape, F32)

    return call(
        functools.partial(expert_sum_kernel, wide),
        scalars,
        1,
        [whole(got)],
        [
            out(here, 2 * r, wide),
            out(here, 2, r, narrow),
            out(here, r, narrow),
            out(here, r, wide),
        ],
        [],
    )


def attention_sum_kernel(wide, scalars, got, qkv_in, query_out, kv_out, proj_in, proj_out):
    for out in (qkv_in, query_out, kv_out, proj_in, proj_out):
        out[...] = jnp.zeros_like(out)
    r = ADAPTER_RANK
    for n in range(got.shape[0]):
        a = scalars[3 + n]
        rows = got[n].astype(F32)
        qkv_in[a] += rows[: 3 * r, :wide]
        proj_in[a] += rows[3 * r : 4 * r, :wide]
        query_out[a] += rows[4 * r : 5 * r, :wide]
        proj_out[a] += rows[5 * r :, :wide]
        kv_out[a, 0] += rows[:r, wide:]
        kv_out[a, 1] += rows[r : 2 * r, wide:]


def attention_sum(scalars, got):
    parts = got.shape[0]
    r = ADAPTER_RANK
    wide, narrow = MODEL_WIDTH // parts, KEY_FEATURES // parts

    def out(*shape):
        return whole_out((ADAPTER_CHOICES,) + shape, F32)

    return call(
        functools.partial(attention_sum_kernel, wide),
        scalars,
        1,
        [whole(got)],
        [
            out(3 * r, wide),
            out(r, wide),
            out(2, r, narrow),
            out(r, wide),
            out(r, wide),
        ],
        [],
    )


def query_kernel(scalars, gq, query_w, out_ref):
    out_ref[...] = mm_nt(gq[...], query_w[...])


def query_backward(scalars, gq, query_w):
    steps = 3
    return call(
        query_kernel,
        scalars,
        steps,
        [whole(gq), (query_w, (MODEL_WIDTH // steps, QUERY_FEATURES), lambda i, s: (i, 0))],
        [(gq.shape, F32, (gq.shape[0], MODEL_WIDTH // steps), lambda i, s: (0, i))],
        [],
    )[0]


def input_kernel(blocks, scalars, *refs):
    gkvs, refs = refs[:blocks], refs[blocks:]
    gq, first, kv_w, query_out, kv_out, down, x_ref, gain, grad_middle, out_ref = refs
    grad_kv = functools.reduce(lambda a, b: a + b, [g[...].astype(F32) for g in gkvs])
    grad_k, grad_v = key_and_value(lane_tiles(grad_kv.astype(BF16)))
    lora = jnp.concatenate(
        [
            mm_nt(gq[...], query_out[0]),
            mm_nt(grad_k, kv_out[0, 0]),
            mm_nt(grad_v, kv_out[0, 1]),
        ],
        axis=1,
    )
    lora = (ADAPTER_SCALE * lora).astype(BF16)
    grad = (
        first[...]
        + mm_nt(grad_k, kv_w[:, :KEY_FEATURES])
        + mm_nt(grad_v, kv_w[:, KEY_FEATURES:])
        + mm(lora, down[0])
    )
    x = x_ref[...].astype(F32)
    inv = lax.rsqrt(jnp.mean(x * x, axis=-1, keepdims=True) + EPS)
    scaled = grad * gain[...]
    out_ref[...] = (
        grad_middle[...]
        + inv * scaled
        - x * (inv * inv * inv) * jnp.mean(scaled * x, axis=-1, keepdims=True)
    )


def input_backward(scalars, gkvs, gq, first, kv_w, query_out, kv_out, down, x, gain, grad_middle):
    own = x.shape[0]
    return call(
        functools.partial(input_kernel, len(gkvs)),
        scalars,
        1,
        [whole(g) for g in gkvs]
        + [
            whole(gq),
            whole(first),
            whole(kv_w),
            chosen_whole(query_out),
            chosen_whole(kv_out),
            chosen_whole(down),
            whole(x),
            whole(gain),
            whole(grad_middle),
        ],
        [whole_out((own, MODEL_WIDTH), F32)],
        [],
        flops=20_000_000_000,
    )[0]


def shards(
    layer_input_rows,
    routes,
    prefix,
    sequence_adapter_index,
    attention_norm_gain,
    expert_norm_gain,
    query_weight,
    key_value_weight,
    projection_weight,
    router_weight,
    gate_up_weight,
    down_weight,
    adapter_query_key_value_input,
    adapter_query_output,
    adapter_key_value_output,
    adapter_projection_input,
    adapter_projection_output,
    adapter_gate_up_input,
    adapter_gate_up_output,
    adapter_down_input,
    adapter_down_output,
    cotangent,
):
    ctx_size = lax.axis_size("ctx")
    dp_size = lax.axis_size("dp")
    rank = lax.axis_index("ctx")
    own = layer_input_rows.shape[1]
    span = own * ctx_size
    experts_here = gate_up_weight.shape[0]
    experts_all = experts_here * ctx_size
    half = ctx_size // 2
    scalars = jnp.concatenate([sequence_adapter_index, prefix, rank[None]])
    gain_attn = attention_norm_gain[None]
    gain_ffn = expert_norm_gain[None]

    order = (rank - 1 - jnp.arange(ctx_size, dtype=jnp.int32)) % ctx_size
    positions = (order[:, None] * own + jnp.arange(own, dtype=jnp.int32)[None, :]).reshape(-1)
    size = HEAD_SIZE // 2
    frequency = ROPE_BASE ** (-jnp.arange(size, dtype=F32) / size)
    angles = positions.astype(F32)[:, None] * frequency[None, :]
    cosine, sine = jnp.cos(angles), jnp.sin(angles)
    cosine = jnp.concatenate([cosine] * 4, axis=1)
    sine = jnp.concatenate([-sine, sine] * 2, axis=1)
    allowed = (positions[None, :] <= positions[:, None]) | (positions[None, :] < prefix[0])
    bias = jnp.where(allowed, 0.0, MASKED).astype(F32)
    bias_t = bias[-own:].T
    qkv_in_t = adapter_query_key_value_input.transpose(0, 2, 1)
    proj_in_t = adapter_projection_input.transpose(0, 2, 1)
    router_t = jnp.pad(router_weight.T, ((0, LANES - experts_all), (0, 0)))

    expert_ids = jnp.arange(LANES, dtype=jnp.int32)
    named = jnp.any(routes[0][:, :, None] == expert_ids[None, None, :], axis=1).astype(BF16)
    cot_own = jnp.concatenate([cotangent[0], named], axis=1)
    x_own = layer_input_rows[0]
    step = functools.partial(lax.ppermute, axis_name="ctx", perm=rotation(ctx_size, 1))
    inputs = [step(x_own)]
    inputs.append(step(after(inputs[0], cosine, sine, bias, bias_t, router_t, scalars, cot_own)))
    while len(inputs) < ctx_size - 1:
        inputs.append(step(inputs[-1]))
    inputs.append(x_own)
    cots = None
    q, k, v, normed, lora_in = [], [], [], [], []
    now = scalars
    for some in ([ctx_size - 1] + list(range(ctx_size - 2)), [ctx_size - 2]):
        made = qkv(
            now, [inputs[b] for b in some], gain_attn, qkv_in_t, query_weight, key_value_weight,
            adapter_query_output, adapter_key_value_output, cosine, sine, some,
        )
        for all_of, some_of in zip((q, k, v, normed, lora_in), made):
            all_of += some_of
        now = after(scalars, q[0])
        if cots is None:
            cots = rotations(after(cot_own, q[0]), ctx_size, half)
    q, k, v, normed, lora_in = [a[1:] + a[:1] for a in (q, k, v, normed, lora_in)]
    tables = (
        gate_up_weight,
        down_weight,
        adapter_gate_up_input.transpose(0, 1, 3, 2),
        adapter_gate_up_output,
        adapter_down_input.transpose(0, 1, 3, 2),
        adapter_down_output,
    )

    normed_first, normed_last, attended, lora_out, middle, inv = attend(
        scalars, inputs, q, k, v, bias, projection_weight, proj_in_t, adapter_projection_output,
        gain_ffn,
    )
    cots += rotations(after(cot_own, normed_first), ctx_size, ctx_size - 1 - half, half + 1)
    cots.append(cot_own)
    *rows_first, wide, narrow = experts(
        scalars, dp_size, cots[:half], normed_first, router_t, tables, None
    )
    *rows_last, send, gates = experts(
        scalars, dp_size, cots[half:], normed_last, router_t, tables, (wide, narrow)
    )

    got = send_back(rows_first, ctx_size, 0)
    rows_last[0] = after(rows_last[0], *got)
    got += send_back(rows_last[:-1], ctx_size, half) + rows_last[-1:]
    grad_middle, branch, grad_lora, gq, *gkvs = middle_backward(
        scalars, got, experts_here, gates, router_t, middle, inv, gain_ffn, cot_own,
        projection_weight, proj_in_t, adapter_projection_output, q[-1], k, v, bias_t, cosine, sine,
    )
    expert_got = lax.all_to_all(send, "dp", 0, 0, tiled=True)
    package = partials(
        scalars, dp_size, gkvs, lora_in, after(gq, expert_got), adapter_query_output, adapter_key_value_output,
        lora_out, branch, grad_lora,
    )
    gkvs = list(gkvs)
    gkvs[0] = send_back(gkvs[:1], ctx_size, 0)[0]
    packages = rotations(after(package, gkvs[0]), ctx_size)
    choices = expert_got[:, experts_here * 3 * ADAPTER_RANK, 0].astype(jnp.int32)
    with_choices = jnp.concatenate([scalars, choices])
    first = query_backward(scalars, after(gq, package, gkvs[0], with_choices), query_weight)
    up_in, up_out, down_in, down_out = expert_sum(
        with_choices, after(expert_got, first), experts_here
    )
    later = [after(g, first, up_in, *packages[:-1]) for g in gkvs[1:-1]]
    gkvs[1:-1] = send_back(later, ctx_size, 1)
    packages[1] = after(packages[1], first, up_in)
    attention_send = sequence_sums(scalars, dp_size, packages, normed, attended)
    attention_got = lax.all_to_all(attention_send, "dp", 0, 0, tiled=True)
    grad_inputs = input_backward(
        scalars, gkvs, after(gq, attention_send), first, key_value_weight, adapter_query_output,
        adapter_key_value_output, qkv_in_t, x_own, gain_attn, grad_middle,
    )
    attention_got = after(attention_got, grad_inputs)
    qkv_in, query_out, kv_out, proj_in, proj_out = attention_sum(
        with_choices, attention_got
    )
    return (
        grad_inputs[None],
        qkv_in.transpose(0, 2, 1),
        query_out,
        kv_out,
        proj_in.transpose(0, 2, 1),
        proj_out,
        up_in.transpose(0, 1, 3, 2),
        up_out,
        down_in.transpose(0, 1, 3, 2),
        down_out,
    )


def solution(mesh):
    placed = (
        P("dp", "ctx", None),
        P("dp", "ctx", None),
        P("dp"),
        P("dp"),
        P(),
        P(),
        P(),
        P(),
        P(),
        P(),
        P("ctx", None, None),
        P("ctx", None, None),
        P(),
        P(),
        P(),
        P(),
        P(),
        P(None, "ctx", None, None),
        P(None, "ctx", None, None, None),
        P(None, "ctx", None, None),
        P(None, "ctx", None, None),
        P("dp", "ctx", None),
    )
    return jax.shard_map(
        shards,
        mesh=mesh,
        in_specs=placed,
        out_specs=(
            P("dp", "ctx", None),
            P(None, "dp", None),
            P(None, None, "dp"),
            P(None, None, None, "dp"),
            P(None, "dp", None),
            P(None, None, "dp"),
            P(None, "ctx", "dp", None),
            P(None, "ctx", None, None, "dp"),
            P(None, "ctx", "dp", None),
            P(None, "ctx", None, "dp"),
        ),
        check_vma=False,
    )
```
